128 devices in a mesh: pipe: 2 (over x_hi), tensor: 4 (over x_lo, core), dp: 16 (over z, y).
Axes of the slice: x: 4 (x_hi: 2, x_lo: 2; x = x_hi * 2 + x_lo), y: 4, z: 4, core: 2. Of those that a mesh axis runs over, the one named last changes fastest.
Arguments:
- hidden_in: bfloat16 [256, 16, 4, 256], P(None, 'dp', 'tensor')
- norm_gain: bfloat16 [2, 16384], P('pipe', 'dp'), may hold values from 0.25 to 1.75
- w_query: bfloat16 [2, 16384, 8192], P('pipe', 'dp', 'tensor'), may hold values from -0.046875 to 0.046875
- w_keyval: bfloat16 [2, 16384, 8, 256], P('pipe', 'dp', 'tensor'), may hold values from -0.046875 to 0.046875
- w_out: bfloat16 [2, 8192, 16384], P('pipe', 'tensor', 'dp'), may hold values from -1 to 1
- head_group: int32 [64], replicated, may hold values from 0 to 7, as said below
Outputs:
- layer_out: bfloat16 [2, 256, 16, 4, 256], P('pipe', None, 'dp', 'tensor')
- importance: float32 [2, 8], P('pipe')
The draws below stay inside these ranges and needn't reach their ends.
Inputs may be any that keep to these rules, and one draw needn't show every extreme that they name: `head_group`: each of the 8 groups is named by exactly 8 heads.
All inputs are finite; a program needn't handle non-finite values.
Results may differ from the reference program's by a relative error of at most 0.023.
Values may be sent and summed in bfloat16 or wider, within the bound.
No kernel may reach another device: no remote copies, remote signals or barrier semaphores. Data moves between devices by JAX's collectives and lax.ppermute only.
A program may use at most 64 MiB of HBM per device.

```python
import jax
import jax.numpy as jnp
from jax import lax

D = 16384
HD = 128
GROUPS = 8
HEADS = 64
ROWS = 256
LAYERS = 2
WIDE_DP = 1024
SLICE = 256
N_TENSOR = 4
N_DP = 16


def draw_hidden_in(key, part):
    key = jax.random.fold_in(key, 11)
    key_vals, key_cols, key_rows = jax.random.split(key, 3)
    columns = jnp.arange(D, dtype=jnp.float32) / (D - 1)
    values = jnp.clip(jax.random.normal(key_vals, (ROWS, D), jnp.float32), -3.0, 3.0)
    rising = 0.4 * jnp.exp(jnp.log(3.0) * columns)
    spread = jnp.exp(jax.random.uniform(key_cols, (D,), jnp.float32, -0.6, 0.6))
    row_scale = jnp.exp(jax.random.uniform(key_rows, (ROWS, 1), jnp.float32, -0.25, 0.25))
    field = values * rising[None, :] * spread[None, :] * row_scale
    return field.reshape(ROWS, D // WIDE_DP, WIDE_DP // SLICE, SLICE).astype(jnp.bfloat16)


def draw_w_out(key, part):
    key = jax.random.fold_in(key, 23)
    columns = jnp.arange(D, dtype=jnp.float32) / (D - 1)
    scale = (HEADS * HD) ** (-0.5)
    values = jnp.clip(jax.random.normal(key, (LAYERS, HEADS * HD, D), jnp.float32), -4.0, 4.0)
    rising = jnp.exp(jnp.log(4.0) * (columns - 0.5))
    return (values * (scale * rising)[None, None, :]).astype(jnp.bfloat16)


def draw_head_group(key, part):
    key = jax.random.fold_in(key, 7)
    order = jax.random.permutation(key, HEADS)
    return (order % GROUPS).astype(jnp.int32)


def level_of(stream_key, shape, cuts, least, largest):
    def one(position, parts):
        steps = jax.random.uniform(jax.random.fold_in(jax.random.fold_in(stream_key, 6), position), (parts,), jnp.float32, least / len(cuts), largest / len(cuts))
        return jnp.repeat(jnp.exp(steps), shape[position] // parts).reshape((-1,) + (1,) * (len(shape) - position - 1))

    level = one(*cuts[0])
    for cut in cuts[1:]:
        level = level * one(*cut)
    return level


def centred(rng, shape, width, reach, shards=(), held_as=jnp.bfloat16):
    loudness = level_of(rng, shape, shards, -0.22, 0.18) if shards else 1.0
    array = jax.random.normal(rng, shape, jnp.float32) * width * loudness
    return jnp.minimum(jnp.maximum(array, -reach), reach).astype(held_as)


def setup_inputs(seed: int = 0) -> dict:
    streams_of = jax.random.split(jax.random.key(seed), 7)
    hidden_in = draw_hidden_in(jax.random.fold_in(streams_of[6], 71), 0)
    norm_gain = jnp.clip(1.0 + 0.15 * jax.random.normal(streams_of[1], (LAYERS, D), jnp.float32), 0.25, 1.75).astype(jnp.bfloat16)
    w_query = centred(streams_of[2], (LAYERS, D, HEADS * HD), D ** -0.5, 0.046875, ((0, 2), (1, 16), (2, 4)))
    w_keyval = centred(streams_of[3], (LAYERS, D, GROUPS, 2 * HD), D ** -0.5, 0.046875, ((0, 2), (1, 16), (2, 4)))
    w_out = draw_w_out(jax.random.fold_in(streams_of[6], 71), 0)
    head_group = draw_head_group(jax.random.fold_in(streams_of[6], 71), 0)
    return {"hidden_in": hidden_in, "norm_gain": norm_gain, "w_query": w_query, "w_keyval": w_keyval, "w_out": w_out, "head_group": head_group}


THETA_LOG = 13.122363377404328
EPS_NORM = 1e-05
EPS_RMS = 1e-06

def rotate(values, positions, first_col, period):
    count_rows, count_cols = values.shape
    pair_cols = first_col + 2 * jnp.arange(count_cols // 2, dtype=jnp.int32)
    within = pair_cols % period
    freq = (within % HD // 2).astype(jnp.float32)
    inverse = jnp.exp(-THETA_LOG * 2.0 * freq / HD)
    angle = positions[:, None].astype(jnp.float32) * inverse[None, :]
    pairs = values.reshape(count_rows, count_cols // 2, 2)
    first = pairs[:, :, 0]
    second = pairs[:, :, 1]
    cosine = jnp.cos(angle)
    sine = jnp.sin(angle)
    keep = (within < HD)[None, :]
    new_first = jnp.where(keep, first * cosine - second * sine, first)
    new_second = jnp.where(keep, first * sine + second * cosine, second)
    return jnp.stack([new_first, new_second], axis=-1).reshape(count_rows, count_cols)

def attend(query, keys, vals, allowed):
    scores = lax.dot_general(query, keys, (((1,), (1,)), ((), ())), preferred_element_type=jnp.float32)
    expo = jnp.where(allowed, jnp.exp(scores / jnp.sqrt(jnp.float32(HD))), jnp.float32(0.0))
    weights = (expo / lax.optimization_barrier(jnp.sum(expo, axis=1, keepdims=True))).astype(jnp.bfloat16)
    return jnp.dot(weights, vals, preferred_element_type=jnp.float32).astype(jnp.bfloat16)

def reference(hidden_in, norm_gain, w_query, w_keyval, w_out, head_group):
    positions = jnp.arange(ROWS, dtype=jnp.int32)
    allowed = positions[:, None] >= positions[None, :]
    state = hidden_in.reshape(ROWS, D)
    outputs = []
    totals = []
    for layer in range(LAYERS):
        wide = state.astype(jnp.float32)
        square = lax.optimization_barrier(jnp.mean(wide * wide, axis=1, keepdims=True))
        normed = (wide * lax.rsqrt(square + EPS_NORM) * norm_gain[layer].astype(jnp.float32)).astype(jnp.bfloat16)
        keyval = jnp.dot(normed, w_keyval[layer].reshape(D, GROUPS * 2 * HD), preferred_element_type=jnp.float32)
        keyval = rotate(keyval, positions, 0, 2 * HD).astype(jnp.bfloat16)
        query = jnp.dot(normed, w_query[layer], preferred_element_type=jnp.float32)
        query = rotate(query, positions, 0, HD).astype(jnp.bfloat16)
        out_layer = w_out[layer]

        def one_head(carry, head):
            total, groups = carry
            group = head_group[head]
            block = lax.dynamic_slice_in_dim(keyval, group * 2 * HD, 2 * HD, 1)
            single = lax.dynamic_slice_in_dim(query, head * HD, HD, 1)
            attended = attend(single, block[:, :HD], block[:, HD:], allowed)
            rows_out = lax.dynamic_slice_in_dim(out_layer, head * HD, HD, 0)
            term = jnp.dot(attended, rows_out, preferred_element_type=jnp.float32)
            spread = jnp.sqrt(lax.optimization_barrier(jnp.mean(term * term, axis=1)) + EPS_RMS)
            picked = (jnp.arange(GROUPS, dtype=jnp.int32) == group).astype(jnp.float32)
            return ((total + term, groups + picked * jnp.mean(spread)), None)
        start = (jnp.zeros((ROWS, D), jnp.float32), jnp.zeros((GROUPS,), jnp.float32))
        (total, groups), _ = lax.scan(one_head, start, jnp.arange(HEADS, dtype=jnp.int32))
        state = (wide + total).astype(jnp.bfloat16)
        outputs.append(state.reshape(ROWS, N_DP, N_TENSOR, D // (N_DP * N_TENSOR)))
        totals.append(groups)
    return (jnp.stack(outputs), jnp.stack(totals))
```

```python
import functools
import math

import jax
import jax.numpy as jnp
import numpy as np
from jax import lax
from jax.experimental import pallas as pl
from jax.experimental.pallas import tpu as pltpu
from jax.sharding import PartitionSpec as P

HD = 128
GROUPS = 8
N_TENSOR = 4
N_DP = 16
THETA = 500000.0
EPS_NORM = 1e-05
EPS_RMS = 1e-06
STATS = 16

BF16 = jnp.bfloat16
F32 = jnp.float32
VMEM = pltpu.VMEM

S_SECTION, S_TENSOR, S_DATA, S_GROUPS = 0, 1, 2, 3


def rotary_tables(rows):
    positions = np.arange(rows, dtype=np.float64)[:, None]
    lanes = np.arange(HD)
    angle = positions * THETA ** (-2.0 * (lanes // 2) / HD)[None, :]
    sign = np.where(lanes % 2 == 0, -1.0, 1.0)[None, :]
    return np.cos(angle).astype(np.float32), (np.sin(angle) * sign).astype(np.float32)


def rotated(values, cosine, sine):
    lanes = lax.broadcasted_iota(jnp.int32, values.shape, 1)
    swapped = jnp.where(
        lanes % 2 == 0, pltpu.roll(values, HD - 1, 1), pltpu.roll(values, 1, 1)
    )
    return values * cosine + swapped * sine


def diagonal():
    return lax.broadcasted_iota(jnp.int32, (HD, HD), 0) == lax.broadcasted_iota(
        jnp.int32, (HD, HD), 1
    )


def two_parts(values):
    high = values.astype(BF16)
    return high, (values - high.astype(F32)).astype(BF16)


def project_kernel(step, scal, x0, x1, x2, x3, gain, wq, wkv, wout, send, scaled, kvs, stats):
    rows = x0.shape[0]
    cols = x0.shape[1]
    data_heads = send.shape[0]
    i = pl.program_id(0)
    active = scal[S_SECTION] == step

    @pl.when(jnp.logical_and(active, i == 0))
    def _():
        total = jnp.zeros((rows, 1), F32)
        for mask, ref in enumerate((x0, x1, x2, x3)):
            place = pl.multiple_of(lax.bitwise_xor(scal[S_TENSOR], mask) * cols, cols)
            wide = ref[...].astype(F32)
            total = total + jnp.sum(wide * wide, axis=1, keepdims=True)
            scaled[:, pl.ds(place, cols)] = (wide * gain[:, pl.ds(place, cols)]).astype(BF16)
        eye = diagonal()
        row = lax.broadcasted_iota(jnp.int32, (STATS, HD), 0)
        lines = jnp.zeros((STATS, HD), F32)
        for b in range(rows // HD):
            line = jnp.sum(
                jnp.where(eye, total[b * HD : (b + 1) * HD], 0.0), axis=0, keepdims=True
            )
            high, low = two_parts(line)
            lines = jnp.where(row == 2 * b, high.astype(F32), lines)
            lines = jnp.where(row == 2 * b + 1, low.astype(F32), lines)
        stats[...] = lines.astype(BF16)
        kvs[...] = jnp.dot(scaled[...], wkv[...], preferred_element_type=F32).astype(BF16)

    @pl.when(active)
    def _():
        part = jnp.dot(scaled[...], wq[...], preferred_element_type=F32).astype(BF16)
        for j in range(data_heads):
            send[j, :rows, :] = part[:, j * HD : (j + 1) * HD]
            first = pl.multiple_of((i * data_heads + j) * 16, 16)
            for c in range(4):
                send[j, rows + 16 * c : rows + 16 * c + 16, :] = kvs[
                    pl.ds(first, 16), c * HD : (c + 1) * HD
                ]
            send[j, rows + 64 :, :] = stats[...]

    @pl.when(jnp.logical_not(active))
    def _():
        for j in range(data_heads):
            head = wout[j * HD : (j + 1) * HD, :]
            gram = lax.dot_general(
                head, head, (((1,), (1,)), ((), ())), preferred_element_type=F32
            )
            high, low = two_parts(gram)
            send[j, :HD, :] = high
            send[j, HD:rows, :] = low
            send[j, rows:, :] = jnp.zeros((64 + STATS, HD), BF16)


def project(step, scal, pieces, gain, wq, wkv, wout):
    rows, cols = pieces[0].shape
    wide = cols * N_TENSOR
    heads = wq.shape[1] // HD
    steps = 4
    per = heads // steps
    whole = lambda shape: pl.BlockSpec(shape, lambda i, s: (0,) * len(shape))

    def q_block(i, s):
        return (0, jnp.where(s[S_SECTION] == step, i, 0))

    def out_block(i, s):
        return (jnp.where(s[S_SECTION] == step, 0, i), 0)

    return pl.pallas_call(
        functools.partial(project_kernel, step),
        out_shape=jax.ShapeDtypeStruct((heads, rows + 64 + STATS, HD), BF16),
        grid_spec=pltpu.PrefetchScalarGridSpec(
            num_scalar_prefetch=1,
            grid=(steps,),
            in_specs=[whole((rows, cols))] * 4
            + [
                whole((1, wide)),
                pl.BlockSpec((wide, per * HD), q_block),
                whole(wkv.shape),
                pl.BlockSpec((per * HD, wide), out_block),
            ],
            out_specs=pl.BlockSpec((per, rows + 64 + STATS, HD), lambda i, s: (i, 0, 0)),
            scratch_shapes=[
                VMEM((rows, wide), BF16),
                VMEM((rows, wkv.shape[1]), BF16),
                VMEM((STATS, HD), BF16),
            ],
        ),
        compiler_params=pltpu.CompilerParams(vmem_limit_bytes=24 * 2**20),
        name="project",
    )(scal, *pieces, gain, wq, wkv, wout)


def combine_kernel(width, scal, recv, cosine, sine, query, kv, gram, scale):
    rows = cosine.shape[0]
    raw = recv[0, :rows, :].astype(F32)
    for s in range(1, N_DP):
        raw = raw + recv[s, :rows, :].astype(F32)
    gram[...] = raw[:HD] + raw[HD : 2 * HD]
    tail = recv[0, rows:, :].astype(F32)
    for s in range(1, N_DP):
        tail = tail + recv[s, rows:, :].astype(F32)
    eye = diagonal()
    for b in range(rows // HD):
        line = tail[64 + 2 * b : 65 + 2 * b, :] + tail[65 + 2 * b : 66 + 2 * b, :]
        column = jnp.sum(jnp.where(eye, line, 0.0), axis=1, keepdims=True)
        factor = lax.rsqrt(column / width + EPS_NORM)
        scale[b * HD : (b + 1) * HD, :] = jnp.broadcast_to(factor, (HD, HD))
    query[...] = rotated(raw * scale[...], cosine[...], sine[...]).astype(BF16)
    first = pl.multiple_of(scal[S_DATA] * 16, 16)
    here = scale[pl.ds(first, 16), :]
    cos_here = cosine[pl.ds(first, 16), :]
    sin_here = sine[pl.ds(first, 16), :]
    for g in range(2):
        keys = tail[32 * g : 32 * g + 16] * here
        vals = tail[32 * g + 16 : 32 * g + 32] * here
        kv[g, :, :HD] = rotated(keys, cos_here, sin_here).astype(BF16)
        kv[g, :, HD:] = vals.astype(BF16)


def combine(scal, recv, cosine, sine, width):
    rows = cosine.shape[0]
    smem = pl.BlockSpec(memory_space=pltpu.SMEM)
    vmem = pl.BlockSpec(memory_space=VMEM)
    return pl.pallas_call(
        functools.partial(combine_kernel, float(width)),
        out_shape=(
            jax.ShapeDtypeStruct((rows, HD), BF16),
            jax.ShapeDtypeStruct((2, 16, 2 * HD), BF16),
            jax.ShapeDtypeStruct((HD, HD), F32),
        ),
        in_specs=[smem, vmem, vmem, vmem],
        out_specs=(vmem, vmem, vmem),
        scratch_shapes=[VMEM((rows, HD), F32)],
        compiler_params=pltpu.CompilerParams(vmem_limit_bytes=8 * 2**20),
        name="combine",
    )(scal, recv, cosine, sine)


def choose_kernel(scal, kv, send):
    for j in range(N_DP):
        send[j] = kv[scal[S_GROUPS + j]]


def choose(scal, kv):
    vmem = pl.BlockSpec(memory_space=VMEM)
    return pl.pallas_call(
        choose_kernel,
        out_shape=jax.ShapeDtypeStruct((N_DP,) + kv.shape[1:], BF16),
        in_specs=[pl.BlockSpec(memory_space=pltpu.SMEM), vmem],
        out_specs=vmem,
        name="choose",
    )(scal, kv)


def attended(query, kv):
    rows = query.shape[0]
    scores = lax.dot_general(
        query, kv[:, :HD], (((1,), (1,)), ((), ())), preferred_element_type=F32
    )
    allowed = lax.broadcasted_iota(jnp.int32, (rows, rows), 0) >= lax.broadcasted_iota(
        jnp.int32, (rows, rows), 1
    )
    expo = jnp.where(allowed, jnp.exp(scores * (1.0 / math.sqrt(HD))), 0.0)
    weights = (expo / jnp.sum(expo, axis=1, keepdims=True)).astype(BF16)
    return jnp.dot(weights, kv[:, HD:], preferred_element_type=F32).astype(BF16)


def attend_kernel(query, kv, send):
    result = attended(query[...], kv[...])
    for j in range(N_DP):
        send[j] = result


def attend(query, kv):
    rows = query.shape[0]
    vmem = pl.BlockSpec(memory_space=VMEM)
    return pl.pallas_call(
        attend_kernel,
        out_shape=jax.ShapeDtypeStruct((N_DP, rows, HD), BF16),
        in_specs=[vmem, vmem],
        out_specs=vmem,
        compiler_params=pltpu.CompilerParams(vmem_limit_bytes=8 * 2**20),
        name="attend",
    )(query, kv)


def attend_last_kernel(width, scal, query, kv, before, gram0, gram1, send):
    rows = query.shape[0]
    result = attended(query[...], kv[...])
    first_section = scal[S_SECTION] == 0
    mine = jnp.where(first_section, before[0], result)
    gram = jnp.where(first_section, gram1[...], gram0[...])
    high, low = two_parts(gram)
    image = jnp.dot(mine, high, preferred_element_type=F32) + jnp.dot(
        mine, low, preferred_element_type=F32
    )
    squares = jnp.sum(image * mine.astype(F32), axis=1, keepdims=True)
    spread = jnp.sqrt(jnp.maximum(squares / width, 0.0) + EPS_RMS)
    mean = jnp.sum(spread, axis=0, keepdims=True) / rows
    high, low = two_parts(mean)
    row = lax.broadcasted_iota(jnp.int32, (STATS, HD), 0)
    lines = jnp.where(row == 0, high.astype(F32), jnp.where(row == 1, low.astype(F32), 0.0))
    lines = lines.astype(BF16)
    for j in range(N_DP):
        send[j, :rows] = result
        send[j, rows:] = lines


def attend_last(scal, query, kv, before, gram0, gram1, width):
    rows = query.shape[0]
    vmem = pl.BlockSpec(memory_space=VMEM)
    return pl.pallas_call(
        functools.partial(attend_last_kernel, float(width)),
        out_shape=jax.ShapeDtypeStruct((N_DP, rows + STATS, HD), BF16),
        in_specs=[pl.BlockSpec(memory_space=pltpu.SMEM)] + [vmem] * 5,
        out_specs=vmem,
        compiler_params=pltpu.CompilerParams(vmem_limit_bytes=8 * 2**20),
        name="attend_last",
    )(scal, query, kv, before, gram0, gram1)


def out_kernel(rows, scal, recv, wout, o0, o1, o2, o3, joined):
    i = pl.program_id(0)
    heads = recv.shape[0]

    @pl.when(i == 0)
    def _():
        for h in range(heads):
            joined[:, h * HD : (h + 1) * HD] = recv[h, :rows, :]

    part = jnp.dot(joined[...], wout[...], preferred_element_type=F32).astype(BF16)
    extra = recv.shape[1] > rows
    if extra:
        lane = lax.broadcasted_iota(jnp.int32, (1, part.shape[1]), 1)
        sums = jnp.zeros((1, part.shape[1]), F32)
        for h in range(heads):
            value = recv[h, rows : rows + 1, :].astype(F32) + recv[
                h, rows + 1 : rows + 2, :
            ].astype(F32)
            value = jnp.concatenate([value] * (part.shape[1] // HD), axis=1)
            sums = sums + jnp.where(lane == scal[S_GROUPS + h], value, 0.0)
        high, low = two_parts(sums)
        row = lax.broadcasted_iota(jnp.int32, (STATS, part.shape[1]), 0)
        lines = jnp.where(
            row == 0, high.astype(F32), jnp.where(row == 1, low.astype(F32), 0.0)
        ).astype(BF16)
    for mask, ref in enumerate((o0, o1, o2, o3)):

        @pl.when(i == (mask + 3) % 4)
        def _():
            ref[:rows] = part
            if extra:
                ref[rows:] = lines


def project_out(scal, recv, wout, rows):
    heads, deep, _ = recv.shape
    wide = wout.shape[1]
    cols = wide // N_TENSOR
    whole = lambda shape: pl.BlockSpec(shape, lambda i, s: (0,) * len(shape))
    piece = jax.ShapeDtypeStruct((deep, cols), BF16)
    return pl.pallas_call(
        functools.partial(out_kernel, rows),
        out_shape=(piece,) * 4,
        grid_spec=pltpu.PrefetchScalarGridSpec(
            num_scalar_prefetch=1,
            grid=(N_TENSOR,),
            in_specs=[
                whole(recv.shape),
                pl.BlockSpec(
                    (heads * HD, cols),
                    lambda i, s: (0, lax.bitwise_xor(s[S_TENSOR], (i + 1) % 4)),
                ),
            ],
            out_specs=(whole((deep, cols)),) * 4,
            scratch_shapes=[VMEM((rows, heads * HD), BF16)],
        ),
        compiler_params=pltpu.CompilerParams(vmem_limit_bytes=24 * 2**20),
        name="project_out",
    )(scal, recv, wout)


def fresh_kernel(wide, o0, o1, o2, o3, fresh):
    total = o0[...].astype(F32)
    for ref in (o1, o2, o3):
        total = total + ref[...].astype(F32)
    fresh[...] = (wide[...].astype(F32) + total).astype(BF16)


def add_fresh(wide, parts):
    vmem = pl.BlockSpec(memory_space=VMEM)
    return pl.pallas_call(
        fresh_kernel,
        out_shape=jax.ShapeDtypeStruct(wide.shape, BF16),
        in_specs=[vmem] * 5,
        out_specs=vmem,
        name="add_fresh",
    )(wide, *parts)


def last_kernel(scal, before, wide, o0, o1, o2, o3, out, importance):
    rows = wide.shape[0]
    total = o0[...].astype(F32)
    for ref in (o1, o2, o3):
        total = total + ref[...].astype(F32)
    fresh = (wide[...].astype(F32) + total[:rows]).astype(BF16)
    out[...] = jnp.where(scal[S_SECTION] == 0, before[...], fresh)
    importance[...] = total[rows : rows + 1, :HD] + total[rows + 1 : rows + 2, :HD]


def add_last(scal, before, wide, parts):
    vmem = pl.BlockSpec(memory_space=VMEM)
    return pl.pallas_call(
        last_kernel,
        out_shape=(
            jax.ShapeDtypeStruct(wide.shape, BF16),
            jax.ShapeDtypeStruct((1, HD), F32),
        ),
        in_specs=[pl.BlockSpec(memory_space=pltpu.SMEM)] + [vmem] * 6,
        out_specs=(vmem, vmem),
        name="add_last",
    )(scal, before, wide, *parts)


def swap(block, mask):
    return lax.ppermute(block, "tensor", [(t, t ^ mask) for t in range(N_TENSOR)])


def to_next_section(block, mask):
    route = [(t, N_TENSOR + (t ^ mask)) for t in range(N_TENSOR)]
    return lax.ppermute(block, ("pipe", "tensor"), route)


def local(hidden_in, norm_gain, w_query, w_keyval, w_out, head_group):
    section = lax.axis_index("pipe")
    tensor = lax.axis_index("tensor")
    data = lax.axis_index("dp")
    rows, cols = hidden_in.shape[0], hidden_in.shape[3]
    width = cols * N_TENSOR * N_DP
    gain = norm_gain.astype(F32)
    wq = w_query[0]
    wkv = w_keyval[0].reshape(wq.shape[0], -1)
    wout = w_out[0]
    heads = wq.shape[1] // HD
    groups = lax.dynamic_slice_in_dim(head_group, tensor * heads, heads, 0)
    scal = jnp.concatenate([jnp.stack([section, tensor, data]).astype(jnp.int32), groups])
    cosine, sine = map(jnp.asarray, rotary_tables(rows))

    def to_heads(step, pieces):
        send = project(step, scal, pieces, gain, wq, wkv, wout)
        recv = lax.all_to_all(send, "dp", 0, 0)
        query, kv, gram = combine(scal, recv, cosine, sine, width)
        every = lax.all_gather(kv, "tensor")
        mine = choose(scal, every.reshape(GROUPS, 16, 2 * HD))
        kv_mine = lax.all_to_all(mine, "dp", 0, 0).reshape(rows, 2 * HD)
        return query, kv_mine, gram

    mine = hidden_in.reshape(rows, cols)
    far = swap(mine, 2)
    pieces = (mine, swap(mine, 1), far, swap(far, 1))
    query, kv, gram0 = to_heads(0, pieces)
    att0 = attend(query, kv)
    recv = lax.all_to_all(att0, "dp", 0, 0)
    parts = project_out(scal, recv, wout, rows)
    fresh0 = add_fresh(mine, (parts[0],) + tuple(swap(parts[m], m) for m in (1, 2, 3)))

    far = to_next_section(fresh0, 2)
    near = to_next_section(fresh0, 0)
    pieces = (near, swap(near, 1), far, swap(far, 1))
    query, kv, gram1 = to_heads(1, pieces)
    att1 = attend_last(scal, query, kv, att0, gram0, gram1, width)
    recv = lax.all_to_all(att1, "dp", 0, 0)
    parts = project_out(scal, recv, wout, rows)
    out, importance = add_last(
        scal, fresh0, near, (parts[0],) + tuple(swap(parts[m], m) for m in (1, 2, 3))
    )
    return out.reshape(1, rows, 1, 1, cols), importance[:, :GROUPS]


def solution(mesh):
    in_specs = (
        P(None, "dp", "tensor", None),
        P("pipe", "dp"),
        P("pipe", "dp", "tensor"),
        P("pipe", "dp", "tensor", None),
        P("pipe", "tensor", "dp"),
        P(),
    )
    out_specs = (P("pipe", None, "dp", "tensor", None), P("pipe", None))
    return jax.shard_map(local, mesh=mesh, in_specs=in_specs, out_specs=out_specs, check_vma=False)
```

```python
import functools
import math

import jax
import jax.numpy as jnp
import numpy as np
from jax import lax
from jax.experimental import pallas as pl
from jax.experimental.pallas import tpu as pltpu
from jax.sharding import PartitionSpec as P

HD = 128
GROUPS = 8
N_TENSOR = 4
N_DP = 16
THETA = 500000.0
EPS_NORM = 1e-05
EPS_RMS = 1e-06
STATS = 16

BF16 = jnp.bfloat16
F32 = jnp.float32
VMEM = pltpu.VMEM

S_SECTION, S_TENSOR, S_DATA, S_GROUPS = 0, 1, 2, 3


def rotary_tables(rows):
    positions = np.arange(rows, dtype=np.float64)[:, None]
    lanes = np.arange(HD)
    angle = positions * THETA ** (-2.0 * (lanes // 2) / HD)[None, :]
    sign = np.where(lanes % 2 == 0, -1.0, 1.0)[None, :]
    return np.cos(angle).astype(np.float32), (np.sin(angle) * sign).astype(np.float32)


def rotated(values, cosine, sine):
    lanes = lax.broadcasted_iota(jnp.int32, values.shape, 1)
    swapped = jnp.where(
        lanes % 2 == 0, pltpu.roll(values, HD - 1, 1), pltpu.roll(values, 1, 1)
    )
    return values * cosine + swapped * sine


def diagonal():
    return lax.broadcasted_iota(jnp.int32, (HD, HD), 0) == lax.broadcasted_iota(
        jnp.int32, (HD, HD), 1
    )


def two_parts(values):
    high = values.astype(BF16)
    return high, (values - high.astype(F32)).astype(BF16)


def project_kernel(
    step, count, scal, *refs
):
    pieces, refs = refs[:count], refs[count:]
    gain, wkv, wq, wout, send, scaled, kvs, wide_buf, head_buf, sems = refs
    rows, cols = pieces[0].shape[-2:]
    if count == 4:
        blocks = [(mask, ref) for mask, ref in enumerate(pieces)]
    else:
        blocks = [(n + 2 * k, pieces[n].at[k]) for n in range(2) for k in range(2)]
    chunks = wide_buf.shape[0]
    heads = send.shape[0]
    per = heads // chunks
    active = scal[S_SECTION] == step

    def wq_copy(i):
        return pltpu.make_async_copy(
            wq.at[:, pl.ds(pl.multiple_of(i * per * HD, per * HD), per * HD)],
            wide_buf.at[i],
            sems.at[i],
        )

    def wout_copy(i):
        return pltpu.make_async_copy(
            wout.at[pl.ds(pl.multiple_of(i * per * HD, per * HD), per * HD), :],
            head_buf.at[i],
            sems.at[i],
        )

    @pl.when(active)
    def _():
        for i in range(chunks):
            wq_copy(i).start()
        total = jnp.zeros((rows, 1), F32)
        for mask, ref in blocks:
            place = pl.multiple_of(lax.bitwise_xor(scal[S_TENSOR], mask) * cols, cols)
            wide = ref[...].astype(F32)
            total = total + jnp.sum(wide * wide, axis=1, keepdims=True)
            scaled[:, pl.ds(place, cols)] = (
                wide * gain[:, pl.ds(place, cols)].astype(F32)
            ).astype(BF16)
        eye = diagonal()
        row = lax.broadcasted_iota(jnp.int32, (STATS, HD), 0)
        lines = jnp.zeros((STATS, HD), F32)
        for b in range(rows // HD):
            line = jnp.sum(
                jnp.where(eye, total[b * HD : (b + 1) * HD], 0.0), axis=0, keepdims=True
            )
            high, low = two_parts(line)
            lines = jnp.where(row == 2 * b, high.astype(F32), lines)
            lines = jnp.where(row == 2 * b + 1, low.astype(F32), lines)
        lines = lines.astype(BF16)
        kvs[...] = jnp.dot(scaled[...], wkv[...], preferred_element_type=F32).astype(BF16)
        for j in range(heads):
            for c in range(4):
                send[j, rows + 16 * c : rows + 16 * c + 16, :] = kvs[
                    16 * j : 16 * j + 16, c * HD : (c + 1) * HD
                ]
            send[j, rows + 64 :, :] = lines

        @pl.loop(0, chunks)
        def _(i):
            wq_copy(i).wait()
            part = jnp.dot(scaled[...], wide_buf[i], preferred_element_type=F32).astype(BF16)
            for j in range(per):
                send[i * per + j, :rows, :] = part[:, j * HD : (j + 1) * HD]

    @pl.when(jnp.logical_not(active))
    def _():
        for i in range(chunks):
            wout_copy(i).start()

        @pl.loop(0, chunks)
        def _(i):
            wout_copy(i).wait()
            for j in range(per):
                head = head_buf[i, j * HD : (j + 1) * HD, :]
                gram = lax.dot_general(
                    head, head, (((1,), (1,)), ((), ())), preferred_element_type=F32
                )
                high, low = two_parts(gram)
                send[i * per + j, :HD, :] = high
                send[i * per + j, HD:rows, :] = low
                send[i * per + j, rows:, :] = jnp.zeros((64 + STATS, HD), BF16)


def project(step, scal, pieces, gain, wq, wkv, wout):
    rows, cols = pieces[0].shape[-2:]
    wide = cols * N_TENSOR
    heads = wq.shape[1] // HD
    chunks = 4
    per = heads // chunks
    vmem = pl.BlockSpec(memory_space=VMEM)
    hbm = pl.BlockSpec(memory_space=pltpu.HBM)
    return pl.pallas_call(
        functools.partial(project_kernel, step, len(pieces)),
        out_shape=jax.ShapeDtypeStruct((heads, rows + 64 + STATS, HD), BF16),
        in_specs=[pl.BlockSpec(memory_space=pltpu.SMEM)] + [vmem] * (len(pieces) + 2) + [hbm] * 2,
        out_specs=vmem,
        scratch_shapes=[
            VMEM((rows, wide), BF16),
            VMEM((rows, wkv.shape[1]), BF16),
            VMEM((chunks, wide, per * HD), BF16),
            VMEM((chunks, per * HD, wide), BF16),
            pltpu.SemaphoreType.DMA((chunks,)),
        ],
        compiler_params=pltpu.CompilerParams(vmem_limit_bytes=20 * 2**20),
        name="project",
    )(scal, *pieces, gain, wkv, wq, wout)


def combine_kernel(width, scal, recv, cosine, sine, query, kv, gram, scale):
    rows = cosine.shape[0]
    raw = recv[0, :rows, :].astype(F32)
    for s in range(1, N_DP):
        raw = raw + recv[s, :rows, :].astype(F32)
    gram[...] = raw[:HD] + raw[HD : 2 * HD]
    tail = recv[0, rows:, :].astype(F32)
    for s in range(1, N_DP):
        tail = tail + recv[s, rows:, :].astype(F32)
    eye = diagonal()
    for b in range(rows // HD):
        line = tail[64 + 2 * b : 65 + 2 * b, :] + tail[65 + 2 * b : 66 + 2 * b, :]
        column = jnp.sum(jnp.where(eye, line, 0.0), axis=1, keepdims=True)
        factor = lax.rsqrt(column / width + EPS_NORM)
        scale[b * HD : (b + 1) * HD, :] = jnp.broadcast_to(factor, (HD, HD))
    query[...] = rotated(raw * scale[...], cosine[...], sine[...]).astype(BF16)
    first = pl.multiple_of(scal[S_DATA] * 16, 16)
    here = scale[pl.ds(first, 16), :]
    cos_here = cosine[pl.ds(first, 16), :]
    sin_here = sine[pl.ds(first, 16), :]
    for g in range(2):
        keys = tail[32 * g : 32 * g + 16] * here
        vals = tail[32 * g + 16 : 32 * g + 32] * here
        kv[g, :, :HD] = rotated(keys, cos_here, sin_here).astype(BF16)
        kv[g, :, HD:] = vals.astype(BF16)


def combine(scal, recv, cosine, sine, width):
    rows = cosine.shape[0]
    smem = pl.BlockSpec(memory_space=pltpu.SMEM)
    vmem = pl.BlockSpec(memory_space=VMEM)
    return pl.pallas_call(
        functools.partial(combine_kernel, float(width)),
        out_shape=(
            jax.ShapeDtypeStruct((rows, HD), BF16),
            jax.ShapeDtypeStruct((2, 16, 2 * HD), BF16),
            jax.ShapeDtypeStruct((HD, HD), F32),
        ),
        in_specs=[smem, vmem, vmem, vmem],
        out_specs=(vmem, vmem, vmem),
        scratch_shapes=[VMEM((rows, HD), F32)],
        compiler_params=pltpu.CompilerParams(vmem_limit_bytes=8 * 2**20),
        name="combine",
    )(scal, recv, cosine, sine)


def choose_kernel(scal, kv, send):
    for j in range(N_DP):
        send[j] = kv[scal[S_GROUPS + j]]


def choose(scal, kv):
    vmem = pl.BlockSpec(memory_space=VMEM)
    return pl.pallas_call(
        choose_kernel,
        out_shape=jax.ShapeDtypeStruct((N_DP,) + kv.shape[1:], BF16),
        in_specs=[pl.BlockSpec(memory_space=pltpu.SMEM), vmem],
        out_specs=vmem,
        compiler_params=pltpu.CompilerParams(vmem_limit_bytes=4 * 2**20),
        name="choose",
    )(scal, kv)


def attended(query, kv):
    rows = query.shape[0]
    scores = lax.dot_general(
        query, kv[:, :HD], (((1,), (1,)), ((), ())), preferred_element_type=F32
    )
    allowed = lax.broadcasted_iota(jnp.int32, (rows, rows), 0) >= lax.broadcasted_iota(
        jnp.int32, (rows, rows), 1
    )
    expo = jnp.where(allowed, jnp.exp(scores * (1.0 / math.sqrt(HD))), 0.0)
    weights = (expo / jnp.sum(expo, axis=1, keepdims=True)).astype(BF16)
    return jnp.dot(weights, kv[:, HD:], preferred_element_type=F32).astype(BF16)


def attend_kernel(query, kv, send):
    result = attended(query[...], kv[...])
    for j in range(N_DP):
        send[j] = result


def attend(query, kv):
    rows = query.shape[0]
    vmem = pl.BlockSpec(memory_space=VMEM)
    return pl.pallas_call(
        attend_kernel,
        out_shape=jax.ShapeDtypeStruct((N_DP, rows, HD), BF16),
        in_specs=[vmem, vmem],
        out_specs=vmem,
        compiler_params=pltpu.CompilerParams(vmem_limit_bytes=8 * 2**20),
        name="attend",
    )(query, kv)


def attend_last_kernel(width, scal, query, kv, before, gram0, gram1, send):
    rows = query.shape[0]
    result = attended(query[...], kv[...])
    first_section = scal[S_SECTION] == 0
    mine = jnp.where(first_section, before[0], result)
    gram = jnp.where(first_section, gram1[...], gram0[...])
    high, low = two_parts(gram)
    image = jnp.dot(mine, high, preferred_element_type=F32) + jnp.dot(
        mine, low, preferred_element_type=F32
    )
    squares = jnp.sum(image * mine.astype(F32), axis=1, keepdims=True)
    spread = jnp.sqrt(jnp.maximum(squares / width, 0.0) + EPS_RMS)
    mean = jnp.sum(spread, axis=0, keepdims=True) / rows
    high, low = two_parts(mean)
    row = lax.broadcasted_iota(jnp.int32, (STATS, HD), 0)
    lines = jnp.where(row == 0, high.astype(F32), jnp.where(row == 1, low.astype(F32), 0.0))
    lines = lines.astype(BF16)
    for j in range(N_DP):
        send[j, :rows] = result
        send[j, rows:] = lines


def attend_last(scal, query, kv, before, gram0, gram1, width):
    rows = query.shape[0]
    vmem = pl.BlockSpec(memory_space=VMEM)
    return pl.pallas_call(
        functools.partial(attend_last_kernel, float(width)),
        out_shape=jax.ShapeDtypeStruct((N_DP, rows + STATS, HD), BF16),
        in_specs=[pl.BlockSpec(memory_space=pltpu.SMEM)] + [vmem] * 5,
        out_specs=vmem,
        compiler_params=pltpu.CompilerParams(vmem_limit_bytes=8 * 2**20),
        name="attend_last",
    )(scal, query, kv, before, gram0, gram1)


def out_kernel(rows, masks, scal, recv, saved, wout, parts, buf, sems):
    heads, deep, _ = recv.shape
    cols = parts.shape[2]
    last = saved is not None

    def copy(n):
        place = lax.bitwise_xor(scal[S_TENSOR], masks[n]) * cols
        return pltpu.make_async_copy(
            wout.at[:, pl.ds(pl.multiple_of(place, cols), cols)], buf.at[n], sems.at[n]
        )

    for n in range(2):
        copy(n).start()
    if last:
        lane = lax.broadcasted_iota(jnp.int32, (1, cols), 1)
        sums = jnp.zeros((1, cols), F32)
        for h in range(heads):
            value = recv[h, rows : rows + 1, :].astype(F32) + recv[
                h, rows + 1 : rows + 2, :
            ].astype(F32)
            value = jnp.concatenate([value] * (cols // HD), axis=1)
            sums = sums + jnp.where(lane == scal[S_GROUPS + h], value, 0.0)
        high, low = two_parts(sums)
        row = lax.broadcasted_iota(jnp.int32, (STATS, cols), 0)
        lines = jnp.where(
            row == 0, high.astype(F32), jnp.where(row == 1, low.astype(F32), 0.0)
        ).astype(BF16)
        for n in range(2):
            parts[n, rows:] = lines
    for n in range(2):
        copy(n).wait()
        total = jnp.zeros((rows, cols), F32)
        for h in range(0, heads, 2):
            pair = jnp.concatenate([recv[h, :rows, :], recv[h + 1, :rows, :]], axis=1)
            total = total + jnp.dot(
                pair, buf[n, h * HD : (h + 2) * HD, :], preferred_element_type=F32
            )
        part = total.astype(BF16)
        if last:
            part = jnp.where(scal[S_SECTION] == 0, saved[n], part)
        parts[n, :rows] = part


def first_out_kernel(rows, masks, scal, recv, wout, parts, buf, sems):
    out_kernel(rows, masks, scal, recv, None, wout, parts, buf, sems)


def project_out(scal, recv, wout, rows, masks, saved=None):
    heads, deep, _ = recv.shape
    cols = wout.shape[1] // N_TENSOR
    vmem = pl.BlockSpec(memory_space=VMEM)
    kernel = first_out_kernel if saved is None else out_kernel
    extra = () if saved is None else (saved,)
    return pl.pallas_call(
        functools.partial(kernel, rows, masks),
        out_shape=jax.ShapeDtypeStruct((2, deep, cols), BF16),
        in_specs=[pl.BlockSpec(memory_space=pltpu.SMEM), vmem]
        + [vmem] * len(extra)
        + [pl.BlockSpec(memory_space=pltpu.HBM)],
        out_specs=vmem,
        scratch_shapes=[
            VMEM((2, heads * HD, cols), BF16),
            pltpu.SemaphoreType.DMA((2,)),
        ],
        compiler_params=pltpu.CompilerParams(vmem_limit_bytes=8 * 2**20),
        cost_estimate=pl.CostEstimate(
            flops=4 * rows * heads * HD * cols, bytes_accessed=2**22, transcendentals=0
        ),
        name="project_out",
    )(scal, recv, *extra, wout)


def pair_kernel(rows, a, b, out):
    total = a[...].astype(F32) + b[...].astype(F32)
    out[...] = total.astype(BF16)
    if out.shape[1] > rows:
        for n in range(2):
            high, low = two_parts(total[n, rows : rows + 1] + total[n, rows + 1 : rows + 2])
            row = lax.broadcasted_iota(jnp.int32, (STATS, out.shape[2]), 0)
            lines = jnp.where(row == 0, high.astype(F32), 0.0)
            lines = jnp.where(row == 1, low.astype(F32), lines)
            out[n, rows:] = lines.astype(BF16)


def add_pair(a, b, rows):
    vmem = pl.BlockSpec(memory_space=VMEM)
    return pl.pallas_call(
        functools.partial(pair_kernel, rows),
        out_shape=jax.ShapeDtypeStruct(a.shape, BF16),
        in_specs=[vmem] * 2,
        out_specs=vmem,
        compiler_params=pltpu.CompilerParams(vmem_limit_bytes=4 * 2**20),
        name="add_pair",
    )(a, b)


def next_kernel(wide0, wide1, same, other, fresh):
    fresh[0] = (
        wide0[...].astype(F32) + (same[0].astype(F32) + other[1].astype(F32))
    ).astype(BF16)
    fresh[1] = (
        wide1[...].astype(F32) + (same[1].astype(F32) + other[0].astype(F32))
    ).astype(BF16)


def add_next(wide0, wide1, same, other):
    vmem = pl.BlockSpec(memory_space=VMEM)
    return pl.pallas_call(
        next_kernel,
        out_shape=jax.ShapeDtypeStruct(same.shape, BF16),
        in_specs=[vmem] * 4,
        out_specs=vmem,
        compiler_params=pltpu.CompilerParams(vmem_limit_bytes=4 * 2**20),
        name="add_next",
    )(wide0, wide1, same, other)


def last_kernel(scal, mine, state, here, there, out, importance):
    rows = mine.shape[0]
    total = here[0].astype(F32) + there[...].astype(F32)
    wide = jnp.where(scal[S_SECTION] == 0, mine[...], state[0]).astype(F32)
    out[...] = (wide + total[:rows]).astype(BF16)
    importance[...] = total[rows : rows + 1, :HD] + total[rows + 1 : rows + 2, :HD]


def add_last(scal, mine, state, here, there):
    vmem = pl.BlockSpec(memory_space=VMEM)
    return pl.pallas_call(
        last_kernel,
        out_shape=(
            jax.ShapeDtypeStruct(mine.shape, BF16),
            jax.ShapeDtypeStruct((1, HD), F32),
        ),
        in_specs=[pl.BlockSpec(memory_space=pltpu.SMEM)] + [vmem] * 4,
        out_specs=(vmem, vmem),
        compiler_params=pltpu.CompilerParams(vmem_limit_bytes=4 * 2**20),
        name="add_last",
    )(scal, mine, state, here, there)


def swap(block, mask):
    return lax.ppermute(block, "tensor", [(t, t ^ mask) for t in range(N_TENSOR)])


def to_next_section(block, mask):
    route = [(t, N_TENSOR + (t ^ mask)) for t in range(N_TENSOR)]
    return lax.ppermute(block, ("pipe", "tensor"), route)


def local(hidden_in, norm_gain, w_query, w_keyval, w_out, head_group):
    section = lax.axis_index("pipe")
    tensor = lax.axis_index("tensor")
    data = lax.axis_index("dp")
    rows, cols = hidden_in.shape[0], hidden_in.shape[3]
    width = cols * N_TENSOR * N_DP
    gain = norm_gain
    wq = w_query[0]
    wkv = w_keyval[0].reshape(wq.shape[0], -1)
    wout = w_out[0]
    heads = wq.shape[1] // HD
    groups = lax.dynamic_slice_in_dim(head_group, tensor * heads, heads, 0)
    scal = jnp.concatenate([jnp.stack([section, tensor, data]).astype(jnp.int32), groups])
    cosine, sine = map(jnp.asarray, rotary_tables(rows))

    def to_heads(step, pieces):
        send = project(step, scal, pieces, gain, wq, wkv, wout)
        recv = lax.all_to_all(send, "dp", 0, 0)
        query, kv, gram = combine(scal, recv, cosine, sine, width)
        every = lax.all_gather(kv, "tensor")
        mine = choose(scal, every.reshape(GROUPS, 16, 2 * HD))
        kv_mine = lax.all_to_all(mine, "dp", 0, 0).reshape(rows, 2 * HD)
        return query, kv_mine, gram

    mine = hidden_in.reshape(rows, cols)
    far = swap(mine, 2)
    pieces = (mine, swap(mine, 1), far, swap(far, 1))
    query, kv, gram0 = to_heads(0, pieces)
    att0 = attend(query, kv)
    recv = lax.all_to_all(att0, "dp", 0, 0)
    other0 = project_out(scal, recv, wout, rows, (1, 3))
    own0 = project_out(scal, recv, wout, rows, (0, 2))
    here = add_pair(own0, swap(other0, 1), rows)
    state = add_next(mine, far, to_next_section(here, 0), to_next_section(here, 2))

    beside = swap(state, 1)
    pieces = (state, beside)
    query, kv, gram1 = to_heads(1, pieces)
    att1 = attend_last(scal, query, kv, att0, gram0, gram1, width)
    recv = lax.all_to_all(att1, "dp", 0, 0)
    other1 = project_out(scal, recv, wout, rows, (1, 3), other0)
    own1 = project_out(scal, recv, wout, rows, (0, 2), own0)
    here = add_pair(own1, swap(other1, 1), rows)
    out, importance = add_last(scal, mine, state, here, swap(here[1], 2))
    return out.reshape(1, rows, 1, 1, cols), importance[:, :GROUPS]


def solution(mesh):
    in_specs = (
        P(None, "dp", "tensor", None),
        P("pipe", "dp"),
        P("pipe", "dp", "tensor"),
        P("pipe", "dp", "tensor", None),
        P("pipe", "tensor", "dp"),
        P(),
    )
    out_specs = (P("pipe", None, "dp", "tensor", None), P("pipe", None))
    return jax.shard_map(local, mesh=mesh, in_specs=in_specs, out_specs=out_specs, check_vma=False)
```

```python
import functools
import math

import jax
import jax.numpy as jnp
import numpy as np
from jax import lax
from jax.experimental import pallas as pl
from jax.experimental.pallas import tpu as pltpu
from jax.sharding import PartitionSpec as P

HD = 128
GROUPS = 8
N_TENSOR = 4
N_DP = 16
THETA = 500000.0
EPS_NORM = 1e-05
EPS_RMS = 1e-06
STATS = 16

BF16 = jnp.bfloat16
F32 = jnp.float32
VMEM = pltpu.VMEM

S_SECTION, S_TENSOR, S_DATA = 0, 1, 2


def rotary_tables(rows):
    positions = np.arange(rows, dtype=np.float64)[:, None]
    lanes = np.arange(HD)
    angle = positions * THETA ** (-2.0 * (lanes // 2) / HD)[None, :]
    sign = np.where(lanes % 2 == 0, -1.0, 1.0)[None, :]
    return np.cos(angle).astype(np.float32), (np.sin(angle) * sign).astype(np.float32)


def rotated(values, cosine, sine):
    lanes = lax.broadcasted_iota(jnp.int32, values.shape, 1)
    swapped = jnp.where(
        lanes % 2 == 0, pltpu.roll(values, HD - 1, 1), pltpu.roll(values, 1, 1)
    )
    return values * cosine + swapped * sine


def diagonal():
    return lax.broadcasted_iota(jnp.int32, (HD, HD), 0) == lax.broadcasted_iota(
        jnp.int32, (HD, HD), 1
    )


def two_parts(values):
    high = values.astype(BF16)
    return high, (values - high.astype(F32)).astype(BF16)


def load_kernel(scal, wq, wkv, wout, held, wkv_out, raw, sems):
    chunks = sems.shape[0] - 1
    deep, cols = wq.shape[0], wq.shape[1] // chunks
    halves = wout.shape[1] // cols
    long = wout.shape[0]
    first = pltpu.make_async_copy(wkv, raw, sems.at[chunks])
    first.start()

    def wq_copy(i):
        return pltpu.make_async_copy(
            wq.at[:, i * cols : (i + 1) * cols],
            held.at[i * deep : (i + 1) * deep, :],
            sems.at[i],
        )

    def wout_copy(i):
        return pltpu.make_async_copy(
            wout.at[:, i * cols : (i + 1) * cols],
            held.at[i * long : (i + 1) * long, :],
            sems.at[i],
        )

    @pl.when(scal[S_SECTION] == 0)
    def _():
        for i in range(chunks):
            wq_copy(i).start()

    @pl.when(scal[S_SECTION] != 0)
    def _():
        for i in range(halves):
            wout_copy(i).start()

    first.wait()
    width = wkv.shape[2]
    for g in range(wkv.shape[1]):
        wkv_out[:, g * width : (g + 1) * width] = raw[:, g, :]

    @pl.when(scal[S_SECTION] == 0)
    def _():
        for i in range(chunks):
            wq_copy(i).wait()

    @pl.when(scal[S_SECTION] != 0)
    def _():
        for i in range(halves):
            wout_copy(i).wait()


def load(scal, wq, wkv, wout):
    deep, cols = wq.shape
    chunks = 4
    hbm = pl.BlockSpec(memory_space=pltpu.HBM)
    vmem = pl.BlockSpec(memory_space=VMEM)
    return pl.pallas_call(
        load_kernel,
        out_shape=(
            jax.ShapeDtypeStruct((chunks * deep, cols // chunks), BF16),
            jax.ShapeDtypeStruct((deep, wkv.shape[1] * wkv.shape[2]), BF16),
        ),
        in_specs=[pl.BlockSpec(memory_space=pltpu.SMEM)] + [hbm] * 3,
        out_specs=(vmem,) * 2,
        scratch_shapes=[VMEM(wkv.shape, BF16), pltpu.SemaphoreType.DMA((chunks + 1,))],
        compiler_params=pltpu.CompilerParams(vmem_limit_bytes=40 * 2**20),
        cost_estimate=pl.CostEstimate(flops=10**9, bytes_accessed=1, transcendentals=0),
        name="load",
    )(scal, wq, wkv, wout)


def project_kernel(step, count, scal, *refs):
    pieces, refs = refs[:count], refs[count:]
    gain, wkv, *weights, send, scaled = refs
    rows, cols = pieces[0].shape[-2:]
    deep = cols * N_TENSOR
    per = 4
    heads = N_DP
    pitch = rows + 64 + STATS
    tensor = scal[S_TENSOR]
    if count == 4:
        by_mask = [ref[...] for ref in pieces]
    else:
        by_mask = [pieces[mask % 2][mask // 2] for mask in range(4)]

    def block(place):
        low = [jnp.where(tensor % 2 == place % 2, by_mask[n], by_mask[n + 1]) for n in (0, 2)]
        return jnp.where(tensor // 2 == place // 2, low[0], low[1])

    active = scal[S_SECTION] == step

    def query_chunk(i):
        if len(weights) == 1:
            return weights[0][i * deep : (i + 1) * deep, :]
        return weights[0][:, i * per * HD : (i + 1) * per * HD]

    def two_heads(i):
        at = pl.ds(pl.multiple_of(i * 2 * HD, 2 * HD), 2 * HD)
        if len(weights) == 1:
            long = heads * HD
            return [weights[0].at[n * long : (n + 1) * long, :][at, :] for n in range(2)]
        return [weights[1][at, :]]

    @pl.when(active)
    def _():
        total = jnp.zeros((rows, 1), F32)
        for place in range(N_TENSOR):
            at = slice(place * cols, (place + 1) * cols)
            wide = block(place).astype(F32)
            total = total + jnp.sum(wide * wide, axis=1, keepdims=True)
            scaled[:, at] = (wide * gain[:, at].astype(F32)).astype(BF16)
        eye = diagonal()
        row = lax.broadcasted_iota(jnp.int32, (STATS, HD), 0)
        lines = jnp.zeros((STATS, HD), F32)
        for b in range(rows // HD):
            line = jnp.sum(
                jnp.where(eye, total[b * HD : (b + 1) * HD], 0.0), axis=0, keepdims=True
            )
            high, low = two_parts(line)
            lines = jnp.where(row == 2 * b, high.astype(F32), lines)
            lines = jnp.where(row == 2 * b + 1, low.astype(F32), lines)
        lines = lines.astype(BF16)
        part = jnp.dot(scaled[...], wkv[...], preferred_element_type=F32).astype(BF16)
        for j in range(heads):
            first = j * pitch + rows
            for c in range(4):
                send[first + 16 * c : first + 16 * c + 16, :] = part[
                    16 * j : 16 * j + 16, c * HD : (c + 1) * HD
                ]
            send[first + 64 : first + 64 + STATS, :] = lines
        for i in range(heads // per):
            part = jnp.dot(scaled[...], query_chunk(i), preferred_element_type=F32).astype(BF16)
            for j in range(per):
                first = (i * per + j) * pitch
                send[first : first + rows, :] = part[:, j * HD : (j + 1) * HD]

    @pl.when(jnp.logical_not(active))
    def _():
        @pl.loop(0, heads // 2)
        def _(i):
            both = jnp.zeros((2 * HD, 2 * HD), F32)
            for pair in two_heads(i):
                both = both + lax.dot_general(
                    pair, pair, (((1,), (1,)), ((), ())), preferred_element_type=F32
                )
            for n in range(2):
                high, low = two_parts(both[n * HD : (n + 1) * HD, n * HD : (n + 1) * HD])
                first = pl.multiple_of((2 * i + n) * pitch, 16)
                send[pl.ds(first, HD), :] = high
                send[pl.ds(first + HD, HD), :] = low
                send[pl.ds(first + rows, 64 + STATS), :] = jnp.zeros((64 + STATS, HD), BF16)


def project(step, scal, pieces, gain, wkv, *weights):
    rows, cols = pieces[0].shape[-2:]
    wide = cols * N_TENSOR
    pitch = rows + 64 + STATS
    vmem = pl.BlockSpec(memory_space=VMEM)
    send = pl.pallas_call(
        functools.partial(project_kernel, step, len(pieces)),
        out_shape=jax.ShapeDtypeStruct((N_DP * pitch, HD), BF16),
        in_specs=[pl.BlockSpec(memory_space=pltpu.SMEM)]
        + [vmem] * (len(pieces) + 2 + len(weights)),
        out_specs=vmem,
        scratch_shapes=[VMEM((rows, wide), BF16)],
        compiler_params=pltpu.CompilerParams(vmem_limit_bytes=8 * 2**20),
        name="project",
    )(scal, *pieces, gain, wkv, *weights)
    return send.reshape(N_DP, pitch, HD)


def combine_kernel(step, width, scal, recv, cosine, sine, query, kv, gram, scale):
    rows = cosine.shape[0]
    active = scal[S_SECTION] == step

    def total(first, size):
        at = slice(first, first + size)
        value = recv[0, at, :].astype(F32)
        for s in range(1, N_DP):
            value = value + recv[s, at, :].astype(F32)
        return value

    @pl.when(active)
    def _():
        raw = total(0, rows)
        tail = total(rows, 64 + STATS)
        eye = diagonal()
        for b in range(rows // HD):
            line = tail[64 + 2 * b : 65 + 2 * b, :] + tail[65 + 2 * b : 66 + 2 * b, :]
            column = jnp.sum(jnp.where(eye, line, 0.0), axis=1, keepdims=True)
            factor = lax.rsqrt(column / width + EPS_NORM)
            scale[b * HD : (b + 1) * HD, :] = jnp.broadcast_to(factor, (HD, HD))
        query[...] = rotated(raw * scale[...], cosine[...], sine[...]).astype(BF16)
        first = pl.multiple_of(scal[S_DATA] * 16, 16)
        here = scale[pl.ds(first, 16), :]
        cos_here = cosine[pl.ds(first, 16), :]
        sin_here = sine[pl.ds(first, 16), :]
        for g in range(2):
            keys = tail[32 * g : 32 * g + 16] * here
            vals = tail[32 * g + 16 : 32 * g + 32] * here
            kv[g, :, :HD] = rotated(keys, cos_here, sin_here).astype(BF16)
            kv[g, :, HD:] = vals.astype(BF16)
        gram[...] = jnp.zeros_like(gram)

    @pl.when(jnp.logical_not(active))
    def _():
        gram[...] = total(0, HD) + total(HD, HD)
        query[...] = jnp.zeros_like(query)
        kv[...] = jnp.zeros_like(kv)


def combine(step, scal, recv, cosine, sine, width):
    rows = cosine.shape[0]
    smem = pl.BlockSpec(memory_space=pltpu.SMEM)
    vmem = pl.BlockSpec(memory_space=VMEM)
    return pl.pallas_call(
        functools.partial(combine_kernel, step, float(width)),
        out_shape=(
            jax.ShapeDtypeStruct((rows, HD), BF16),
            jax.ShapeDtypeStruct((2, 16, 2 * HD), BF16),
            jax.ShapeDtypeStruct((HD, HD), F32),
        ),
        in_specs=[smem, vmem, vmem, vmem],
        out_specs=(vmem, vmem, vmem),
        scratch_shapes=[VMEM((rows, HD), F32)],
        compiler_params=pltpu.CompilerParams(vmem_limit_bytes=8 * 2**20),
        name="combine",
    )(scal, recv, cosine, sine)


def choose_kernel(scal, group, kv, send):
    for j in range(N_DP):
        send[j] = kv[group[scal[S_TENSOR] * N_DP + j]]


def choose(scal, group, kv):
    vmem = pl.BlockSpec(memory_space=VMEM)
    return pl.pallas_call(
        choose_kernel,
        out_shape=jax.ShapeDtypeStruct((N_DP,) + kv.shape[1:], BF16),
        in_specs=[pl.BlockSpec(memory_space=pltpu.SMEM)] * 2 + [vmem],
        out_specs=vmem,
        compiler_params=pltpu.CompilerParams(vmem_limit_bytes=4 * 2**20),
        name="choose",
    )(scal, group, kv)


def attended(query, kv):
    rows = query.shape[0]
    scores = lax.dot_general(
        query, kv[:, :HD], (((1,), (1,)), ((), ())), preferred_element_type=F32
    )
    allowed = lax.broadcasted_iota(jnp.int32, (rows, rows), 0) >= lax.broadcasted_iota(
        jnp.int32, (rows, rows), 1
    )
    expo = jnp.where(allowed, jnp.exp(scores * (1.0 / math.sqrt(HD))), 0.0)
    weights = (expo / jnp.sum(expo, axis=1, keepdims=True)).astype(BF16)
    return jnp.dot(weights, kv[:, HD:], preferred_element_type=F32).astype(BF16)


def attend_kernel(scal, query, kv, send):
    active = scal[S_SECTION] == 0

    @pl.when(active)
    def _():
        result = attended(query[...], kv[...])
        for j in range(N_DP):
            send[j] = result

    @pl.when(jnp.logical_not(active))
    def _():
        send[...] = jnp.zeros_like(send)


def attend(scal, query, kv):
    rows = query.shape[0]
    vmem = pl.BlockSpec(memory_space=VMEM)
    return pl.pallas_call(
        attend_kernel,
        out_shape=jax.ShapeDtypeStruct((N_DP, rows, HD), BF16),
        in_specs=[pl.BlockSpec(memory_space=pltpu.SMEM), vmem, vmem],
        out_specs=vmem,
        compiler_params=pltpu.CompilerParams(vmem_limit_bytes=8 * 2**20),
        name="attend",
    )(scal, query, kv)


def attend_last_kernel(width, scal, query, kv, before, gram0, gram1, send):
    rows = query.shape[0]
    result = attended(query[...], kv[...])
    first_section = scal[S_SECTION] == 0
    mine = jnp.where(first_section, before[0], result)
    gram = jnp.where(first_section, gram1[...], gram0[...])
    high, low = two_parts(gram)
    image = jnp.dot(mine, high, preferred_element_type=F32) + jnp.dot(
        mine, low, preferred_element_type=F32
    )
    squares = jnp.sum(image * mine.astype(F32), axis=1, keepdims=True)
    spread = jnp.sqrt(jnp.maximum(squares / width, 0.0) + EPS_RMS)
    mean = jnp.sum(spread, axis=0, keepdims=True) / rows
    high, low = two_parts(mean)
    row = lax.broadcasted_iota(jnp.int32, (STATS, HD), 0)
    lines = jnp.where(row == 0, high.astype(F32), jnp.where(row == 1, low.astype(F32), 0.0))
    lines = lines.astype(BF16)
    for j in range(N_DP):
        send[j, :rows] = result
        send[j, rows:] = lines


def attend_last(scal, query, kv, before, gram0, gram1, width):
    rows = query.shape[0]
    vmem = pl.BlockSpec(memory_space=VMEM)
    return pl.pallas_call(
        functools.partial(attend_last_kernel, float(width)),
        out_shape=jax.ShapeDtypeStruct((N_DP, rows + STATS, HD), BF16),
        in_specs=[pl.BlockSpec(memory_space=pltpu.SMEM)] + [vmem] * 5,
        out_specs=vmem,
        compiler_params=pltpu.CompilerParams(vmem_limit_bytes=8 * 2**20),
        name="attend_last",
    )(scal, query, kv, before, gram0, gram1)


def out_kernel(rows, masks, scal, group, recv, saved, wout, parts):
    heads = recv.shape[0]
    cols = parts.shape[2]
    last = saved is not None
    if last:
        lane = lax.broadcasted_iota(jnp.int32, (1, cols), 1)
        sums = jnp.zeros((1, cols), F32)
        for h in range(heads):
            value = recv[h, rows : rows + 1, :].astype(F32) + recv[
                h, rows + 1 : rows + 2, :
            ].astype(F32)
            value = jnp.concatenate([value] * (cols // HD), axis=1)
            sums = sums + jnp.where(lane == group[scal[S_TENSOR] * heads + h], value, 0.0)
        high, low = two_parts(sums)
        row = lax.broadcasted_iota(jnp.int32, (STATS, cols), 0)
        lines = jnp.where(
            row == 0, high.astype(F32), jnp.where(row == 1, low.astype(F32), 0.0)
        ).astype(BF16)
        for n in range(2):
            parts[n, rows:] = lines
    active = (scal[S_SECTION] != 0) if last else (scal[S_SECTION] == 0)
    for parity in range(2):
        mine = (scal[S_TENSOR] + masks[0] + parity) % 2 == 0

        @pl.when(jnp.logical_and(active, mine))
        def _():
            for place in (parity, parity + 2):
                total = None
                for h in range(0, heads, 2):
                    pair = jnp.concatenate([recv[h, :rows, :], recv[h + 1, :rows, :]], axis=1)
                    one = jnp.dot(
                        pair,
                        wout[h * HD : (h + 2) * HD, place * cols : (place + 1) * cols],
                        preferred_element_type=F32,
                    )
                    total = one if total is None else total + one
                n = lax.bitwise_xor(scal[S_TENSOR], place) // 2
                parts[n, :rows] = total.astype(BF16)

    @pl.when(jnp.logical_not(active))
    def _():
        for n in range(2):
            parts[n, :rows] = saved[n] if last else jnp.zeros((rows, cols), BF16)


def first_out_kernel(rows, masks, scal, group, recv, wout, parts):
    out_kernel(rows, masks, scal, group, recv, None, wout, parts)


def project_out(scal, group, recv, wout, rows, masks, saved=None):
    heads, deep, _ = recv.shape
    cols = wout.shape[1] // N_TENSOR
    kernel = first_out_kernel if saved is None else out_kernel
    extra = () if saved is None else (saved,)
    return pl.pallas_call(
        functools.partial(kernel, rows, masks),
        out_shape=jax.ShapeDtypeStruct((2, deep, cols), BF16),
        in_specs=[pl.BlockSpec(memory_space=pltpu.SMEM)] * 2
        + [pl.BlockSpec(memory_space=VMEM)] * (2 + len(extra)),
        out_specs=pl.BlockSpec(memory_space=VMEM),
        compiler_params=pltpu.CompilerParams(vmem_limit_bytes=6 * 2**20),
        cost_estimate=pl.CostEstimate(
            flops=4 * rows * heads * HD * cols, bytes_accessed=2**22, transcendentals=0
        ),
        name="project_out",
    )(scal, group, recv, *extra, wout)


def pair_kernel(rows, a, b, out):
    total = a[...].astype(F32) + b[...].astype(F32)
    out[...] = total.astype(BF16)
    if out.shape[1] > rows:
        for n in range(2):
            high, low = two_parts(total[n, rows : rows + 1] + total[n, rows + 1 : rows + 2])
            row = lax.broadcasted_iota(jnp.int32, (STATS, out.shape[2]), 0)
            lines = jnp.where(row == 0, high.astype(F32), 0.0)
            lines = jnp.where(row == 1, low.astype(F32), lines)
            out[n, rows:] = lines.astype(BF16)


def add_pair(a, b, rows):
    vmem = pl.BlockSpec(memory_space=VMEM)
    return pl.pallas_call(
        functools.partial(pair_kernel, rows),
        out_shape=jax.ShapeDtypeStruct(a.shape, BF16),
        in_specs=[vmem] * 2,
        out_specs=vmem,
        compiler_params=pltpu.CompilerParams(vmem_limit_bytes=4 * 2**20),
        name="add_pair",
    )(a, b)


def next_kernel(wide0, wide1, same, other, fresh):
    fresh[0] = (
        wide0[...].astype(F32) + (same[0].astype(F32) + other[1].astype(F32))
    ).astype(BF16)
    fresh[1] = (
        wide1[...].astype(F32) + (same[1].astype(F32) + other[0].astype(F32))
    ).astype(BF16)


def add_next(wide0, wide1, same, other):
    vmem = pl.BlockSpec(memory_space=VMEM)
    return pl.pallas_call(
        next_kernel,
        out_shape=jax.ShapeDtypeStruct(same.shape, BF16),
        in_specs=[vmem] * 4,
        out_specs=vmem,
        compiler_params=pltpu.CompilerParams(vmem_limit_bytes=4 * 2**20),
        name="add_next",
    )(wide0, wide1, same, other)


def last_kernel(scal, mine, state, here, there, out, importance):
    rows = mine.shape[0]
    total = here[0].astype(F32) + there[...].astype(F32)
    wide = jnp.where(scal[S_SECTION] == 0, mine[...], state[0]).astype(F32)
    out[...] = (wide + total[:rows]).astype(BF16)
    importance[...] = total[rows : rows + 1, :HD] + total[rows + 1 : rows + 2, :HD]


def add_last(scal, mine, state, here, there):
    vmem = pl.BlockSpec(memory_space=VMEM)
    return pl.pallas_call(
        last_kernel,
        out_shape=(
            jax.ShapeDtypeStruct(mine.shape, BF16),
            jax.ShapeDtypeStruct((1, HD), F32),
        ),
        in_specs=[pl.BlockSpec(memory_space=pltpu.SMEM)] + [vmem] * 4,
        out_specs=(vmem, vmem),
        compiler_params=pltpu.CompilerParams(vmem_limit_bytes=4 * 2**20),
        name="add_last",
    )(scal, mine, state, here, there)


def swap(block, mask):
    return lax.ppermute(block, "tensor", [(t, t ^ mask) for t in range(N_TENSOR)])


def to_next_section(block, mask):
    route = [(t, N_TENSOR + (t ^ mask)) for t in range(N_TENSOR)]
    return lax.ppermute(block, ("pipe", "tensor"), route)


def local(hidden_in, norm_gain, w_query, w_keyval, w_out, head_group):
    section = lax.axis_index("pipe")
    tensor = lax.axis_index("tensor")
    data = lax.axis_index("dp")
    rows, cols = hidden_in.shape[0], hidden_in.shape[3]
    width = cols * N_TENSOR * N_DP
    wq, wkv, wout = w_query[0], w_keyval[0], w_out[0]
    scal = jnp.stack([section, tensor, data]).astype(jnp.int32)
    cosine, sine = map(jnp.asarray, rotary_tables(rows))

    def to_heads(step, pieces, *weights):
        send = project(step, scal, pieces, norm_gain, *weights)
        recv = lax.all_to_all(send, "dp", 0, 0)
        query, kv, gram = combine(step, scal, recv, cosine, sine, width)
        every = lax.all_gather(kv, "tensor")
        mine = choose(scal, head_group, every.reshape(GROUPS, 16, 2 * HD))
        kv_mine = lax.all_to_all(mine, "dp", 0, 0).reshape(rows, 2 * HD)
        return query, kv_mine, gram

    mine = hidden_in.reshape(rows, cols)
    far = swap(mine, 2)
    pieces = (mine, swap(mine, 1), far, swap(mine, 3))
    query, kv, gram0 = to_heads(0, pieces, *load(scal, wq, wkv, wout)[::-1])
    att0 = attend(scal, query, kv)
    recv = lax.all_to_all(att0, "dp", 0, 0)
    other0 = project_out(scal, head_group, recv, wout, rows, (1, 3))
    own0 = project_out(scal, head_group, recv, wout, rows, (0, 2))
    here = add_pair(own0, swap(other0, 1), rows)
    state = add_next(mine, far, to_next_section(here, 0), to_next_section(here, 2))

    beside = swap(state, 1)
    pieces = (state, beside)
    query, kv, gram1 = to_heads(1, pieces, wkv.reshape(wq.shape[0], -1), wq, wout)
    att1 = attend_last(scal, query, kv, att0, gram0, gram1, width)
    recv = lax.all_to_all(att1, "dp", 0, 0)
    other1 = project_out(scal, head_group, recv, wout, rows, (1, 3), other0)
    own1 = project_out(scal, head_group, recv, wout, rows, (0, 2), own0)
    here = add_pair(own1, swap(other1, 1), rows)
    out, importance = add_last(scal, mine, state, here, swap(here[1], 2))
    return out.reshape(1, rows, 1, 1, cols), importance[:, :GROUPS]


def solution(mesh):
    in_specs = (
        P(None, "dp", "tensor", None),
        P("pipe", "dp"),
        P("pipe", "dp", "tensor"),
        P("pipe", "dp", "tensor", None),
        P("pipe", "tensor", "dp"),
        P(),
    )
    out_specs = (P("pipe", None, "dp", "tensor", None), P("pipe", None))
    return jax.shard_map(local, mesh=mesh, in_specs=in_specs, out_specs=out_specs, check_vma=False)
```

```python
import functools
import math

import jax
import jax.numpy as jnp
import numpy as np
from jax import lax
from jax.experimental import pallas as pl
from jax.experimental.pallas import tpu as pltpu
from jax.sharding import PartitionSpec as P

HD = 128
GROUPS = 8
N_TENSOR = 4
N_DP = 16
THETA = 500000.0
EPS_NORM = 1e-05
EPS_RMS = 1e-06
STATS = 16

BF16 = jnp.bfloat16
F32 = jnp.float32
VMEM = pltpu.VMEM


def rotary_tables(rows):
    positions = np.arange(rows, dtype=np.float64)[:, None]
    lanes = np.arange(HD)
    angle = positions * THETA ** (-2.0 * (lanes // 2) / HD)[None, :]
    sign = np.where(lanes % 2 == 0, -1.0, 1.0)[None, :]
    return np.cos(angle).astype(np.float32), (np.sin(angle) * sign).astype(np.float32)


def rotated(values, cosine, sine):
    lanes = lax.broadcasted_iota(jnp.int32, values.shape, 1)
    swapped = jnp.where(
        lanes % 2 == 0, pltpu.roll(values, HD - 1, 1), pltpu.roll(values, 1, 1)
    )
    return values * cosine + swapped * sine


def diagonal():
    return lax.broadcasted_iota(jnp.int32, (HD, HD), 0) == lax.broadcasted_iota(
        jnp.int32, (HD, HD), 1
    )


def two_parts(values):
    high = values.astype(BF16)
    return high, (values - high.astype(F32)).astype(BF16)


def load_kernel(wq, wkv, out):
    cols = wkv.shape[2]
    for g in range(wkv.shape[1]):
        out[:, g * cols : (g + 1) * cols] = wkv[:, g, :]


def load(wq, wkv):
    vmem = pl.BlockSpec(memory_space=VMEM)
    return pl.pallas_call(
        load_kernel,
        out_shape=jax.ShapeDtypeStruct((wkv.shape[0], wkv.shape[1] * wkv.shape[2]), BF16),
        in_specs=[vmem] * 2,
        out_specs=vmem,
        compiler_params=pltpu.CompilerParams(vmem_limit_bytes=12 * 2**20),
        cost_estimate=pl.CostEstimate(flops=10**9, bytes_accessed=10**7, transcendentals=0),
        name="load",
    )(wq, wkv)


def gram_parts(wout, target):
    @pl.loop(0, wout.shape[0] // (2 * HD))
    def _(i):
        pair = wout[pl.ds(pl.multiple_of(i * 2 * HD, 2 * HD), 2 * HD), :]
        both = lax.dot_general(pair, pair, (((1,), (1,)), ((), ())), preferred_element_type=F32)
        for n in range(2):
            high, low = two_parts(both[n * HD : (n + 1) * HD, n * HD : (n + 1) * HD])
            ref, first = target(2 * i + n)
            ref[pl.ds(first, HD), :] = high
            ref[pl.ds(first + HD, HD), :] = low


def project_kernel(step, count, *refs):
    pieces, refs = refs[:count], refs[count:]
    gain, wkv, wq, *wout, send, scaled = refs
    rows, cols = pieces[0].shape[-2:]
    per = 4
    heads = N_DP
    pitch = rows + 64 + STATS
    tensor = lax.axis_index("tensor")
    if count == 4:
        by_mask = [ref[...] for ref in pieces]
    else:
        by_mask = [pieces[mask % 2][mask // 2] for mask in range(4)]

    def block(place):
        low = [jnp.where(tensor % 2 == place % 2, by_mask[n], by_mask[n + 1]) for n in (0, 2)]
        return jnp.where(tensor // 2 == place // 2, low[0], low[1])

    active = lax.axis_index("pipe") == step

    @pl.when(active)
    def _():
        total = jnp.zeros((rows, 1), F32)
        for place in range(N_TENSOR):
            at = slice(place * cols, (place + 1) * cols)
            wide = block(place).astype(F32)
            total = total + jnp.sum(wide * wide, axis=1, keepdims=True)
            scaled[:, at] = (wide * gain[:, at].astype(F32)).astype(BF16)
        eye = diagonal()
        row = lax.broadcasted_iota(jnp.int32, (STATS, HD), 0)
        lines = jnp.zeros((STATS, HD), F32)
        for b in range(rows // HD):
            line = jnp.sum(
                jnp.where(eye, total[b * HD : (b + 1) * HD], 0.0), axis=0, keepdims=True
            )
            high, low = two_parts(line)
            lines = jnp.where(row == 2 * b, high.astype(F32), lines)
            lines = jnp.where(row == 2 * b + 1, low.astype(F32), lines)
        lines = lines.astype(BF16)
        part = jnp.dot(scaled[...], wkv[...], preferred_element_type=F32).astype(BF16)
        for j in range(heads):
            first = j * pitch + rows
            for c in range(4):
                send[first + 16 * c : first + 16 * c + 16, :] = part[
                    16 * j : 16 * j + 16, c * HD : (c + 1) * HD
                ]
            send[first + 64 : first + 64 + STATS, :] = lines
        for i in range(heads // per):
            part = jnp.dot(
                scaled[...], wq[:, i * per * HD : (i + 1) * per * HD], preferred_element_type=F32
            ).astype(BF16)
            for j in range(per):
                first = (i * per + j) * pitch
                send[first : first + rows, :] = part[:, j * HD : (j + 1) * HD]

    @pl.when(jnp.logical_not(active))
    def _():
        if wout:
            gram_parts(wout[0], lambda h: (send, pl.multiple_of(h * pitch, 16)))
            for j in range(heads):
                first = j * pitch + rows
                send[first : first + 64 + STATS, :] = jnp.zeros((64 + STATS, HD), BF16)
        else:
            send[...] = jnp.zeros_like(send)


def project(step, pieces, gain, wkv, *weights):
    rows, cols = pieces[0].shape[-2:]
    wide = cols * N_TENSOR
    pitch = rows + 64 + STATS
    vmem = pl.BlockSpec(memory_space=VMEM)
    send = pl.pallas_call(
        functools.partial(project_kernel, step, len(pieces)),
        out_shape=jax.ShapeDtypeStruct((N_DP * pitch, HD), BF16),
        in_specs=[vmem] * (len(pieces) + 2 + len(weights)),
        out_specs=vmem,
        scratch_shapes=[VMEM((rows, wide), BF16)],
        compiler_params=pltpu.CompilerParams(vmem_limit_bytes=8 * 2**20),
        name="project",
    )(*pieces, gain, wkv, *weights)
    return send.reshape(N_DP, pitch, HD)


def combine_kernel(step, width, recv, cosine, sine, query, kv, gram, scale):
    rows = cosine.shape[0]
    active = lax.axis_index("pipe") == step

    def total(first, size):
        at = slice(first, first + size)
        value = recv[0, at, :].astype(F32)
        for s in range(1, N_DP):
            value = value + recv[s, at, :].astype(F32)
        return value

    @pl.when(active)
    def _():
        raw = total(0, rows)
        tail = total(rows, 64 + STATS)
        eye = diagonal()
        for b in range(rows // HD):
            line = tail[64 + 2 * b : 65 + 2 * b, :] + tail[65 + 2 * b : 66 + 2 * b, :]
            column = jnp.sum(jnp.where(eye, line, 0.0), axis=1, keepdims=True)
            factor = lax.rsqrt(column / width + EPS_NORM)
            scale[b * HD : (b + 1) * HD, :] = jnp.broadcast_to(factor, (HD, HD))
        query[...] = rotated(raw * scale[...], cosine[...], sine[...]).astype(BF16)
        first = pl.multiple_of(lax.axis_index("dp") * 16, 16)
        here = scale[pl.ds(first, 16), :]
        cos_here = cosine[pl.ds(first, 16), :]
        sin_here = sine[pl.ds(first, 16), :]
        for g in range(2):
            keys = tail[32 * g : 32 * g + 16] * here
            vals = tail[32 * g + 16 : 32 * g + 32] * here
            kv[g, :, :HD] = rotated(keys, cos_here, sin_here).astype(BF16)
            kv[g, :, HD:] = vals.astype(BF16)
        gram[...] = jnp.zeros_like(gram)

    @pl.when(jnp.logical_not(active))
    def _():
        gram[...] = total(0, HD) + total(HD, HD)
        query[...] = jnp.zeros_like(query)
        kv[...] = jnp.zeros_like(kv)


def combine(step, recv, cosine, sine, width):
    rows = cosine.shape[0]
    vmem = pl.BlockSpec(memory_space=VMEM)
    return pl.pallas_call(
        functools.partial(combine_kernel, step, float(width)),
        out_shape=(
            jax.ShapeDtypeStruct((rows, HD), BF16),
            jax.ShapeDtypeStruct((2, 16, 2 * HD), BF16),
            jax.ShapeDtypeStruct((HD, HD), F32),
        ),
        in_specs=[vmem] * 3,
        out_specs=(vmem, vmem, vmem),
        scratch_shapes=[VMEM((rows, HD), F32)],
        compiler_params=pltpu.CompilerParams(vmem_limit_bytes=8 * 2**20),
        name="combine",
    )(recv, cosine, sine)


def choose_kernel(group, kv, send):
    for j in range(N_DP):
        send[j] = kv[group[lax.axis_index("tensor") * N_DP + j]]


def choose(group, kv):
    vmem = pl.BlockSpec(memory_space=VMEM)
    return pl.pallas_call(
        choose_kernel,
        out_shape=jax.ShapeDtypeStruct((N_DP,) + kv.shape[1:], BF16),
        in_specs=[pl.BlockSpec(memory_space=pltpu.SMEM), vmem],
        out_specs=vmem,
        compiler_params=pltpu.CompilerParams(vmem_limit_bytes=4 * 2**20),
        name="choose",
    )(group, kv)


def attended(query, kv):
    rows = query.shape[0]
    scores = lax.dot_general(
        query, kv[:, :HD], (((1,), (1,)), ((), ())), preferred_element_type=F32
    )
    allowed = lax.broadcasted_iota(jnp.int32, (rows, rows), 0) >= lax.broadcasted_iota(
        jnp.int32, (rows, rows), 1
    )
    expo = jnp.where(allowed, jnp.exp(scores * (1.0 / math.sqrt(HD))), 0.0)
    weights = (expo / jnp.sum(expo, axis=1, keepdims=True)).astype(BF16)
    return jnp.dot(weights, kv[:, HD:], preferred_element_type=F32).astype(BF16)


def attend_kernel(query, kv, wout, send):
    active = lax.axis_index("pipe") == 0

    @pl.when(active)
    def _():
        result = attended(query[...], kv[...])
        for j in range(N_DP):
            send[j] = result

    @pl.when(jnp.logical_not(active))
    def _():
        gram_parts(wout, lambda h: (send.at[h], 0))


def attend(query, kv, wout):
    rows = query.shape[0]
    vmem = pl.BlockSpec(memory_space=VMEM)
    return pl.pallas_call(
        attend_kernel,
        out_shape=jax.ShapeDtypeStruct((N_DP, rows, HD), BF16),
        in_specs=[vmem] * 3,
        out_specs=vmem,
        compiler_params=pltpu.CompilerParams(vmem_limit_bytes=8 * 2**20),
        name="attend",
    )(query, kv, wout)


def attend_last_kernel(width, query, kv, before, gram0, gram1, send):
    rows = query.shape[0]
    result = attended(query[...], kv[...])
    first_section = lax.axis_index("pipe") == 0
    mine = jnp.where(first_section, before[0], result)
    gram = jnp.where(first_section, gram1[...], gram0[...])
    high, low = two_parts(gram)
    image = jnp.dot(mine, high, preferred_element_type=F32) + jnp.dot(
        mine, low, preferred_element_type=F32
    )
    squares = jnp.sum(image * mine.astype(F32), axis=1, keepdims=True)
    spread = jnp.sqrt(jnp.maximum(squares / width, 0.0) + EPS_RMS)
    mean = jnp.sum(spread, axis=0, keepdims=True) / rows
    high, low = two_parts(mean)
    row = lax.broadcasted_iota(jnp.int32, (STATS, HD), 0)
    lines = jnp.where(row == 0, high.astype(F32), jnp.where(row == 1, low.astype(F32), 0.0))
    lines = lines.astype(BF16)
    for j in range(N_DP):
        send[j, :rows] = result
        send[j, rows:] = lines


def attend_last(query, kv, before, gram0, gram1, width):
    rows = query.shape[0]
    vmem = pl.BlockSpec(memory_space=VMEM)
    return pl.pallas_call(
        functools.partial(attend_last_kernel, float(width)),
        out_shape=jax.ShapeDtypeStruct((N_DP, rows + STATS, HD), BF16),
        in_specs=[vmem] * 5,
        out_specs=vmem,
        compiler_params=pltpu.CompilerParams(vmem_limit_bytes=8 * 2**20),
        name="attend_last",
    )(query, kv, before, gram0, gram1)


def out_kernel(rows, masks, last, *refs):
    if last:
        group, recv, saved, wout, parts = refs
    else:
        recv, wout, parts, *gram = refs
    heads = recv.shape[0]
    cols = parts.shape[2]
    tensor = lax.axis_index("tensor")
    active = lax.axis_index("pipe") == (1 if last else 0)
    if last:
        lane = lax.broadcasted_iota(jnp.int32, (1, cols), 1)
        sums = jnp.zeros((1, cols), F32)
        for h in range(heads):
            value = recv[h, rows : rows + 1, :].astype(F32) + recv[
                h, rows + 1 : rows + 2, :
            ].astype(F32)
            value = jnp.concatenate([value] * (cols // HD), axis=1)
            sums = sums + jnp.where(lane == group[tensor * heads + h], value, 0.0)
        high, low = two_parts(sums)
        row = lax.broadcasted_iota(jnp.int32, (STATS, cols), 0)
        lines = jnp.where(
            row == 0, high.astype(F32), jnp.where(row == 1, low.astype(F32), 0.0)
        ).astype(BF16)
        for n in range(2):
            parts[n, rows:] = lines
    for parity in range(2):

        @pl.when(jnp.logical_and(active, (tensor + masks[0] + parity) % 2 == 0))
        def _():
            for place in (parity, parity + 2):
                total = None
                for h in range(0, heads, 2):
                    pair = jnp.concatenate([recv[h, :rows, :], recv[h + 1, :rows, :]], axis=1)
                    one = jnp.dot(
                        pair,
                        wout[h * HD : (h + 2) * HD, place * cols : (place + 1) * cols],
                        preferred_element_type=F32,
                    )
                    total = one if total is None else total + one
                n = lax.bitwise_xor(tensor, place) // 2
                parts[n, :rows] = total.astype(BF16)

    @pl.when(jnp.logical_not(active))
    def _():
        for n in range(2):
            parts[n, :rows] = saved[n] if last else jnp.zeros((rows, cols), BF16)
        if not last and gram:
            total = jnp.zeros((HD, HD), F32)
            for s in range(heads):
                total = total + (recv[s, :HD].astype(F32) + recv[s, HD : 2 * HD].astype(F32))
            gram[0][...] = total

    if not last and gram:

        @pl.when(active)
        def _():
            gram[0][...] = jnp.zeros((HD, HD), F32)


def project_out(recv, wout, rows, masks, group=None, saved=None):
    heads, deep, _ = recv.shape
    cols = wout.shape[1] // N_TENSOR
    last = saved is not None
    vmem = pl.BlockSpec(memory_space=VMEM)
    shapes = (jax.ShapeDtypeStruct((2, deep, cols), BF16),)
    if not last and masks[0] == 0:
        shapes += (jax.ShapeDtypeStruct((HD, HD), F32),)
    operands = (group, recv, saved, wout) if last else (recv, wout)
    return pl.pallas_call(
        functools.partial(out_kernel, rows, masks, last),
        out_shape=shapes,
        in_specs=[pl.BlockSpec(memory_space=pltpu.SMEM)] * last
        + [vmem] * (len(operands) - last),
        out_specs=(vmem,) * len(shapes),
        compiler_params=pltpu.CompilerParams(vmem_limit_bytes=6 * 2**20),
        cost_estimate=pl.CostEstimate(
            flops=4 * rows * heads * HD * cols, bytes_accessed=2**22, transcendentals=0
        ),
        name="project_out",
    )(*operands)


def pair_kernel(rows, a, b, out):
    total = a[...].astype(F32) + b[...].astype(F32)
    out[...] = total.astype(BF16)
    if out.shape[1] > rows:
        for n in range(2):
            high, low = two_parts(total[n, rows : rows + 1] + total[n, rows + 1 : rows + 2])
            row = lax.broadcasted_iota(jnp.int32, (STATS, out.shape[2]), 0)
            lines = jnp.where(row == 0, high.astype(F32), 0.0)
            lines = jnp.where(row == 1, low.astype(F32), lines)
            out[n, rows:] = lines.astype(BF16)


def add_pair(a, b, rows):
    vmem = pl.BlockSpec(memory_space=VMEM)
    return pl.pallas_call(
        functools.partial(pair_kernel, rows),
        out_shape=jax.ShapeDtypeStruct(a.shape, BF16),
        in_specs=[vmem] * 2,
        out_specs=vmem,
        compiler_params=pltpu.CompilerParams(vmem_limit_bytes=4 * 2**20),
        name="add_pair",
    )(a, b)


def next_kernel(wide0, wide1, same, other, fresh):
    fresh[0] = (
        wide0[...].astype(F32) + (same[0].astype(F32) + other[1].astype(F32))
    ).astype(BF16)
    fresh[1] = (
        wide1[...].astype(F32) + (same[1].astype(F32) + other[0].astype(F32))
    ).astype(BF16)


def add_next(wide0, wide1, same, other):
    vmem = pl.BlockSpec(memory_space=VMEM)
    return pl.pallas_call(
        next_kernel,
        out_shape=jax.ShapeDtypeStruct(same.shape, BF16),
        in_specs=[vmem] * 4,
        out_specs=vmem,
        compiler_params=pltpu.CompilerParams(vmem_limit_bytes=4 * 2**20),
        name="add_next",
    )(wide0, wide1, same, other)


def last_kernel(mine, state, here, there, out, importance):
    rows = mine.shape[0]
    total = here[0].astype(F32) + there[...].astype(F32)
    wide = jnp.where(lax.axis_index("pipe") == 0, mine[...], state[0]).astype(F32)
    out[...] = (wide + total[:rows]).astype(BF16)
    importance[...] = total[rows : rows + 1, :HD] + total[rows + 1 : rows + 2, :HD]


def add_last(mine, state, here, there):
    vmem = pl.BlockSpec(memory_space=VMEM)
    return pl.pallas_call(
        last_kernel,
        out_shape=(
            jax.ShapeDtypeStruct(mine.shape, BF16),
            jax.ShapeDtypeStruct((1, HD), F32),
        ),
        in_specs=[vmem] * 4,
        out_specs=(vmem, vmem),
        compiler_params=pltpu.CompilerParams(vmem_limit_bytes=4 * 2**20),
        name="add_last",
    )(mine, state, here, there)


def swap(block, mask):
    return lax.ppermute(block, "tensor", [(t, t ^ mask) for t in range(N_TENSOR)])


def to_next_section(block, mask):
    route = [(t, N_TENSOR + (t ^ mask)) for t in range(N_TENSOR)]
    return lax.ppermute(block, ("pipe", "tensor"), route)


def local(hidden_in, norm_gain, w_query, w_keyval, w_out, head_group):
    rows, cols = hidden_in.shape[0], hidden_in.shape[3]
    width = cols * N_TENSOR * N_DP
    wq, wout = w_query[0], w_out[0]
    wkv = load(wq, w_keyval[0])
    cosine, sine = map(jnp.asarray, rotary_tables(rows))

    def to_heads(step, pieces, *weights):
        send = project(step, pieces, norm_gain, wkv, wq, *weights)
        recv = lax.all_to_all(send, "dp", 0, 0)
        query, kv, gram = combine(step, recv, cosine, sine, width)
        every = lax.all_gather(kv, "tensor")
        mine = choose(head_group, every.reshape(GROUPS, 16, 2 * HD))
        kv_mine = lax.all_to_all(mine, "dp", 0, 0).reshape(rows, 2 * HD)
        return query, kv_mine, gram

    mine = hidden_in.reshape(rows, cols)
    far = swap(mine, 2)
    query, kv, _ = to_heads(0, (mine, swap(mine, 1), far, swap(mine, 3)))
    att0 = attend(query, kv, wout)
    recv = lax.all_to_all(att0, "dp", 0, 0)
    (other0,) = project_out(recv, wout, rows, (1, 3))
    own0, gram0 = project_out(recv, wout, rows, (0, 2))
    here = add_pair(own0, swap(other0, 1), rows)
    state = add_next(mine, far, to_next_section(here, 0), to_next_section(here, 2))

    query, kv, gram1 = to_heads(1, (state, swap(state, 1)), wout)
    att1 = attend_last(query, kv, att0, gram0, gram1, width)
    recv = lax.all_to_all(att1, "dp", 0, 0)
    (other1,) = project_out(recv, wout, rows, (1, 3), head_group, other0)
    (own1,) = project_out(recv, wout, rows, (0, 2), head_group, own0)
    here = add_pair(own1, swap(other1, 1), rows)
    out, importance = add_last(mine, state, here, swap(here[1], 2))
    return out.reshape(1, rows, 1, 1, cols), importance[:, :GROUPS]


def solution(mesh):
    in_specs = (
        P(None, "dp", "tensor", None),
        P("pipe", "dp"),
        P("pipe", "dp", "tensor"),
        P("pipe", "dp", "tensor", None),
        P("pipe", "tensor", "dp"),
        P(),
    )
    out_specs = (P("pipe", None, "dp", "tensor", None), P("pipe", None))
    return jax.shard_map(local, mesh=mesh, in_specs=in_specs, out_specs=out_specs, check_vma=False)
```

```python
import functools
import math

import jax
import jax.numpy as jnp
import numpy as np
from jax import lax
from jax.experimental import pallas as pl
from jax.experimental.pallas import tpu as pltpu
from jax.sharding import PartitionSpec as P

HD = 128
GROUPS = 8
N_TENSOR = 4
N_DP = 16
THETA = 500000.0
EPS_NORM = 1e-05
EPS_RMS = 1e-06
STATS = 16

BF16 = jnp.bfloat16
F32 = jnp.float32
VMEM = pltpu.VMEM


def rotary_tables(rows):
    positions = np.arange(rows, dtype=np.float64)[:, None]
    lanes = np.arange(HD)
    angle = positions * THETA ** (-2.0 * (lanes // 2) / HD)[None, :]
    sign = np.where(lanes % 2 == 0, -1.0, 1.0)[None, :]
    return np.cos(angle).astype(np.float32), (np.sin(angle) * sign).astype(np.float32)


def rotated(values, cosine, sine):
    lanes = lax.broadcasted_iota(jnp.int32, values.shape, 1)
    swapped = jnp.where(
        lanes % 2 == 0, pltpu.roll(values, HD - 1, 1), pltpu.roll(values, 1, 1)
    )
    return values * cosine + swapped * sine


def diagonal():
    return lax.broadcasted_iota(jnp.int32, (HD, HD), 0) == lax.broadcasted_iota(
        jnp.int32, (HD, HD), 1
    )


def two_parts(values):
    high = values.astype(BF16)
    return high, (values - high.astype(F32)).astype(BF16)


def load_kernel(wq, wkv, out):
    cols = wkv.shape[2]
    for g in range(wkv.shape[1]):
        out[:, g * cols : (g + 1) * cols] = wkv[:, g, :]


def load(wq, wkv):
    vmem = pl.BlockSpec(memory_space=VMEM)
    return pl.pallas_call(
        load_kernel,
        out_shape=jax.ShapeDtypeStruct((wkv.shape[0], wkv.shape[1] * wkv.shape[2]), BF16),
        in_specs=[vmem] * 2,
        out_specs=vmem,
        compiler_params=pltpu.CompilerParams(vmem_limit_bytes=12 * 2**20),
        cost_estimate=pl.CostEstimate(flops=10**9, bytes_accessed=10**7, transcendentals=0),
        name="load",
    )(wq, wkv)


def gram_parts(wout, target):
    @pl.loop(0, wout.shape[0] // (2 * HD))
    def _(i):
        pair = wout[pl.ds(pl.multiple_of(i * 2 * HD, 2 * HD), 2 * HD), :]
        both = lax.dot_general(pair, pair, (((1,), (1,)), ((), ())), preferred_element_type=F32)
        for n in range(2):
            high, low = two_parts(both[n * HD : (n + 1) * HD, n * HD : (n + 1) * HD])
            ref, first = target(2 * i + n)
            ref[pl.ds(first, HD), :] = high
            ref[pl.ds(first + HD, HD), :] = low


def project_kernel(step, count, *refs):
    pieces, refs = refs[:count], refs[count:]
    gain, wkv, wq, *wout, send, scaled = refs
    rows, cols = pieces[0].shape[-2:]
    per = 4
    heads = N_DP
    pitch = rows + 64 + STATS
    tensor = lax.axis_index("tensor")
    if count == 4:
        by_mask = [ref[...] for ref in pieces]
    else:
        by_mask = [pieces[mask % 2][mask // 2] for mask in range(4)]

    def block(place):
        low = [jnp.where(tensor % 2 == place % 2, by_mask[n], by_mask[n + 1]) for n in (0, 2)]
        return jnp.where(tensor // 2 == place // 2, low[0], low[1])

    active = lax.axis_index("pipe") == step

    @pl.when(active)
    def _():
        total = jnp.zeros((rows, 1), F32)
        for place in range(N_TENSOR):
            at = slice(place * cols, (place + 1) * cols)
            wide = block(place).astype(F32)
            total = total + jnp.sum(wide * wide, axis=1, keepdims=True)
            scaled[:, at] = (wide * gain[:, at].astype(F32)).astype(BF16)
        eye = diagonal()
        row = lax.broadcasted_iota(jnp.int32, (STATS, HD), 0)
        lines = jnp.zeros((STATS, HD), F32)
        for b in range(rows // HD):
            line = jnp.sum(
                jnp.where(eye, total[b * HD : (b + 1) * HD], 0.0), axis=0, keepdims=True
            )
            high, low = two_parts(line)
            lines = jnp.where(row == 2 * b, high.astype(F32), lines)
            lines = jnp.where(row == 2 * b + 1, low.astype(F32), lines)
        lines = lines.astype(BF16)
        part = jnp.dot(scaled[...], wkv[...], preferred_element_type=F32).astype(BF16)
        for j in range(heads):
            first = j * pitch + rows
            for c in range(4):
                send[first + 16 * c : first + 16 * c + 16, :] = part[
                    16 * j : 16 * j + 16, c * HD : (c + 1) * HD
                ]
            send[first + 64 : first + 64 + STATS, :] = lines
        for i in range(heads // per):
            part = jnp.dot(
                scaled[...], wq[:, i * per * HD : (i + 1) * per * HD], preferred_element_type=F32
            ).astype(BF16)
            for j in range(per):
                first = (i * per + j) * pitch
                send[first : first + rows, :] = part[:, j * HD : (j + 1) * HD]

    @pl.when(jnp.logical_not(active))
    def _():
        if wout:
            gram_parts(wout[0], lambda h: (send, pl.multiple_of(h * pitch, 16)))
            for j in range(heads):
                first = j * pitch + rows
                send[first : first + 64 + STATS, :] = jnp.zeros((64 + STATS, HD), BF16)
        else:
            send[...] = jnp.zeros_like(send)


def project(step, pieces, gain, wkv, *weights):
    rows, cols = pieces[0].shape[-2:]
    wide = cols * N_TENSOR
    pitch = rows + 64 + STATS
    vmem = pl.BlockSpec(memory_space=VMEM)
    send = pl.pallas_call(
        functools.partial(project_kernel, step, len(pieces)),
        out_shape=jax.ShapeDtypeStruct((N_DP * pitch, HD), BF16),
        in_specs=[vmem] * (len(pieces) + 2 + len(weights)),
        out_specs=vmem,
        scratch_shapes=[VMEM((rows, wide), BF16)],
        compiler_params=pltpu.CompilerParams(vmem_limit_bytes=8 * 2**20),
        name="project",
    )(*pieces, gain, wkv, *weights)
    return send.reshape(N_DP, pitch, HD)


def combine_kernel(step, width, recv, cosine, sine, query, kv, gram, scale):
    rows = cosine.shape[0]
    active = lax.axis_index("pipe") == step

    def total(first, size):
        at = slice(first, first + size)
        value = recv[0, at, :].astype(F32)
        for s in range(1, N_DP):
            value = value + recv[s, at, :].astype(F32)
        return value

    @pl.when(active)
    def _():
        raw = total(0, rows)
        tail = total(rows, 64 + STATS)
        eye = diagonal()
        for b in range(rows // HD):
            line = tail[64 + 2 * b : 65 + 2 * b, :] + tail[65 + 2 * b : 66 + 2 * b, :]
            column = jnp.sum(jnp.where(eye, line, 0.0), axis=1, keepdims=True)
            factor = lax.rsqrt(column / width + EPS_NORM)
            scale[b * HD : (b + 1) * HD, :] = jnp.broadcast_to(factor, (HD, HD))
        query[...] = rotated(raw * scale[...], cosine[...], sine[...]).astype(BF16)
        first = pl.multiple_of(lax.axis_index("dp") * 16, 16)
        here = scale[pl.ds(first, 16), :]
        cos_here = cosine[pl.ds(first, 16), :]
        sin_here = sine[pl.ds(first, 16), :]
        for g in range(2):
            keys = tail[32 * g : 32 * g + 16] * here
            vals = tail[32 * g + 16 : 32 * g + 32] * here
            kv[g, :, :HD] = rotated(keys, cos_here, sin_here).astype(BF16)
            kv[g, :, HD:] = vals.astype(BF16)
        gram[...] = jnp.zeros_like(gram)

    @pl.when(jnp.logical_not(active))
    def _():
        gram[...] = total(0, HD) + total(HD, HD)
        query[...] = jnp.zeros_like(query)
        kv[...] = jnp.zeros_like(kv)


def combine(step, recv, cosine, sine, width):
    rows = cosine.shape[0]
    vmem = pl.BlockSpec(memory_space=VMEM)
    return pl.pallas_call(
        functools.partial(combine_kernel, step, float(width)),
        out_shape=(
            jax.ShapeDtypeStruct((rows, HD), BF16),
            jax.ShapeDtypeStruct((2, 16, 2 * HD), BF16),
            jax.ShapeDtypeStruct((HD, HD), F32),
        ),
        in_specs=[vmem] * 3,
        out_specs=(vmem, vmem, vmem),
        scratch_shapes=[VMEM((rows, HD), F32)],
        compiler_params=pltpu.CompilerParams(vmem_limit_bytes=8 * 2**20),
        name="combine",
    )(recv, cosine, sine)


def choose_kernel(group, own, other, send, picked, four):
    tensor, data = lax.axis_index("tensor"), lax.axis_index("dp")
    chip, core = tensor // 2, tensor % 2
    for n in range(2):
        four[2 * core + n] = own[n]
        four[2 * (1 - core) + n] = other[n]
    for d in range(N_DP):
        for a in range(2):
            wanted = group[(2 * a + core) * N_DP + d]
            block = four[wanted % 4]
            send[2 * d + a] = jnp.where(wanted // 4 == chip, block, jnp.zeros_like(block))
    lane = lax.broadcasted_iota(jnp.int32, picked.shape, 1)
    picked[...] = jnp.where(lane == group[tensor * N_DP + data], 1.0, 0.0).astype(F32)


def choose(group, own, other):
    vmem = pl.BlockSpec(memory_space=VMEM)
    return pl.pallas_call(
        choose_kernel,
        out_shape=(
            jax.ShapeDtypeStruct((2 * N_DP,) + own.shape[1:], BF16),
            jax.ShapeDtypeStruct((8, HD), F32),
        ),
        in_specs=[pl.BlockSpec(memory_space=pltpu.SMEM), vmem, vmem],
        out_specs=(vmem,) * 2,
        scratch_shapes=[VMEM((4,) + own.shape[1:], BF16)],
        compiler_params=pltpu.CompilerParams(vmem_limit_bytes=4 * 2**20),
        name="choose",
    )(group, own, other)


def attended(query, recv, kv):
    rows = query.shape[0]
    few = rows // N_DP
    for d in range(N_DP):
        both = recv[2 * d].astype(F32) + recv[2 * d + 1].astype(F32)
        kv[d * few : (d + 1) * few, :] = both.astype(BF16)
    scores = lax.dot_general(
        query, kv[:, :HD], (((1,), (1,)), ((), ())), preferred_element_type=F32
    )
    allowed = lax.broadcasted_iota(jnp.int32, (rows, rows), 0) >= lax.broadcasted_iota(
        jnp.int32, (rows, rows), 1
    )
    expo = jnp.where(allowed, jnp.exp(scores * (1.0 / math.sqrt(HD))), 0.0)
    weights = (expo / jnp.sum(expo, axis=1, keepdims=True)).astype(BF16)
    return jnp.dot(weights, kv[:, HD:], preferred_element_type=F32).astype(BF16)


def attend_kernel(query, recv, wout, send, kv):
    active = lax.axis_index("pipe") == 0

    @pl.when(active)
    def _():
        result = attended(query[...], recv, kv)
        for j in range(N_DP):
            send[j] = result

    @pl.when(jnp.logical_not(active))
    def _():
        gram_parts(wout, lambda h: (send.at[h], 0))


def attend(query, recv, wout):
    rows = query.shape[0]
    vmem = pl.BlockSpec(memory_space=VMEM)
    return pl.pallas_call(
        attend_kernel,
        out_shape=jax.ShapeDtypeStruct((N_DP, rows, HD), BF16),
        in_specs=[vmem] * 3,
        out_specs=vmem,
        scratch_shapes=[VMEM((rows, 2 * HD), BF16)],
        compiler_params=pltpu.CompilerParams(vmem_limit_bytes=8 * 2**20),
        name="attend",
    )(query, recv, wout)


def attend_last_kernel(width, query, recv, before, gram0, gram1, picked, send, kv):
    rows = query.shape[0]
    result = attended(query[...], recv, kv)
    first_section = lax.axis_index("pipe") == 0
    mine = jnp.where(first_section, before[0], result)
    gram = jnp.where(first_section, gram1[...], gram0[...])
    high, low = two_parts(gram)
    image = jnp.dot(mine, high, preferred_element_type=F32) + jnp.dot(
        mine, low, preferred_element_type=F32
    )
    squares = jnp.sum(image * mine.astype(F32), axis=1, keepdims=True)
    spread = jnp.sqrt(jnp.maximum(squares / width, 0.0) + EPS_RMS)
    mean = jnp.sum(spread, axis=0, keepdims=True) / rows
    high, low = two_parts(mean * picked[0:1, :])
    row = lax.broadcasted_iota(jnp.int32, (STATS, HD), 0)
    lines = jnp.where(row == 0, high.astype(F32), jnp.where(row == 1, low.astype(F32), 0.0))
    lines = lines.astype(BF16)
    for j in range(N_DP):
        send[j, :rows] = result
        send[j, rows:] = lines


def attend_last(query, recv, before, gram0, gram1, picked, width):
    rows = query.shape[0]
    vmem = pl.BlockSpec(memory_space=VMEM)
    return pl.pallas_call(
        functools.partial(attend_last_kernel, float(width)),
        out_shape=jax.ShapeDtypeStruct((N_DP, rows + STATS, HD), BF16),
        in_specs=[vmem] * 6,
        out_specs=vmem,
        scratch_shapes=[VMEM((rows, 2 * HD), BF16)],
        compiler_params=pltpu.CompilerParams(vmem_limit_bytes=8 * 2**20),
        name="attend_last",
    )(query, recv, before, gram0, gram1, picked)


def out_kernel(rows, masks, last, *refs):
    if last:
        recv, saved, wout, parts = refs
    else:
        recv, wout, parts, *gram = refs
    heads = recv.shape[0]
    cols = parts.shape[2]
    tensor = lax.axis_index("tensor")
    active = lax.axis_index("pipe") == (1 if last else 0)
    if last:
        sums = jnp.zeros((1, HD), F32)
        for h in range(heads):
            sums = sums + (
                recv[h, rows : rows + 1, :].astype(F32)
                + recv[h, rows + 1 : rows + 2, :].astype(F32)
            )
        sums = jnp.concatenate([sums, jnp.zeros((1, cols - HD), F32)], axis=1)
        high, low = two_parts(sums)
        row = lax.broadcasted_iota(jnp.int32, (STATS, cols), 0)
        lines = jnp.where(
            row == 0, high.astype(F32), jnp.where(row == 1, low.astype(F32), 0.0)
        ).astype(BF16)
        for n in range(2):
            parts[n, rows:] = lines
    for parity in range(2):

        @pl.when(jnp.logical_and(active, (tensor + masks[0] + parity) % 2 == 0))
        def _():
            for place in (parity, parity + 2):
                total = None
                for h in range(0, heads, 2):
                    pair = jnp.concatenate([recv[h, :rows, :], recv[h + 1, :rows, :]], axis=1)
                    one = jnp.dot(
                        pair,
                        wout[h * HD : (h + 2) * HD, place * cols : (place + 1) * cols],
                        preferred_element_type=F32,
                    )
                    total = one if total is None else total + one
                n = lax.bitwise_xor(tensor, place) // 2
                parts[n, :rows] = total.astype(BF16)

    @pl.when(jnp.logical_not(active))
    def _():
        for n in range(2):
            parts[n, :rows] = saved[n] if last else jnp.zeros((rows, cols), BF16)
        if not last and gram:
            total = jnp.zeros((HD, HD), F32)
            for s in range(heads):
                total = total + (recv[s, :HD].astype(F32) + recv[s, HD : 2 * HD].astype(F32))
            gram[0][...] = total

    if not last and gram:

        @pl.when(active)
        def _():
            gram[0][...] = jnp.zeros((HD, HD), F32)


def project_out(recv, wout, rows, masks, saved=None):
    heads, deep, _ = recv.shape
    cols = wout.shape[1] // N_TENSOR
    last = saved is not None
    vmem = pl.BlockSpec(memory_space=VMEM)
    shapes = (jax.ShapeDtypeStruct((2, deep, cols), BF16),)
    if not last and masks[0] == 0:
        shapes += (jax.ShapeDtypeStruct((HD, HD), F32),)
    operands = (recv, saved, wout) if last else (recv, wout)
    return pl.pallas_call(
        functools.partial(out_kernel, rows, masks, last),
        out_shape=shapes,
        in_specs=[vmem] * len(operands),
        out_specs=(vmem,) * len(shapes),
        compiler_params=pltpu.CompilerParams(vmem_limit_bytes=6 * 2**20),
        cost_estimate=pl.CostEstimate(
            flops=4 * rows * heads * HD * cols, bytes_accessed=2**22, transcendentals=0
        ),
        name="project_out",
    )(*operands)


def pair_kernel(a, b, out):
    out[...] = (a[...].astype(F32) + b[...].astype(F32)).astype(BF16)


def add_pair(a, b):
    vmem = pl.BlockSpec(memory_space=VMEM)
    return pl.pallas_call(
        pair_kernel,
        out_shape=jax.ShapeDtypeStruct(a.shape, BF16),
        in_specs=[vmem] * 2,
        out_specs=vmem,
        compiler_params=pltpu.CompilerParams(vmem_limit_bytes=4 * 2**20),
        name="add_pair",
    )(a, b)


def last_pair_kernel(rows, a, b, out0, out1):
    for n, out in enumerate((out0, out1)):
        total = a[n].astype(F32) + b[n].astype(F32)
        out[:rows] = total[:rows].astype(BF16)
        high, low = two_parts(total[rows : rows + 1] + total[rows + 1 : rows + 2])
        row = lax.broadcasted_iota(jnp.int32, (STATS, out.shape[1]), 0)
        lines = jnp.where(row == 0, high.astype(F32), 0.0)
        out[rows:] = jnp.where(row == 1, low.astype(F32), lines).astype(BF16)


def add_last_pair(a, b, rows):
    vmem = pl.BlockSpec(memory_space=VMEM)
    return pl.pallas_call(
        functools.partial(last_pair_kernel, rows),
        out_shape=(jax.ShapeDtypeStruct(a.shape[1:], BF16),) * 2,
        in_specs=[vmem] * 2,
        out_specs=(vmem,) * 2,
        compiler_params=pltpu.CompilerParams(vmem_limit_bytes=4 * 2**20),
        name="add_last_pair",
    )(a, b)


def next_kernel(wide0, wide1, same, other, fresh):
    fresh[0] = (
        wide0[...].astype(F32) + (same[0].astype(F32) + other[1].astype(F32))
    ).astype(BF16)
    fresh[1] = (
        wide1[...].astype(F32) + (same[1].astype(F32) + other[0].astype(F32))
    ).astype(BF16)


def add_next(wide0, wide1, same, other):
    vmem = pl.BlockSpec(memory_space=VMEM)
    return pl.pallas_call(
        next_kernel,
        out_shape=jax.ShapeDtypeStruct(same.shape, BF16),
        in_specs=[vmem] * 4,
        out_specs=vmem,
        compiler_params=pltpu.CompilerParams(vmem_limit_bytes=4 * 2**20),
        name="add_next",
    )(wide0, wide1, same, other)


def last_kernel(mine, state, here, there, out, importance):
    rows = mine.shape[0]
    total = here[...].astype(F32) + there[...].astype(F32)
    wide = jnp.where(lax.axis_index("pipe") == 0, mine[...], state[0]).astype(F32)
    out[...] = (wide + total[:rows]).astype(BF16)
    importance[...] = total[rows : rows + 1, :HD] + total[rows + 1 : rows + 2, :HD]


def add_last(mine, state, here, there):
    vmem = pl.BlockSpec(memory_space=VMEM)
    return pl.pallas_call(
        last_kernel,
        out_shape=(
            jax.ShapeDtypeStruct(mine.shape, BF16),
            jax.ShapeDtypeStruct((1, HD), F32),
        ),
        in_specs=[vmem] * 4,
        out_specs=(vmem, vmem),
        compiler_params=pltpu.CompilerParams(vmem_limit_bytes=4 * 2**20),
        name="add_last",
    )(mine, state, here, there)


def swap(block, mask):
    return lax.ppermute(block, "tensor", [(t, t ^ mask) for t in range(N_TENSOR)])


def to_next_section(block, mask):
    route = [(t, N_TENSOR + (t ^ mask)) for t in range(N_TENSOR)]
    return lax.ppermute(block, ("pipe", "tensor"), route)


def local(hidden_in, norm_gain, w_query, w_keyval, w_out, head_group):
    rows, cols = hidden_in.shape[0], hidden_in.shape[3]
    width = cols * N_TENSOR * N_DP
    wq, wout = w_query[0], w_out[0]
    wkv = load(wq, w_keyval[0])
    cosine, sine = map(jnp.asarray, rotary_tables(rows))

    runs = [
        [d * N_TENSOR + 2 * a + core for d in range(N_DP) for a in range(2)] for core in range(2)
    ]

    def to_heads(step, pieces, *weights):
        send = project(step, pieces, norm_gain, wkv, wq, *weights)
        recv = lax.all_to_all(send, "dp", 0, 0)
        query, kv, gram = combine(step, recv, cosine, sine, width)
        send, picked = choose(head_group, kv, swap(kv, 1))
        recv = lax.all_to_all(send, ("dp", "tensor"), 0, 0, axis_index_groups=runs)
        return query, recv, gram, picked

    mine = hidden_in.reshape(rows, cols)
    far = swap(mine, 2)
    query, kv, _, _ = to_heads(0, (mine, swap(mine, 1), far, swap(mine, 3)))
    att0 = attend(query, kv, wout)
    recv = lax.all_to_all(att0, "dp", 0, 0)
    (other0,) = project_out(recv, wout, rows, (1, 3))
    own0, gram0 = project_out(recv, wout, rows, (0, 2))
    here = add_pair(own0, swap(other0, 1))
    state = add_next(mine, far, to_next_section(here, 0), to_next_section(here, 2))

    query, kv, gram1, picked = to_heads(1, (state, swap(state, 1)), wout)
    att1 = attend_last(query, kv, att0, gram0, gram1, picked, width)
    recv = lax.all_to_all(att1, "dp", 0, 0)
    (other1,) = project_out(recv, wout, rows, (1, 3), other0)
    (own1,) = project_out(recv, wout, rows, (0, 2), own0)
    here, away = add_last_pair(own1, swap(other1, 1), rows)
    out, importance = add_last(mine, state, here, swap(away, 2))
    return out.reshape(1, rows, 1, 1, cols), importance[:, :GROUPS]


def solution(mesh):
    in_specs = (
        P(None, "dp", "tensor", None),
        P("pipe", "dp"),
        P("pipe", "dp", "tensor"),
        P("pipe", "dp", "tensor", None),
        P("pipe", "tensor", "dp"),
        P(),
    )
    out_specs = (P("pipe", None, "dp", "tensor", None), P("pipe", None))
    return jax.shard_map(local, mesh=mesh, in_specs=in_specs, out_specs=out_specs, check_vma=False)
```

```python
import functools
import math

import jax
import jax.numpy as jnp
import numpy as np
from jax import lax
from jax.experimental import pallas as pl
from jax.experimental.pallas import tpu as pltpu
from jax.sharding import PartitionSpec as P

HD = 128
GROUPS = 8
N_TENSOR = 4
N_DP = 16
THETA = 500000.0
EPS_NORM = 1e-05
EPS_RMS = 1e-06
STATS = 16

BF16 = jnp.bfloat16
F32 = jnp.float32
VMEM = pltpu.VMEM


def rotary_tables(rows):
    positions = np.arange(rows, dtype=np.float64)[:, None]
    lanes = np.arange(HD)
    angle = positions * THETA ** (-2.0 * (lanes // 2) / HD)[None, :]
    sign = np.where(lanes % 2 == 0, -1.0, 1.0)[None, :]
    return np.cos(angle).astype(np.float32), (np.sin(angle) * sign).astype(np.float32)


def rotated(values, cosine, sine):
    lanes = lax.broadcasted_iota(jnp.int32, values.shape, 1)
    swapped = jnp.where(
        lanes % 2 == 0, pltpu.roll(values, HD - 1, 1), pltpu.roll(values, 1, 1)
    )
    return values * cosine + swapped * sine


def diagonal():
    return lax.broadcasted_iota(jnp.int32, (HD, HD), 0) == lax.broadcasted_iota(
        jnp.int32, (HD, HD), 1
    )


def two_parts(values):
    high = values.astype(BF16)
    return high, (values - high.astype(F32)).astype(BF16)


def load_kernel(wq, wkv, out):
    cols = wkv.shape[2]
    for g in range(wkv.shape[1]):
        out[:, g * cols : (g + 1) * cols] = wkv[:, g, :]


def load(wq, wkv):
    vmem = pl.BlockSpec(memory_space=VMEM)
    return pl.pallas_call(
        load_kernel,
        out_shape=jax.ShapeDtypeStruct((wkv.shape[0], wkv.shape[1] * wkv.shape[2]), BF16),
        in_specs=[vmem] * 2,
        out_specs=vmem,
        compiler_params=pltpu.CompilerParams(vmem_limit_bytes=12 * 2**20),
        cost_estimate=pl.CostEstimate(flops=10**9, bytes_accessed=10**7, transcendentals=0),
        name="load",
    )(wq, wkv)


def gram_parts(wout, target):
    @pl.loop(0, wout.shape[0] // (2 * HD))
    def _(i):
        pair = wout[pl.ds(pl.multiple_of(i * 2 * HD, 2 * HD), 2 * HD), :]
        both = lax.dot_general(pair, pair, (((1,), (1,)), ((), ())), preferred_element_type=F32)
        for n in range(2):
            high, low = two_parts(both[n * HD : (n + 1) * HD, n * HD : (n + 1) * HD])
            ref, first = target(2 * i + n)
            ref[pl.ds(first, HD), :] = high
            ref[pl.ds(first + HD, HD), :] = low


def project_kernel(step, count, *refs):
    pieces, refs = refs[:count], refs[count:]
    gain, wkv, wq, *wout, send, scaled = refs
    rows, cols = pieces[0].shape[-2:]
    per = 4
    heads = N_DP
    pitch = rows + 64 + STATS
    tensor = lax.axis_index("tensor")
    if count == 4:
        by_mask = [ref[...] for ref in pieces]
    else:
        by_mask = [pieces[mask % 2][mask // 2] for mask in range(4)]

    def block(place):
        low = [jnp.where(tensor % 2 == place % 2, by_mask[n], by_mask[n + 1]) for n in (0, 2)]
        return jnp.where(tensor // 2 == place // 2, low[0], low[1])

    active = lax.axis_index("pipe") == step

    @pl.when(active)
    def _():
        total = jnp.zeros((rows, 1), F32)
        for place in range(N_TENSOR):
            at = slice(place * cols, (place + 1) * cols)
            wide = block(place).astype(F32)
            total = total + jnp.sum(wide * wide, axis=1, keepdims=True)
            scaled[:, at] = (wide * gain[:, at].astype(F32)).astype(BF16)
        eye = diagonal()
        row = lax.broadcasted_iota(jnp.int32, (STATS, HD), 0)
        lines = jnp.zeros((STATS, HD), F32)
        for b in range(rows // HD):
            line = jnp.sum(
                jnp.where(eye, total[b * HD : (b + 1) * HD], 0.0), axis=0, keepdims=True
            )
            high, low = two_parts(line)
            lines = jnp.where(row == 2 * b, high.astype(F32), lines)
            lines = jnp.where(row == 2 * b + 1, low.astype(F32), lines)
        lines = lines.astype(BF16)
        part = jnp.dot(scaled[...], wkv[...], preferred_element_type=F32).astype(BF16)
        for j in range(heads):
            first = j * pitch + rows
            for c in range(4):
                send[first + 16 * c : first + 16 * c + 16, :] = part[
                    16 * j : 16 * j + 16, c * HD : (c + 1) * HD
                ]
            send[first + 64 : first + 64 + STATS, :] = lines
        for i in range(heads // per):
            part = jnp.dot(
                scaled[...], wq[:, i * per * HD : (i + 1) * per * HD], preferred_element_type=F32
            ).astype(BF16)
            for j in range(per):
                first = (i * per + j) * pitch
                send[first : first + rows, :] = part[:, j * HD : (j + 1) * HD]

    @pl.when(jnp.logical_not(active))
    def _():
        if wout:
            gram_parts(wout[0], lambda h: (send, pl.multiple_of(h * pitch, 16)))
            for j in range(heads):
                first = j * pitch + rows
                send[first : first + 64 + STATS, :] = jnp.zeros((64 + STATS, HD), BF16)
        else:
            send[...] = jnp.zeros_like(send)


def project(step, pieces, gain, wkv, *weights):
    rows, cols = pieces[0].shape[-2:]
    wide = cols * N_TENSOR
    pitch = rows + 64 + STATS
    vmem = pl.BlockSpec(memory_space=VMEM)
    send = pl.pallas_call(
        functools.partial(project_kernel, step, len(pieces)),
        out_shape=jax.ShapeDtypeStruct((N_DP * pitch, HD), BF16),
        in_specs=[vmem] * (len(pieces) + 2 + len(weights)),
        out_specs=vmem,
        scratch_shapes=[VMEM((rows, wide), BF16)],
        compiler_params=pltpu.CompilerParams(vmem_limit_bytes=8 * 2**20),
        name="project",
    )(*pieces, gain, wkv, *weights)
    return send.reshape(N_DP, pitch, HD)


def combine_kernel(step, width, recv, cosine, sine, query, kv, gram, scale):
    rows = cosine.shape[0]
    active = lax.axis_index("pipe") == step

    def total(first, size):
        at = slice(first, first + size)
        value = recv[0, at, :].astype(F32)
        for s in range(1, N_DP):
            value = value + recv[s, at, :].astype(F32)
        return value

    @pl.when(active)
    def _():
        raw = total(0, rows)
        tail = total(rows, 64 + STATS)
        eye = diagonal()
        for b in range(rows // HD):
            line = tail[64 + 2 * b : 65 + 2 * b, :] + tail[65 + 2 * b : 66 + 2 * b, :]
            column = jnp.sum(jnp.where(eye, line, 0.0), axis=1, keepdims=True)
            factor = lax.rsqrt(column / width + EPS_NORM)
            scale[b * HD : (b + 1) * HD, :] = jnp.broadcast_to(factor, (HD, HD))
        query[...] = rotated(raw * scale[...], cosine[...], sine[...]).astype(BF16)
        first = pl.multiple_of(lax.axis_index("dp") * 16, 16)
        here = scale[pl.ds(first, 16), :]
        cos_here = cosine[pl.ds(first, 16), :]
        sin_here = sine[pl.ds(first, 16), :]
        for g in range(2):
            keys = tail[32 * g : 32 * g + 16] * here
            vals = tail[32 * g + 16 : 32 * g + 32] * here
            kv[g, :, :HD] = rotated(keys, cos_here, sin_here).astype(BF16)
            kv[g, :, HD:] = vals.astype(BF16)
        gram[...] = jnp.zeros_like(gram)

    @pl.when(jnp.logical_not(active))
    def _():
        gram[...] = total(0, HD) + total(HD, HD)
        query[...] = jnp.zeros_like(query)
        kv[...] = jnp.zeros_like(kv)


def combine(step, recv, cosine, sine, width):
    rows = cosine.shape[0]
    vmem = pl.BlockSpec(memory_space=VMEM)
    return pl.pallas_call(
        functools.partial(combine_kernel, step, float(width)),
        out_shape=(
            jax.ShapeDtypeStruct((rows, HD), BF16),
            jax.ShapeDtypeStruct((2, 16, 2 * HD), BF16),
            jax.ShapeDtypeStruct((HD, HD), F32),
        ),
        in_specs=[vmem] * 3,
        out_specs=(vmem, vmem, vmem),
        scratch_shapes=[VMEM((rows, HD), F32)],
        compiler_params=pltpu.CompilerParams(vmem_limit_bytes=8 * 2**20),
        name="combine",
    )(recv, cosine, sine)


def choose_kernel(group, own, other, send, picked, four):
    tensor, data = lax.axis_index("tensor"), lax.axis_index("dp")
    chip, core = tensor // 2, tensor % 2
    for n in range(2):
        four[2 * core + n] = own[n]
        four[2 * (1 - core) + n] = other[n]
    for d in range(N_DP):
        for a in range(2):
            wanted = group[(2 * a + core) * N_DP + d]
            block = four[wanted % 4]
            send[2 * d + a] = jnp.where(wanted // 4 == chip, block, jnp.zeros_like(block))
    lane = lax.broadcasted_iota(jnp.int32, picked.shape, 1)
    picked[...] = jnp.where(lane == group[tensor * N_DP + data], 1.0, 0.0).astype(F32)


def choose(group, own, other):
    vmem = pl.BlockSpec(memory_space=VMEM)
    return pl.pallas_call(
        choose_kernel,
        out_shape=(
            jax.ShapeDtypeStruct((2 * N_DP,) + own.shape[1:], BF16),
            jax.ShapeDtypeStruct((8, HD), F32),
        ),
        in_specs=[pl.BlockSpec(memory_space=pltpu.SMEM), vmem, vmem],
        out_specs=(vmem,) * 2,
        scratch_shapes=[VMEM((4,) + own.shape[1:], BF16)],
        compiler_params=pltpu.CompilerParams(vmem_limit_bytes=4 * 2**20),
        name="choose",
    )(group, own, other)


def attended(query, recv, kv):
    rows = query.shape[0]
    few = rows // N_DP
    for d in range(N_DP):
        both = recv[2 * d].astype(F32) + recv[2 * d + 1].astype(F32)
        kv[d * few : (d + 1) * few, :] = both.astype(BF16)
    scores = lax.dot_general(
        query, kv[:, :HD], (((1,), (1,)), ((), ())), preferred_element_type=F32
    )
    allowed = lax.broadcasted_iota(jnp.int32, (rows, rows), 0) >= lax.broadcasted_iota(
        jnp.int32, (rows, rows), 1
    )
    expo = jnp.where(allowed, jnp.exp(scores * (1.0 / math.sqrt(HD))), 0.0)
    weights = (expo / jnp.sum(expo, axis=1, keepdims=True)).astype(BF16)
    return jnp.dot(weights, kv[:, HD:], preferred_element_type=F32).astype(BF16)


def attend_kernel(query, recv, wout, send, kv):
    active = lax.axis_index("pipe") == 0

    @pl.when(active)
    def _():
        result = attended(query[...], recv, kv)
        for j in range(N_DP):
            send[j] = result

    @pl.when(jnp.logical_not(active))
    def _():
        gram_parts(wout, lambda h: (send.at[h], 0))


def attend(query, recv, wout):
    rows = query.shape[0]
    vmem = pl.BlockSpec(memory_space=VMEM)
    return pl.pallas_call(
        attend_kernel,
        out_shape=jax.ShapeDtypeStruct((N_DP, rows, HD), BF16),
        in_specs=[vmem] * 3,
        out_specs=vmem,
        scratch_shapes=[VMEM((rows, 2 * HD), BF16)],
        compiler_params=pltpu.CompilerParams(vmem_limit_bytes=8 * 2**20),
        name="attend",
    )(query, recv, wout)


def attend_last_kernel(width, query, recv, before, gram0, gram1, picked, send, kv):
    rows = query.shape[0]
    result = attended(query[...], recv, kv)
    first_section = lax.axis_index("pipe") == 0
    mine = jnp.where(first_section, before[0], result)
    gram = jnp.where(first_section, gram1[...], gram0[...])
    high, low = two_parts(gram)
    image = jnp.dot(mine, high, preferred_element_type=F32) + jnp.dot(
        mine, low, preferred_element_type=F32
    )
    squares = jnp.sum(image * mine.astype(F32), axis=1, keepdims=True)
    spread = jnp.sqrt(jnp.maximum(squares / width, 0.0) + EPS_RMS)
    mean = jnp.sum(spread, axis=0, keepdims=True) / rows
    high, low = two_parts(mean * picked[0:1, :])
    row = lax.broadcasted_iota(jnp.int32, (STATS, HD), 0)
    lines = jnp.where(row == 0, high.astype(F32), jnp.where(row == 1, low.astype(F32), 0.0))
    lines = lines.astype(BF16)
    for j in range(N_DP):
        send[j, :rows] = result
        send[j, rows:] = lines


def attend_last(query, recv, before, gram0, gram1, picked, width):
    rows = query.shape[0]
    vmem = pl.BlockSpec(memory_space=VMEM)
    return pl.pallas_call(
        functools.partial(attend_last_kernel, float(width)),
        out_shape=jax.ShapeDtypeStruct((N_DP, rows + STATS, HD), BF16),
        in_specs=[vmem] * 6,
        out_specs=vmem,
        scratch_shapes=[VMEM((rows, 2 * HD), BF16)],
        compiler_params=pltpu.CompilerParams(vmem_limit_bytes=8 * 2**20),
        name="attend_last",
    )(query, recv, before, gram0, gram1, picked)


def out_kernel(rows, masks, last, *refs):
    if last:
        recv, saved, wout, parts = refs
    else:
        recv, wout, parts, *gram = refs
    heads = recv.shape[0]
    cols = parts.shape[2]
    tensor = lax.axis_index("tensor")
    active = lax.axis_index("pipe") == (1 if last else 0)
    if last:
        sums = jnp.zeros((1, HD), F32)
        for h in range(heads):
            sums = sums + (
                recv[h, rows : rows + 1, :].astype(F32)
                + recv[h, rows + 1 : rows + 2, :].astype(F32)
            )
        sums = jnp.concatenate([sums, jnp.zeros((1, cols - HD), F32)], axis=1)
        high, low = two_parts(sums)
        row = lax.broadcasted_iota(jnp.int32, (STATS, cols), 0)
        lines = jnp.where(
            row == 0, high.astype(F32), jnp.where(row == 1, low.astype(F32), 0.0)
        ).astype(BF16)
        for n in range(2):
            parts[n, rows:] = lines
    for parity in range(2):

        @pl.when(jnp.logical_and(active, (tensor + masks[0] + parity) % 2 == 0))
        def _():
            for place in (parity, parity + 2):
                total = None
                for h in range(0, heads, 2):
                    pair = jnp.concatenate([recv[h, :rows, :], recv[h + 1, :rows, :]], axis=1)
                    one = jnp.dot(
                        pair,
                        wout[h * HD : (h + 2) * HD, place * cols : (place + 1) * cols],
                        preferred_element_type=F32,
                    )
                    total = one if total is None else total + one
                n = lax.bitwise_xor(tensor, place) // 2
                parts[n, :rows] = total.astype(BF16)

    @pl.when(jnp.logical_not(active))
    def _():
        for n in range(2):
            parts[n, :rows] = saved[n] if last else jnp.zeros((rows, cols), BF16)
        if not last and gram:
            total = jnp.zeros((HD, HD), F32)
            for s in range(heads):
                total = total + (recv[s, :HD].astype(F32) + recv[s, HD : 2 * HD].astype(F32))
            gram[0][...] = total

    if not last and gram:

        @pl.when(active)
        def _():
            gram[0][...] = jnp.zeros((HD, HD), F32)


def project_out(recv, wout, rows, masks, saved=None):
    heads, deep, _ = recv.shape
    cols = wout.shape[1] // N_TENSOR
    last = saved is not None
    vmem = pl.BlockSpec(memory_space=VMEM)
    shapes = (jax.ShapeDtypeStruct((2, deep, cols), BF16),)
    if not last and masks[0] == 0:
        shapes += (jax.ShapeDtypeStruct((HD, HD), F32),)
    operands = (recv, saved, wout) if last else (recv, wout)
    return pl.pallas_call(
        functools.partial(out_kernel, rows, masks, last),
        out_shape=shapes,
        in_specs=[vmem] * len(operands),
        out_specs=(vmem,) * len(shapes),
        compiler_params=pltpu.CompilerParams(vmem_limit_bytes=6 * 2**20),
        cost_estimate=pl.CostEstimate(
            flops=4 * rows * heads * HD * cols, bytes_accessed=2**22, transcendentals=0
        ),
        name="project_out",
    )(*operands)


def pair_kernel(a, b, out0, out1):
    for n, out in enumerate((out0, out1)):
        out[...] = (a[n].astype(F32) + b[n].astype(F32)).astype(BF16)


def add_pair(a, b):
    vmem = pl.BlockSpec(memory_space=VMEM)
    return pl.pallas_call(
        pair_kernel,
        out_shape=(jax.ShapeDtypeStruct(a.shape[1:], BF16),) * 2,
        in_specs=[vmem] * 2,
        out_specs=(vmem,) * 2,
        compiler_params=pltpu.CompilerParams(vmem_limit_bytes=4 * 2**20),
        name="add_pair",
    )(a, b)


def last_pair_kernel(rows, a, b, out0, out1):
    for n, out in enumerate((out0, out1)):
        total = a[n].astype(F32) + b[n].astype(F32)
        out[:rows] = total[:rows].astype(BF16)
        high, low = two_parts(total[rows : rows + 1] + total[rows + 1 : rows + 2])
        row = lax.broadcasted_iota(jnp.int32, (STATS, out.shape[1]), 0)
        lines = jnp.where(row == 0, high.astype(F32), 0.0)
        out[rows:] = jnp.where(row == 1, low.astype(F32), lines).astype(BF16)


def add_last_pair(a, b, rows):
    vmem = pl.BlockSpec(memory_space=VMEM)
    return pl.pallas_call(
        functools.partial(last_pair_kernel, rows),
        out_shape=(jax.ShapeDtypeStruct(a.shape[1:], BF16),) * 2,
        in_specs=[vmem] * 2,
        out_specs=(vmem,) * 2,
        compiler_params=pltpu.CompilerParams(vmem_limit_bytes=4 * 2**20),
        name="add_last_pair",
    )(a, b)


def next_kernel(wide, here, there, fresh):
    fresh[...] = (
        wide[...].astype(F32) + (here[...].astype(F32) + there[...].astype(F32))
    ).astype(BF16)


def add_next(wide, here, there):
    vmem = pl.BlockSpec(memory_space=VMEM)
    return pl.pallas_call(
        next_kernel,
        out_shape=jax.ShapeDtypeStruct(wide.shape, BF16),
        in_specs=[vmem] * 3,
        out_specs=vmem,
        compiler_params=pltpu.CompilerParams(vmem_limit_bytes=4 * 2**20),
        name="add_next",
    )(wide, here, there)


def last_kernel(mine, state, here, there, out, importance):
    rows = mine.shape[0]
    total = here[...].astype(F32) + there[...].astype(F32)
    wide = jnp.where(lax.axis_index("pipe") == 0, mine[...], state[...]).astype(F32)
    out[...] = (wide + total[:rows]).astype(BF16)
    importance[...] = total[rows : rows + 1, :HD] + total[rows + 1 : rows + 2, :HD]


def add_last(mine, state, here, there):
    vmem = pl.BlockSpec(memory_space=VMEM)
    return pl.pallas_call(
        last_kernel,
        out_shape=(
            jax.ShapeDtypeStruct(mine.shape, BF16),
            jax.ShapeDtypeStruct((1, HD), F32),
        ),
        in_specs=[vmem] * 4,
        out_specs=(vmem, vmem),
        compiler_params=pltpu.CompilerParams(vmem_limit_bytes=4 * 2**20),
        name="add_last",
    )(mine, state, here, there)


def swap(block, *masks):
    route = [
        (p * N_TENSOR + t, p * N_TENSOR + (t ^ masks[min(p, len(masks) - 1)]))
        for p in range(2)
        for t in range(N_TENSOR)
    ]
    return lax.ppermute(block, ("pipe", "tensor"), route)


def to_next_section(block, mask):
    route = [(t, N_TENSOR + (t ^ mask)) for t in range(N_TENSOR)]
    return lax.ppermute(block, ("pipe", "tensor"), route)


def local(hidden_in, norm_gain, w_query, w_keyval, w_out, head_group):
    rows, cols = hidden_in.shape[0], hidden_in.shape[3]
    width = cols * N_TENSOR * N_DP
    wq, wout = w_query[0], w_out[0]
    wkv = load(wq, w_keyval[0])
    cosine, sine = map(jnp.asarray, rotary_tables(rows))

    runs = [
        [d * N_TENSOR + 2 * a + core for d in range(N_DP) for a in range(2)] for core in range(2)
    ]

    def to_heads(step, pieces, *weights):
        send = project(step, pieces, norm_gain, wkv, wq, *weights)
        recv = lax.all_to_all(send, "dp", 0, 0)
        query, kv, gram = combine(step, recv, cosine, sine, width)
        send, picked = choose(head_group, kv, swap(kv, 1))
        recv = lax.all_to_all(send, ("dp", "tensor"), 0, 0, axis_index_groups=runs)
        return query, recv, gram, picked

    mine = hidden_in.reshape(rows, cols)
    pieces = (mine, swap(mine, 1), swap(mine, 2, 1), swap(mine, 3, 1))
    query, kv, _, _ = to_heads(0, pieces)
    att0 = attend(query, kv, wout)
    recv = lax.all_to_all(att0, "dp", 0, 0)
    (other0,) = project_out(recv, wout, rows, (1, 3))
    own0, gram0 = project_out(recv, wout, rows, (0, 2))
    here, away = add_pair(own0, swap(other0, 1))
    fresh = add_next(mine, here, swap(away, 2, 1))
    far = to_next_section(fresh, 2)
    near = to_next_section(fresh, 0)

    query, kv, gram1, picked = to_heads(1, (near, swap(near, 1), far, swap(far, 1)), wout)
    att1 = attend_last(query, kv, att0, gram0, gram1, picked, width)
    recv = lax.all_to_all(att1, "dp", 0, 0)
    (other1,) = project_out(recv, wout, rows, (1, 3), other0)
    (own1,) = project_out(recv, wout, rows, (0, 2), own0)
    here, away = add_last_pair(own1, swap(other1, 1), rows)
    out, importance = add_last(mine, near, here, swap(away, 2))
    return out.reshape(1, rows, 1, 1, cols), importance[:, :GROUPS]


def solution(mesh):
    in_specs = (
        P(None, "dp", "tensor", None),
        P("pipe", "dp"),
        P("pipe", "dp", "tensor"),
        P("pipe", "dp", "tensor", None),
        P("pipe", "tensor", "dp"),
        P(),
    )
    out_specs = (P("pipe", None, "dp", "tensor", None), P("pipe", None))
    return jax.shard_map(local, mesh=mesh, in_specs=in_specs, out_specs=out_specs, check_vma=False)
```

```python
import functools
import math

import jax
import jax.numpy as jnp
import numpy as np
from jax import lax
from jax.experimental import pallas as pl
from jax.experimental.pallas import tpu as pltpu
from jax.sharding import PartitionSpec as P

HD = 128
GROUPS = 8
N_TENSOR = 4
N_DP = 16
THETA = 500000.0
EPS_NORM = 1e-05
EPS_RMS = 1e-06
STATS = 16

BF16 = jnp.bfloat16
F32 = jnp.float32
VMEM = pltpu.VMEM


def rotary_tables(rows):
    positions = np.arange(rows, dtype=np.float64)[:, None]
    lanes = np.arange(HD)
    angle = positions * THETA ** (-2.0 * (lanes // 2) / HD)[None, :]
    sign = np.where(lanes % 2 == 0, -1.0, 1.0)[None, :]
    return np.cos(angle).astype(np.float32), (np.sin(angle) * sign).astype(np.float32)


def rotated(values, cosine, sine):
    lanes = lax.broadcasted_iota(jnp.int32, values.shape, 1)
    swapped = jnp.where(
        lanes % 2 == 0, pltpu.roll(values, HD - 1, 1), pltpu.roll(values, 1, 1)
    )
    return values * cosine + swapped * sine


def diagonal():
    return lax.broadcasted_iota(jnp.int32, (HD, HD), 0) == lax.broadcasted_iota(
        jnp.int32, (HD, HD), 1
    )


def two_parts(values):
    high = values.astype(BF16)
    return high, (values - high.astype(F32)).astype(BF16)


def ready_kernel(gain, wq, wkv, out):
    out[...] = jnp.zeros_like(out)


def ready(gain, wq, wkv):
    vmem = pl.BlockSpec(memory_space=VMEM)
    return pl.pallas_call(
        ready_kernel,
        out_shape=jax.ShapeDtypeStruct((16, HD), BF16),
        in_specs=[vmem] * 3,
        out_specs=vmem,
        compiler_params=pltpu.CompilerParams(vmem_limit_bytes=12 * 2**20),
        cost_estimate=pl.CostEstimate(flops=10**9, bytes_accessed=10**7, transcendentals=0),
        name="ready",
    )(gain, wq, wkv)


def hand_on_kernel(block, tile, out):
    out[...] = block[...]


def hand_on(block, tile):
    vmem = pl.BlockSpec(memory_space=VMEM)
    return pl.pallas_call(
        hand_on_kernel,
        out_shape=jax.ShapeDtypeStruct(block.shape, BF16),
        in_specs=[vmem] * 2,
        out_specs=vmem,
        compiler_params=pltpu.CompilerParams(vmem_limit_bytes=2 * 2**20),
        name="hand_on",
    )(block, tile)


def gram_parts(wout, target):
    @pl.loop(0, wout.shape[0] // (2 * HD))
    def _(i):
        pair = wout[pl.ds(pl.multiple_of(i * 2 * HD, 2 * HD), 2 * HD), :]
        both = lax.dot_general(pair, pair, (((1,), (1,)), ((), ())), preferred_element_type=F32)
        for n in range(2):
            high, low = two_parts(both[n * HD : (n + 1) * HD, n * HD : (n + 1) * HD])
            ref, first = target(2 * i + n)
            ref[pl.ds(first, HD), :] = high
            ref[pl.ds(first + HD, HD), :] = low


def project_kernel(step, count, *refs):
    pieces, refs = refs[:count], refs[count:]
    gain, wkv, wq, *wout, send, scaled = refs
    rows, cols = pieces[0].shape[-2:]
    per = 4
    heads = N_DP
    pitch = rows + 64 + STATS
    tensor = lax.axis_index("tensor")
    if count == 4:
        by_mask = [ref[...] for ref in pieces]
    else:
        by_mask = [pieces[mask % 2][mask // 2] for mask in range(4)]

    def block(place):
        low = [jnp.where(tensor % 2 == place % 2, by_mask[n], by_mask[n + 1]) for n in (0, 2)]
        return jnp.where(tensor // 2 == place // 2, low[0], low[1])

    active = lax.axis_index("pipe") == step

    @pl.when(active)
    def _():
        total = jnp.zeros((rows, 1), F32)
        for place in range(N_TENSOR):
            at = slice(place * cols, (place + 1) * cols)
            wide = block(place).astype(F32)
            total = total + jnp.sum(wide * wide, axis=1, keepdims=True)
            scaled[:, at] = (wide * gain[:, at].astype(F32)).astype(BF16)
        eye = diagonal()
        row = lax.broadcasted_iota(jnp.int32, (STATS, HD), 0)
        lines = jnp.zeros((STATS, HD), F32)
        for b in range(rows // HD):
            line = jnp.sum(
                jnp.where(eye, total[b * HD : (b + 1) * HD], 0.0), axis=0, keepdims=True
            )
            high, low = two_parts(line)
            lines = jnp.where(row == 2 * b, high.astype(F32), lines)
            lines = jnp.where(row == 2 * b + 1, low.astype(F32), lines)
        lines = lines.astype(BF16)
        part = jnp.dot(scaled[...], wkv[...], preferred_element_type=F32).astype(BF16)
        for j in range(heads):
            first = j * pitch + rows
            for c in range(4):
                send[first + 16 * c : first + 16 * c + 16, :] = part[
                    16 * j : 16 * j + 16, c * HD : (c + 1) * HD
                ]
            send[first + 64 : first + 64 + STATS, :] = lines
        for i in range(heads // per):
            part = jnp.dot(
                scaled[...], wq[:, i * per * HD : (i + 1) * per * HD], preferred_element_type=F32
            ).astype(BF16)
            for j in range(per):
                first = (i * per + j) * pitch
                send[first : first + rows, :] = part[:, j * HD : (j + 1) * HD]

    @pl.when(jnp.logical_not(active))
    def _():
        if wout:
            gram_parts(wout[0], lambda h: (send, pl.multiple_of(h * pitch, 16)))
            for j in range(heads):
                first = j * pitch + rows
                send[first : first + 64 + STATS, :] = jnp.zeros((64 + STATS, HD), BF16)
        else:
            send[...] = jnp.zeros_like(send)


def project(step, pieces, gain, wkv, *weights):
    rows, cols = pieces[0].shape[-2:]
    wide = cols * N_TENSOR
    pitch = rows + 64 + STATS
    vmem = pl.BlockSpec(memory_space=VMEM)
    send = pl.pallas_call(
        functools.partial(project_kernel, step, len(pieces)),
        out_shape=jax.ShapeDtypeStruct((N_DP * pitch, HD), BF16),
        in_specs=[vmem] * (len(pieces) + 2 + len(weights)),
        out_specs=vmem,
        scratch_shapes=[VMEM((rows, wide), BF16)],
        compiler_params=pltpu.CompilerParams(vmem_limit_bytes=8 * 2**20),
        name="project",
    )(*pieces, gain, wkv, *weights)
    return send.reshape(N_DP, pitch, HD)


def combine_kernel(step, width, recv, cosine, sine, query, kv, gram, scale):
    rows = cosine.shape[0]
    active = lax.axis_index("pipe") == step

    def total(first, size):
        at = slice(first, first + size)
        value = recv[0, at, :].astype(F32)
        for s in range(1, N_DP):
            value = value + recv[s, at, :].astype(F32)
        return value

    @pl.when(active)
    def _():
        raw = total(0, rows)
        tail = total(rows, 64 + STATS)
        eye = diagonal()
        for b in range(rows // HD):
            line = tail[64 + 2 * b : 65 + 2 * b, :] + tail[65 + 2 * b : 66 + 2 * b, :]
            column = jnp.sum(jnp.where(eye, line, 0.0), axis=1, keepdims=True)
            factor = lax.rsqrt(column / width + EPS_NORM)
            scale[b * HD : (b + 1) * HD, :] = jnp.broadcast_to(factor, (HD, HD))
        query[...] = rotated(raw * scale[...], cosine[...], sine[...]).astype(BF16)
        first = pl.multiple_of(lax.axis_index("dp") * 16, 16)
        here = scale[pl.ds(first, 16), :]
        cos_here = cosine[pl.ds(first, 16), :]
        sin_here = sine[pl.ds(first, 16), :]
        for g in range(2):
            keys = tail[32 * g : 32 * g + 16] * here
            vals = tail[32 * g + 16 : 32 * g + 32] * here
            kv[g, :, :HD] = rotated(keys, cos_here, sin_here).astype(BF16)
            kv[g, :, HD:] = vals.astype(BF16)
        gram[...] = jnp.zeros_like(gram)

    @pl.when(jnp.logical_not(active))
    def _():
        gram[...] = total(0, HD) + total(HD, HD)
        query[...] = jnp.zeros_like(query)
        kv[...] = jnp.zeros_like(kv)


def combine(step, recv, cosine, sine, width):
    rows = cosine.shape[0]
    vmem = pl.BlockSpec(memory_space=VMEM)
    return pl.pallas_call(
        functools.partial(combine_kernel, step, float(width)),
        out_shape=(
            jax.ShapeDtypeStruct((rows, HD), BF16),
            jax.ShapeDtypeStruct((2, 16, 2 * HD), BF16),
            jax.ShapeDtypeStruct((HD, HD), F32),
        ),
        in_specs=[vmem] * 3,
        out_specs=(vmem, vmem, vmem),
        scratch_shapes=[VMEM((rows, HD), F32)],
        compiler_params=pltpu.CompilerParams(vmem_limit_bytes=8 * 2**20),
        name="combine",
    )(recv, cosine, sine)


def choose_kernel(group, own, other, send, picked, four):
    tensor, data = lax.axis_index("tensor"), lax.axis_index("dp")
    chip, core = tensor // 2, tensor % 2
    for n in range(2):
        four[2 * core + n] = own[n]
        four[2 * (1 - core) + n] = other[n]
    for d in range(N_DP):
        for a in range(2):
            wanted = group[(2 * a + core) * N_DP + d]
            block = four[wanted % 4]
            send[2 * d + a] = jnp.where(wanted // 4 == chip, block, jnp.zeros_like(block))
    lane = lax.broadcasted_iota(jnp.int32, picked.shape, 1)
    picked[...] = jnp.where(lane == group[tensor * N_DP + data], 1.0, 0.0).astype(F32)


def choose(group, own, other):
    vmem = pl.BlockSpec(memory_space=VMEM)
    return pl.pallas_call(
        choose_kernel,
        out_shape=(
            jax.ShapeDtypeStruct((2 * N_DP,) + own.shape[1:], BF16),
            jax.ShapeDtypeStruct((8, HD), F32),
        ),
        in_specs=[pl.BlockSpec(memory_space=pltpu.SMEM), vmem, vmem],
        out_specs=(vmem,) * 2,
        scratch_shapes=[VMEM((4,) + own.shape[1:], BF16)],
        compiler_params=pltpu.CompilerParams(vmem_limit_bytes=4 * 2**20),
        name="choose",
    )(group, own, other)


def attended(query, recv, kv):
    rows = query.shape[0]
    few = rows // N_DP
    for d in range(N_DP):
        both = recv[2 * d].astype(F32) + recv[2 * d + 1].astype(F32)
        kv[d * few : (d + 1) * few, :] = both.astype(BF16)
    scores = lax.dot_general(
        query, kv[:, :HD], (((1,), (1,)), ((), ())), preferred_element_type=F32
    )
    allowed = lax.broadcasted_iota(jnp.int32, (rows, rows), 0) >= lax.broadcasted_iota(
        jnp.int32, (rows, rows), 1
    )
    expo = jnp.where(allowed, jnp.exp(scores * (1.0 / math.sqrt(HD))), 0.0)
    weights = (expo / jnp.sum(expo, axis=1, keepdims=True)).astype(BF16)
    return jnp.dot(weights, kv[:, HD:], preferred_element_type=F32).astype(BF16)


def attend_kernel(query, recv, wout, send, kv):
    active = lax.axis_index("pipe") == 0

    @pl.when(active)
    def _():
        result = attended(query[...], recv, kv)
        for j in range(N_DP):
            send[j] = result

    @pl.when(jnp.logical_not(active))
    def _():
        gram_parts(wout, lambda h: (send.at[h], 0))


def attend(query, recv, wout):
    rows = query.shape[0]
    vmem = pl.BlockSpec(memory_space=VMEM)
    return pl.pallas_call(
        attend_kernel,
        out_shape=jax.ShapeDtypeStruct((N_DP, rows, HD), BF16),
        in_specs=[vmem] * 3,
        out_specs=vmem,
        scratch_shapes=[VMEM((rows, 2 * HD), BF16)],
        compiler_params=pltpu.CompilerParams(vmem_limit_bytes=8 * 2**20),
        name="attend",
    )(query, recv, wout)


def attend_last_kernel(width, query, recv, before, gram0, gram1, picked, send, kv):
    rows = query.shape[0]
    result = attended(query[...], recv, kv)
    first_section = lax.axis_index("pipe") == 0
    mine = jnp.where(first_section, before[0], result)
    gram = jnp.where(first_section, gram1[...], gram0[...])
    high, low = two_parts(gram)
    image = jnp.dot(mine, high, preferred_element_type=F32) + jnp.dot(
        mine, low, preferred_element_type=F32
    )
    squares = jnp.sum(image * mine.astype(F32), axis=1, keepdims=True)
    spread = jnp.sqrt(jnp.maximum(squares / width, 0.0) + EPS_RMS)
    mean = jnp.sum(spread, axis=0, keepdims=True) / rows
    high, low = two_parts(mean * picked[0:1, :])
    row = lax.broadcasted_iota(jnp.int32, (STATS, HD), 0)
    lines = jnp.where(row == 0, high.astype(F32), jnp.where(row == 1, low.astype(F32), 0.0))
    lines = lines.astype(BF16)
    for j in range(N_DP):
        send[j, :rows] = result
        send[j, rows:] = lines


def attend_last(query, recv, before, gram0, gram1, picked, width):
    rows = query.shape[0]
    vmem = pl.BlockSpec(memory_space=VMEM)
    return pl.pallas_call(
        functools.partial(attend_last_kernel, float(width)),
        out_shape=jax.ShapeDtypeStruct((N_DP, rows + STATS, HD), BF16),
        in_specs=[vmem] * 6,
        out_specs=vmem,
        scratch_shapes=[VMEM((rows, 2 * HD), BF16)],
        compiler_params=pltpu.CompilerParams(vmem_limit_bytes=8 * 2**20),
        name="attend_last",
    )(query, recv, before, gram0, gram1, picked)


def out_kernel(rows, masks, last, *refs):
    if last:
        recv, saved, wout, parts = refs
    else:
        recv, wout, parts, *gram = refs
    heads = recv.shape[0]
    cols = parts.shape[2]
    tensor = lax.axis_index("tensor")
    active = lax.axis_index("pipe") == (1 if last else 0)
    if last:
        sums = jnp.zeros((1, HD), F32)
        for h in range(heads):
            sums = sums + (
                recv[h, rows : rows + 1, :].astype(F32)
                + recv[h, rows + 1 : rows + 2, :].astype(F32)
            )
        sums = jnp.concatenate([sums, jnp.zeros((1, cols - HD), F32)], axis=1)
        high, low = two_parts(sums)
        row = lax.broadcasted_iota(jnp.int32, (STATS, cols), 0)
        lines = jnp.where(
            row == 0, high.astype(F32), jnp.where(row == 1, low.astype(F32), 0.0)
        ).astype(BF16)
        for n in range(2):
            parts[n, rows:] = lines
    for parity in range(2):

        @pl.when(jnp.logical_and(active, (tensor + masks[0] + parity) % 2 == 0))
        def _():
            for place in (parity, parity + 2):
                total = None
                for h in range(0, heads, 2):
                    pair = jnp.concatenate([recv[h, :rows, :], recv[h + 1, :rows, :]], axis=1)
                    one = jnp.dot(
                        pair,
                        wout[h * HD : (h + 2) * HD, place * cols : (place + 1) * cols],
                        preferred_element_type=F32,
                    )
                    total = one if total is None else total + one
                n = lax.bitwise_xor(tensor, place) // 2
                parts[n, :rows] = total.astype(BF16)

    @pl.when(jnp.logical_not(active))
    def _():
        for n in range(2):
            parts[n, :rows] = saved[n] if last else jnp.zeros((rows, cols), BF16)
        if not last and gram:
            total = jnp.zeros((HD, HD), F32)
            for s in range(heads):
                total = total + (recv[s, :HD].astype(F32) + recv[s, HD : 2 * HD].astype(F32))
            gram[0][...] = total

    if not last and gram:

        @pl.when(active)
        def _():
            gram[0][...] = jnp.zeros((HD, HD), F32)


def project_out(recv, wout, rows, masks, saved=None):
    heads, deep, _ = recv.shape
    cols = wout.shape[1] // N_TENSOR
    last = saved is not None
    vmem = pl.BlockSpec(memory_space=VMEM)
    shapes = (jax.ShapeDtypeStruct((2, deep, cols), BF16),)
    if not last and masks[0] == 0:
        shapes += (jax.ShapeDtypeStruct((HD, HD), F32),)
    operands = (recv, saved, wout) if last else (recv, wout)
    return pl.pallas_call(
        functools.partial(out_kernel, rows, masks, last),
        out_shape=shapes,
        in_specs=[vmem] * len(operands),
        out_specs=(vmem,) * len(shapes),
        compiler_params=pltpu.CompilerParams(vmem_limit_bytes=6 * 2**20),
        cost_estimate=pl.CostEstimate(
            flops=4 * rows * heads * HD * cols, bytes_accessed=2**22, transcendentals=0
        ),
        name="project_out",
    )(*operands)


def pair_kernel(a, b, out0, out1):
    for n, out in enumerate((out0, out1)):
        out[...] = (a[n].astype(F32) + b[n].astype(F32)).astype(BF16)


def add_pair(a, b):
    vmem = pl.BlockSpec(memory_space=VMEM)
    return pl.pallas_call(
        pair_kernel,
        out_shape=(jax.ShapeDtypeStruct(a.shape[1:], BF16),) * 2,
        in_specs=[vmem] * 2,
        out_specs=(vmem,) * 2,
        compiler_params=pltpu.CompilerParams(vmem_limit_bytes=4 * 2**20),
        name="add_pair",
    )(a, b)


def last_pair_kernel(rows, a, b, out0, out1):
    for n, out in enumerate((out0, out1)):
        total = a[n].astype(F32) + b[n].astype(F32)
        out[:rows] = total[:rows].astype(BF16)
        high, low = two_parts(total[rows : rows + 1] + total[rows + 1 : rows + 2])
        row = lax.broadcasted_iota(jnp.int32, (STATS, out.shape[1]), 0)
        lines = jnp.where(row == 0, high.astype(F32), 0.0)
        out[rows:] = jnp.where(row == 1, low.astype(F32), lines).astype(BF16)


def add_last_pair(a, b, rows):
    vmem = pl.BlockSpec(memory_space=VMEM)
    return pl.pallas_call(
        functools.partial(last_pair_kernel, rows),
        out_shape=(jax.ShapeDtypeStruct(a.shape[1:], BF16),) * 2,
        in_specs=[vmem] * 2,
        out_specs=(vmem,) * 2,
        compiler_params=pltpu.CompilerParams(vmem_limit_bytes=4 * 2**20),
        name="add_last_pair",
    )(a, b)


def next_kernel(wide, here, there, fresh):
    fresh[...] = (
        wide[...].astype(F32) + (here[...].astype(F32) + there[...].astype(F32))
    ).astype(BF16)


def add_next(wide, here, there):
    vmem = pl.BlockSpec(memory_space=VMEM)
    return pl.pallas_call(
        next_kernel,
        out_shape=jax.ShapeDtypeStruct(wide.shape, BF16),
        in_specs=[vmem] * 3,
        out_specs=vmem,
        compiler_params=pltpu.CompilerParams(vmem_limit_bytes=4 * 2**20),
        name="add_next",
    )(wide, here, there)


def last_kernel(mine, state, here, there, out, importance):
    rows = mine.shape[0]
    total = here[...].astype(F32) + there[...].astype(F32)
    wide = jnp.where(lax.axis_index("pipe") == 0, mine[...], state[...]).astype(F32)
    out[...] = (wide + total[:rows]).astype(BF16)
    importance[...] = total[rows : rows + 1, :HD] + total[rows + 1 : rows + 2, :HD]


def add_last(mine, state, here, there):
    vmem = pl.BlockSpec(memory_space=VMEM)
    return pl.pallas_call(
        last_kernel,
        out_shape=(
            jax.ShapeDtypeStruct(mine.shape, BF16),
            jax.ShapeDtypeStruct((1, HD), F32),
        ),
        in_specs=[vmem] * 4,
        out_specs=(vmem, vmem),
        compiler_params=pltpu.CompilerParams(vmem_limit_bytes=4 * 2**20),
        name="add_last",
    )(mine, state, here, there)


def swap(block, *masks):
    route = [
        (p * N_TENSOR + t, p * N_TENSOR + (t ^ masks[min(p, len(masks) - 1)]))
        for p in range(2)
        for t in range(N_TENSOR)
    ]
    return lax.ppermute(block, ("pipe", "tensor"), route)


def to_next_section(block, mask):
    route = [(t, N_TENSOR + (t ^ mask)) for t in range(N_TENSOR)]
    return lax.ppermute(block, ("pipe", "tensor"), route)


def local(hidden_in, norm_gain, w_query, w_keyval, w_out, head_group):
    rows, cols = hidden_in.shape[0], hidden_in.shape[3]
    width = cols * N_TENSOR * N_DP
    wq, wout = w_query[0], w_out[0]
    wkv = w_keyval[0].reshape(wq.shape[0], -1)
    cosine, sine = map(jnp.asarray, rotary_tables(rows))

    runs = [
        [d * N_TENSOR + 2 * a + core for d in range(N_DP) for a in range(2)] for core in range(2)
    ]

    def to_heads(step, pieces, *weights):
        send = project(step, pieces, norm_gain, wkv, wq, *weights)
        recv = lax.all_to_all(send, "dp", 0, 0)
        query, kv, gram = combine(step, recv, cosine, sine, width)
        send, picked = choose(head_group, kv, swap(kv, 1))
        recv = lax.all_to_all(send, ("dp", "tensor"), 0, 0, axis_index_groups=runs)
        return query, recv, gram, picked

    mine = hidden_in.reshape(rows, cols)
    far = hand_on(swap(mine, 2, 1), ready(norm_gain, wq, wkv))
    pieces = (mine, swap(mine, 1), far, swap(far, 1))
    query, kv, _, _ = to_heads(0, pieces)
    att0 = attend(query, kv, wout)
    recv = lax.all_to_all(att0, "dp", 0, 0)
    (other0,) = project_out(recv, wout, rows, (1, 3))
    own0, gram0 = project_out(recv, wout, rows, (0, 2))
    here, away = add_pair(own0, swap(other0, 1))
    fresh = add_next(mine, here, swap(away, 2, 1))
    far = to_next_section(fresh, 2)
    near = to_next_section(fresh, 0)

    query, kv, gram1, picked = to_heads(1, (near, swap(near, 1), far, swap(far, 1)), wout)
    att1 = attend_last(query, kv, att0, gram0, gram1, picked, width)
    recv = lax.all_to_all(att1, "dp", 0, 0)
    (other1,) = project_out(recv, wout, rows, (1, 3), other0)
    (own1,) = project_out(recv, wout, rows, (0, 2), own0)
    here, away = add_last_pair(own1, swap(other1, 1), rows)
    out, importance = add_last(mine, near, here, swap(away, 2))
    return out.reshape(1, rows, 1, 1, cols), importance[:, :GROUPS]


def solution(mesh):
    in_specs = (
        P(None, "dp", "tensor", None),
        P("pipe", "dp"),
        P("pipe", "dp", "tensor"),
        P("pipe", "dp", "tensor", None),
        P("pipe", "tensor", "dp"),
        P(),
    )
    out_specs = (P("pipe", None, "dp", "tensor", None), P("pipe", None))
    return jax.shard_map(local, mesh=mesh, in_specs=in_specs, out_specs=out_specs, check_vma=False)
```

```python
import functools
import math

import jax
import jax.numpy as jnp
import numpy as np
from jax import lax
from jax.experimental import pallas as pl
from jax.experimental.pallas import tpu as pltpu
from jax.sharding import PartitionSpec as P

HD = 128
GROUPS = 8
N_TENSOR = 4
N_DP = 16
THETA = 500000.0
EPS_NORM = 1e-05
EPS_RMS = 1e-06
STATS = 16

BF16 = jnp.bfloat16
F32 = jnp.float32
VMEM = pltpu.VMEM


def rotary_tables(rows):
    positions = np.arange(rows, dtype=np.float64)[:, None]
    lanes = np.arange(HD)
    angle = positions * THETA ** (-2.0 * (lanes // 2) / HD)[None, :]
    sign = np.where(lanes % 2 == 0, -1.0, 1.0)[None, :]
    return np.cos(angle).astype(np.float32), (np.sin(angle) * sign).astype(np.float32)


def rotated(values, cosine, sine):
    lanes = lax.broadcasted_iota(jnp.int32, values.shape, 1)
    swapped = jnp.where(
        lanes % 2 == 0, pltpu.roll(values, HD - 1, 1), pltpu.roll(values, 1, 1)
    )
    return values * cosine + swapped * sine


def diagonal():
    return lax.broadcasted_iota(jnp.int32, (HD, HD), 0) == lax.broadcasted_iota(
        jnp.int32, (HD, HD), 1
    )


def two_parts(values):
    high = values.astype(BF16)
    return high, (values - high.astype(F32)).astype(BF16)


def ready_kernel(*refs):
    out = refs[-1]
    out[...] = jnp.zeros_like(out)


def ready(*arrays):
    vmem = pl.BlockSpec(memory_space=VMEM)
    return pl.pallas_call(
        ready_kernel,
        out_shape=jax.ShapeDtypeStruct((16, HD), BF16),
        in_specs=[vmem] * len(arrays),
        out_specs=vmem,
        compiler_params=pltpu.CompilerParams(vmem_limit_bytes=12 * 2**20),
        cost_estimate=pl.CostEstimate(flops=10**9, bytes_accessed=10**7, transcendentals=0),
        name="ready",
    )(*arrays)


def hand_on_kernel(block, tile, out):
    out[...] = block[...]


def hand_on(block, tile):
    vmem = pl.BlockSpec(memory_space=VMEM)
    return pl.pallas_call(
        hand_on_kernel,
        out_shape=jax.ShapeDtypeStruct(block.shape, BF16),
        in_specs=[vmem] * 2,
        out_specs=vmem,
        compiler_params=pltpu.CompilerParams(vmem_limit_bytes=2 * 2**20),
        name="hand_on",
    )(block, tile)


def gram_parts(wout, target):
    @pl.loop(0, wout.shape[0] // (2 * HD))
    def _(i):
        pair = wout[pl.ds(pl.multiple_of(i * 2 * HD, 2 * HD), 2 * HD), :]
        both = lax.dot_general(pair, pair, (((1,), (1,)), ((), ())), preferred_element_type=F32)
        for n in range(2):
            high, low = two_parts(both[n * HD : (n + 1) * HD, n * HD : (n + 1) * HD])
            ref, first = target(2 * i + n)
            ref[pl.ds(first, HD), :] = high
            ref[pl.ds(first + HD, HD), :] = low


def project_kernel(step, count, *refs):
    pieces, refs = refs[:count], refs[count:]
    gain, wkv, wq, *wout, send, scaled = refs
    rows, cols = pieces[0].shape[-2:]
    per = 4
    heads = N_DP
    pitch = rows + 64 + STATS
    tensor = lax.axis_index("tensor")
    if count == 4:
        by_mask = [ref[...] for ref in pieces]
    else:
        by_mask = [pieces[mask % 2][mask // 2] for mask in range(4)]

    def block(place):
        low = [jnp.where(tensor % 2 == place % 2, by_mask[n], by_mask[n + 1]) for n in (0, 2)]
        return jnp.where(tensor // 2 == place // 2, low[0], low[1])

    active = lax.axis_index("pipe") == step

    @pl.when(active)
    def _():
        total = jnp.zeros((rows, 1), F32)
        for place in range(N_TENSOR):
            at = slice(place * cols, (place + 1) * cols)
            wide = block(place).astype(F32)
            total = total + jnp.sum(wide * wide, axis=1, keepdims=True)
            scaled[:, at] = (wide * gain[:, at].astype(F32)).astype(BF16)
        eye = diagonal()
        row = lax.broadcasted_iota(jnp.int32, (STATS, HD), 0)
        lines = jnp.zeros((STATS, HD), F32)
        for b in range(rows // HD):
            line = jnp.sum(
                jnp.where(eye, total[b * HD : (b + 1) * HD], 0.0), axis=0, keepdims=True
            )
            high, low = two_parts(line)
            lines = jnp.where(row == 2 * b, high.astype(F32), lines)
            lines = jnp.where(row == 2 * b + 1, low.astype(F32), lines)
        lines = lines.astype(BF16)
        part = jnp.dot(scaled[...], wkv[...], preferred_element_type=F32).astype(BF16)
        for j in range(heads):
            first = j * pitch + rows
            for c in range(4):
                send[first + 16 * c : first + 16 * c + 16, :] = part[
                    16 * j : 16 * j + 16, c * HD : (c + 1) * HD
                ]
            send[first + 64 : first + 64 + STATS, :] = lines
        for i in range(heads // per):
            part = jnp.dot(
                scaled[...], wq[:, i * per * HD : (i + 1) * per * HD], preferred_element_type=F32
            ).astype(BF16)
            for j in range(per):
                first = (i * per + j) * pitch
                send[first : first + rows, :] = part[:, j * HD : (j + 1) * HD]

    @pl.when(jnp.logical_not(active))
    def _():
        if wout:
            gram_parts(wout[0], lambda h: (send, pl.multiple_of(h * pitch, 16)))
            for j in range(heads):
                first = j * pitch + rows
                send[first : first + 64 + STATS, :] = jnp.zeros((64 + STATS, HD), BF16)
        else:
            send[...] = jnp.zeros_like(send)


def project(step, pieces, gain, wkv, *weights):
    rows, cols = pieces[0].shape[-2:]
    wide = cols * N_TENSOR
    pitch = rows + 64 + STATS
    vmem = pl.BlockSpec(memory_space=VMEM)
    send = pl.pallas_call(
        functools.partial(project_kernel, step, len(pieces)),
        out_shape=jax.ShapeDtypeStruct((N_DP * pitch, HD), BF16),
        in_specs=[vmem] * (len(pieces) + 2 + len(weights)),
        out_specs=vmem,
        scratch_shapes=[VMEM((rows, wide), BF16)],
        compiler_params=pltpu.CompilerParams(vmem_limit_bytes=8 * 2**20),
        name="project",
    )(*pieces, gain, wkv, *weights)
    return send.reshape(N_DP, pitch, HD)


def combine_kernel(step, width, recv, cosine, sine, query, kv, *rest):
    *gram, scale = rest
    rows = cosine.shape[0]
    active = lax.axis_index("pipe") == step

    def total(first, size):
        at = slice(first, first + size)
        value = recv[0, at, :].astype(F32)
        for s in range(1, N_DP):
            value = value + recv[s, at, :].astype(F32)
        return value

    @pl.when(active)
    def _():
        raw = total(0, rows)
        tail = total(rows, 64 + STATS)
        eye = diagonal()
        for b in range(rows // HD):
            line = tail[64 + 2 * b : 65 + 2 * b, :] + tail[65 + 2 * b : 66 + 2 * b, :]
            column = jnp.sum(jnp.where(eye, line, 0.0), axis=1, keepdims=True)
            factor = lax.rsqrt(column / width + EPS_NORM)
            scale[b * HD : (b + 1) * HD, :] = jnp.broadcast_to(factor, (HD, HD))
        query[...] = rotated(raw * scale[...], cosine[...], sine[...]).astype(BF16)
        first = pl.multiple_of(lax.axis_index("dp") * 16, 16)
        here = scale[pl.ds(first, 16), :]
        cos_here = cosine[pl.ds(first, 16), :]
        sin_here = sine[pl.ds(first, 16), :]
        for g in range(2):
            keys = tail[32 * g : 32 * g + 16] * here
            vals = tail[32 * g + 16 : 32 * g + 32] * here
            kv[g, :, :HD] = rotated(keys, cos_here, sin_here).astype(BF16)
            kv[g, :, HD:] = vals.astype(BF16)
        for ref in gram:
            ref[...] = jnp.zeros_like(ref)

    @pl.when(jnp.logical_not(active))
    def _():
        for ref in gram:
            ref[...] = total(0, HD) + total(HD, HD)
        query[...] = jnp.zeros_like(query)
        kv[...] = jnp.zeros_like(kv)


def combine(step, recv, cosine, sine, width):
    rows = cosine.shape[0]
    vmem = pl.BlockSpec(memory_space=VMEM)
    shapes = (
        jax.ShapeDtypeStruct((rows, HD), BF16),
        jax.ShapeDtypeStruct((2, 16, 2 * HD), BF16),
        jax.ShapeDtypeStruct((HD, HD), F32),
    )[: 2 + step]
    return pl.pallas_call(
        functools.partial(combine_kernel, step, float(width)),
        out_shape=shapes,
        in_specs=[vmem] * 3,
        out_specs=(vmem,) * len(shapes),
        scratch_shapes=[VMEM((rows, HD), F32)],
        compiler_params=pltpu.CompilerParams(vmem_limit_bytes=8 * 2**20),
        name="combine",
    )(recv, cosine, sine)


def choose_kernel(group, own, other, send, *rest):
    *picked, four = rest
    tensor, data = lax.axis_index("tensor"), lax.axis_index("dp")
    chip, core = tensor // 2, tensor % 2
    for n in range(2):
        four[2 * core + n] = own[n]
        four[2 * (1 - core) + n] = other[n]
    for d in range(N_DP):
        for a in range(2):
            wanted = group[(2 * a + core) * N_DP + d]
            block = four[wanted % 4]
            send[2 * d + a] = jnp.where(wanted // 4 == chip, block, jnp.zeros_like(block))
    for ref in picked:
        lane = lax.broadcasted_iota(jnp.int32, ref.shape, 1)
        ref[...] = jnp.where(lane == group[tensor * N_DP + data], 1.0, 0.0).astype(F32)


def choose(step, group, own, other):
    vmem = pl.BlockSpec(memory_space=VMEM)
    shapes = (
        jax.ShapeDtypeStruct((2 * N_DP,) + own.shape[1:], BF16),
        jax.ShapeDtypeStruct((8, HD), F32),
    )[: 1 + step]
    return pl.pallas_call(
        choose_kernel,
        out_shape=shapes,
        in_specs=[pl.BlockSpec(memory_space=pltpu.SMEM), vmem, vmem],
        out_specs=(vmem,) * len(shapes),
        scratch_shapes=[VMEM((4,) + own.shape[1:], BF16)],
        compiler_params=pltpu.CompilerParams(vmem_limit_bytes=4 * 2**20),
        name="choose",
    )(group, own, other)


def attended(query, recv, kv):
    rows = query.shape[0]
    few = rows // N_DP
    for d in range(N_DP):
        both = recv[2 * d].astype(F32) + recv[2 * d + 1].astype(F32)
        kv[d * few : (d + 1) * few, :] = both.astype(BF16)
    scores = lax.dot_general(
        query, kv[:, :HD], (((1,), (1,)), ((), ())), preferred_element_type=F32
    )
    allowed = lax.broadcasted_iota(jnp.int32, (rows, rows), 0) >= lax.broadcasted_iota(
        jnp.int32, (rows, rows), 1
    )
    expo = jnp.where(allowed, jnp.exp(scores * (1.0 / math.sqrt(HD))), 0.0)
    weights = (expo / jnp.sum(expo, axis=1, keepdims=True)).astype(BF16)
    return jnp.dot(weights, kv[:, HD:], preferred_element_type=F32).astype(BF16)


def attend_kernel(query, recv, wout, send, kv):
    active = lax.axis_index("pipe") == 0

    @pl.when(active)
    def _():
        result = attended(query[...], recv, kv)
        for j in range(N_DP):
            send[j] = result

    @pl.when(jnp.logical_not(active))
    def _():
        gram_parts(wout, lambda h: (send.at[h], 0))


def attend(query, recv, wout):
    rows = query.shape[0]
    vmem = pl.BlockSpec(memory_space=VMEM)
    return pl.pallas_call(
        attend_kernel,
        out_shape=jax.ShapeDtypeStruct((N_DP, rows, HD), BF16),
        in_specs=[vmem] * 3,
        out_specs=vmem,
        scratch_shapes=[VMEM((rows, 2 * HD), BF16)],
        compiler_params=pltpu.CompilerParams(vmem_limit_bytes=8 * 2**20),
        name="attend",
    )(query, recv, wout)


def attend_last_kernel(width, query, recv, before, gram0, gram1, picked, send, kv):
    rows = query.shape[0]
    result = attended(query[...], recv, kv)
    first_section = lax.axis_index("pipe") == 0
    mine = jnp.where(first_section, before[0], result)
    gram = jnp.where(first_section, gram1[...], gram0[...])
    high, low = two_parts(gram)
    image = jnp.dot(mine, high, preferred_element_type=F32) + jnp.dot(
        mine, low, preferred_element_type=F32
    )
    squares = jnp.sum(image * mine.astype(F32), axis=1, keepdims=True)
    spread = jnp.sqrt(jnp.maximum(squares / width, 0.0) + EPS_RMS)
    mean = jnp.sum(spread, axis=0, keepdims=True) / rows
    high, low = two_parts(mean * picked[0:1, :])
    row = lax.broadcasted_iota(jnp.int32, (STATS, HD), 0)
    lines = jnp.where(row == 0, high.astype(F32), jnp.where(row == 1, low.astype(F32), 0.0))
    lines = lines.astype(BF16)
    for j in range(N_DP):
        send[j, :rows] = result
        send[j, rows:] = lines


def attend_last(query, recv, before, gram0, gram1, picked, width):
    rows = query.shape[0]
    vmem = pl.BlockSpec(memory_space=VMEM)
    return pl.pallas_call(
        functools.partial(attend_last_kernel, float(width)),
        out_shape=jax.ShapeDtypeStruct((N_DP, rows + STATS, HD), BF16),
        in_specs=[vmem] * 6,
        out_specs=vmem,
        scratch_shapes=[VMEM((rows, 2 * HD), BF16)],
        compiler_params=pltpu.CompilerParams(vmem_limit_bytes=8 * 2**20),
        name="attend_last",
    )(query, recv, before, gram0, gram1, picked)


def out_kernel(rows, masks, last, *refs):
    if last:
        recv, saved, wout, parts = refs
    else:
        recv, wout, parts, *gram = refs
    heads = recv.shape[0]
    cols = parts.shape[2]
    tensor = lax.axis_index("tensor")
    active = lax.axis_index("pipe") == (1 if last else 0)
    if last:
        sums = jnp.zeros((1, HD), F32)
        for h in range(heads):
            sums = sums + (
                recv[h, rows : rows + 1, :].astype(F32)
                + recv[h, rows + 1 : rows + 2, :].astype(F32)
            )
        sums = jnp.concatenate([sums, jnp.zeros((1, cols - HD), F32)], axis=1)
        high, low = two_parts(sums)
        row = lax.broadcasted_iota(jnp.int32, (STATS, cols), 0)
        lines = jnp.where(
            row == 0, high.astype(F32), jnp.where(row == 1, low.astype(F32), 0.0)
        ).astype(BF16)
        for n in range(2):
            parts[n, rows:] = lines
    for parity in range(2):

        @pl.when(jnp.logical_and(active, (tensor + masks[0] + parity) % 2 == 0))
        def _():
            for place in (parity, parity + 2):
                total = None
                for h in range(0, heads, 2):
                    pair = jnp.concatenate([recv[h, :rows, :], recv[h + 1, :rows, :]], axis=1)
                    one = jnp.dot(
                        pair,
                        wout[h * HD : (h + 2) * HD, place * cols : (place + 1) * cols],
                        preferred_element_type=F32,
                    )
                    total = one if total is None else total + one
                n = lax.bitwise_xor(tensor, place) // 2
                parts[n, :rows] = total.astype(BF16)

    @pl.when(jnp.logical_not(active))
    def _():
        for n in range(2):
            parts[n, :rows] = saved[n] if last else jnp.zeros((rows, cols), BF16)
        if not last and gram:
            total = jnp.zeros((HD, HD), F32)
            for s in range(heads):
                total = total + (recv[s, :HD].astype(F32) + recv[s, HD : 2 * HD].astype(F32))
            gram[0][...] = total

    if not last and gram:

        @pl.when(active)
        def _():
            gram[0][...] = jnp.zeros((HD, HD), F32)


def project_out(recv, wout, rows, masks, saved=None):
    heads, deep, _ = recv.shape
    cols = wout.shape[1] // N_TENSOR
    last = saved is not None
    vmem = pl.BlockSpec(memory_space=VMEM)
    shapes = (jax.ShapeDtypeStruct((2, deep, cols), BF16),)
    if not last and masks[0] == 0:
        shapes += (jax.ShapeDtypeStruct((HD, HD), F32),)
    operands = (recv, saved, wout) if last else (recv, wout)
    return pl.pallas_call(
        functools.partial(out_kernel, rows, masks, last),
        out_shape=shapes,
        in_specs=[vmem] * len(operands),
        out_specs=(vmem,) * len(shapes),
        compiler_params=pltpu.CompilerParams(vmem_limit_bytes=6 * 2**20),
        cost_estimate=pl.CostEstimate(
            flops=4 * rows * heads * HD * cols, bytes_accessed=2**22, transcendentals=0
        ),
        name="project_out",
    )(*operands)


def pair_kernel(a, b, out0, out1):
    for n, out in enumerate((out0, out1)):
        out[...] = (a[n].astype(F32) + b[n].astype(F32)).astype(BF16)


def add_pair(a, b):
    vmem = pl.BlockSpec(memory_space=VMEM)
    return pl.pallas_call(
        pair_kernel,
        out_shape=(jax.ShapeDtypeStruct(a.shape[1:], BF16),) * 2,
        in_specs=[vmem] * 2,
        out_specs=(vmem,) * 2,
        compiler_params=pltpu.CompilerParams(vmem_limit_bytes=4 * 2**20),
        name="add_pair",
    )(a, b)


def last_pair_kernel(rows, a, b, out0, out1):
    for n, out in enumerate((out0, out1)):
        total = a[n].astype(F32) + b[n].astype(F32)
        out[:rows] = total[:rows].astype(BF16)
        high, low = two_parts(total[rows : rows + 1] + total[rows + 1 : rows + 2])
        row = lax.broadcasted_iota(jnp.int32, (STATS, out.shape[1]), 0)
        lines = jnp.where(row == 0, high.astype(F32), 0.0)
        out[rows:] = jnp.where(row == 1, low.astype(F32), lines).astype(BF16)


def add_last_pair(a, b, rows):
    vmem = pl.BlockSpec(memory_space=VMEM)
    return pl.pallas_call(
        functools.partial(last_pair_kernel, rows),
        out_shape=(jax.ShapeDtypeStruct(a.shape[1:], BF16),) * 2,
        in_specs=[vmem] * 2,
        out_specs=(vmem,) * 2,
        compiler_params=pltpu.CompilerParams(vmem_limit_bytes=4 * 2**20),
        name="add_last_pair",
    )(a, b)


def next_kernel(wide, here, there, fresh):
    fresh[...] = (
        wide[...].astype(F32) + (here[...].astype(F32) + there[...].astype(F32))
    ).astype(BF16)


def add_next(wide, here, there):
    vmem = pl.BlockSpec(memory_space=VMEM)
    return pl.pallas_call(
        next_kernel,
        out_shape=jax.ShapeDtypeStruct(wide.shape, BF16),
        in_specs=[vmem] * 3,
        out_specs=vmem,
        compiler_params=pltpu.CompilerParams(vmem_limit_bytes=4 * 2**20),
        name="add_next",
    )(wide, here, there)


def last_kernel(mine, state, here, there, out, importance):
    rows = mine.shape[0]
    total = here[...].astype(F32) + there[...].astype(F32)
    wide = jnp.where(lax.axis_index("pipe") == 0, mine[...], state[...]).astype(F32)
    out[...] = (wide + total[:rows]).astype(BF16)
    importance[...] = total[rows : rows + 1, :HD] + total[rows + 1 : rows + 2, :HD]


def add_last(mine, state, here, there):
    vmem = pl.BlockSpec(memory_space=VMEM)
    return pl.pallas_call(
        last_kernel,
        out_shape=(
            jax.ShapeDtypeStruct(mine.shape, BF16),
            jax.ShapeDtypeStruct((1, HD), F32),
        ),
        in_specs=[vmem] * 4,
        out_specs=(vmem, vmem),
        compiler_params=pltpu.CompilerParams(vmem_limit_bytes=4 * 2**20),
        name="add_last",
    )(mine, state, here, there)


def swap(block, *masks):
    route = [
        (p * N_TENSOR + t, p * N_TENSOR + (t ^ masks[min(p, len(masks) - 1)]))
        for p in range(2)
        for t in range(N_TENSOR)
    ]
    return lax.ppermute(block, ("pipe", "tensor"), route)


def to_next_section(block, mask):
    route = [(t, N_TENSOR + (t ^ mask)) for t in range(N_TENSOR)]
    return lax.ppermute(block, ("pipe", "tensor"), route)


def local(hidden_in, norm_gain, w_query, w_keyval, w_out, head_group):
    rows, cols = hidden_in.shape[0], hidden_in.shape[3]
    width = cols * N_TENSOR * N_DP
    wq, wout = w_query[0], w_out[0]
    wkv = w_keyval[0].reshape(wq.shape[0], -1)
    cosine, sine = map(jnp.asarray, rotary_tables(rows))

    runs = [
        [d * N_TENSOR + 2 * a + core for d in range(N_DP) for a in range(2)] for core in range(2)
    ]

    def to_heads(step, pieces, *weights):
        send = project(step, pieces, norm_gain, wkv, wq, *weights)
        recv = lax.all_to_all(send, "dp", 0, 0)
        query, kv, *gram = combine(step, recv, cosine, sine, width)
        send, *picked = choose(step, head_group, kv, swap(kv, 1))
        recv = lax.all_to_all(send, ("dp", "tensor"), 0, 0, axis_index_groups=runs)
        return query, recv, *gram, *picked

    mine = hidden_in.reshape(rows, cols)
    tile = ready(mine, norm_gain, wkv, cosine, sine, head_group)
    far = hand_on(swap(mine, 2, 1), tile)
    pieces = (mine, swap(mine, 1), far, swap(far, 1))
    query, kv = to_heads(0, pieces)
    att0 = attend(query, kv, wout)
    recv = lax.all_to_all(att0, "dp", 0, 0)
    (other0,) = project_out(recv, wout, rows, (1, 3))
    own0, gram0 = project_out(recv, wout, rows, (0, 2))
    here, away = add_pair(own0, swap(other0, 1))
    fresh = add_next(mine, here, swap(away, 2, 1))
    far = to_next_section(fresh, 2)
    near = to_next_section(fresh, 0)

    query, kv, gram1, picked = to_heads(1, (near, swap(near, 1), far, swap(far, 1)), wout)
    att1 = attend_last(query, kv, att0, gram0, gram1, picked, width)
    recv = lax.all_to_all(att1, "dp", 0, 0)
    (other1,) = project_out(recv, wout, rows, (1, 3), other0)
    (own1,) = project_out(recv, wout, rows, (0, 2), own0)
    here, away = add_last_pair(own1, swap(other1, 1), rows)
    out, importance = add_last(mine, near, here, swap(away, 2))
    return out.reshape(1, rows, 1, 1, cols), importance[:, :GROUPS]


def solution(mesh):
    in_specs = (
        P(None, "dp", "tensor", None),
        P("pipe", "dp"),
        P("pipe", "dp", "tensor"),
        P("pipe", "dp", "tensor", None),
        P("pipe", "tensor", "dp"),
        P(),
    )
    out_specs = (P("pipe", None, "dp", "tensor", None), P("pipe", None))
    return jax.shard_map(local, mesh=mesh, in_specs=in_specs, out_specs=out_specs, check_vma=False)
```

```python
import functools
import math

import jax
import jax.numpy as jnp
import numpy as np
from jax import lax
from jax.experimental import pallas as pl
from jax.experimental.pallas import tpu as pltpu
from jax.sharding import PartitionSpec as P

HD = 128
GROUPS = 8
N_TENSOR = 4
N_DP = 16
THETA = 500000.0
EPS_NORM = 1e-05
EPS_RMS = 1e-06
STATS = 16

BF16 = jnp.bfloat16
F32 = jnp.float32
VMEM = pltpu.VMEM


def rotary_tables(rows):
    positions = np.arange(rows, dtype=np.float64)[:, None]
    lanes = np.arange(HD)
    angle = positions * THETA ** (-2.0 * (lanes // 2) / HD)[None, :]
    sign = np.where(lanes % 2 == 0, -1.0, 1.0)[None, :]
    return np.cos(angle).astype(np.float32), (np.sin(angle) * sign).astype(np.float32)


def rotated(values, cosine, sine):
    lanes = lax.broadcasted_iota(jnp.int32, values.shape, 1)
    swapped = jnp.where(
        lanes % 2 == 0, pltpu.roll(values, HD - 1, 1), pltpu.roll(values, 1, 1)
    )
    return values * cosine + swapped * sine


def diagonal():
    return lax.broadcasted_iota(jnp.int32, (HD, HD), 0) == lax.broadcasted_iota(
        jnp.int32, (HD, HD), 1
    )


def two_parts(values):
    high = values.astype(BF16)
    return high, (values - high.astype(F32)).astype(BF16)


def ready_kernel(*refs):
    out = refs[-1]
    out[...] = jnp.zeros_like(out)


def ready(*arrays):
    vmem = pl.BlockSpec(memory_space=VMEM)
    return pl.pallas_call(
        ready_kernel,
        out_shape=jax.ShapeDtypeStruct((16, HD), BF16),
        in_specs=[vmem] * len(arrays),
        out_specs=vmem,
        compiler_params=pltpu.CompilerParams(vmem_limit_bytes=12 * 2**20),
        cost_estimate=pl.CostEstimate(flops=10**9, bytes_accessed=10**7, transcendentals=0),
        name="ready",
    )(*arrays)


def hand_on_kernel(block, tile, out):
    out[...] = block[...]


def hand_on(block, tile):
    vmem = pl.BlockSpec(memory_space=VMEM)
    return pl.pallas_call(
        hand_on_kernel,
        out_shape=jax.ShapeDtypeStruct(block.shape, BF16),
        in_specs=[vmem] * 2,
        out_specs=vmem,
        compiler_params=pltpu.CompilerParams(vmem_limit_bytes=2 * 2**20),
        name="hand_on",
    )(block, tile)


def gram_parts(wout, target):
    @pl.loop(0, wout.shape[0] // (2 * HD))
    def _(i):
        pair = wout[pl.ds(pl.multiple_of(i * 2 * HD, 2 * HD), 2 * HD), :]
        both = lax.dot_general(pair, pair, (((1,), (1,)), ((), ())), preferred_element_type=F32)
        for n in range(2):
            high, low = two_parts(both[n * HD : (n + 1) * HD, n * HD : (n + 1) * HD])
            ref, first = target(2 * i + n)
            ref[pl.ds(first, HD), :] = high
            ref[pl.ds(first + HD, HD), :] = low


def project_kernel(step, count, *refs):
    pieces, refs = refs[:count], refs[count:]
    gain, wkv, wq, *wout, send, scaled = refs
    rows, cols = pieces[0].shape[-2:]
    per = 4
    heads = N_DP
    pitch = rows + 64 + STATS
    tensor = lax.axis_index("tensor")
    if count == 4:
        by_mask = [ref[...] for ref in pieces]
    else:
        by_mask = [pieces[mask % 2][mask // 2] for mask in range(4)]

    def block(place):
        low = [jnp.where(tensor % 2 == place % 2, by_mask[n], by_mask[n + 1]) for n in (0, 2)]
        return jnp.where(tensor // 2 == place // 2, low[0], low[1])

    active = lax.axis_index("pipe") == step

    @pl.when(active)
    def _():
        total = jnp.zeros((rows, 1), F32)
        for place in range(N_TENSOR):
            at = slice(place * cols, (place + 1) * cols)
            wide = block(place).astype(F32)
            total = total + jnp.sum(wide * wide, axis=1, keepdims=True)
            scaled[:, at] = (wide * gain[:, at].astype(F32)).astype(BF16)
        eye = diagonal()
        row = lax.broadcasted_iota(jnp.int32, (STATS, HD), 0)
        lines = jnp.zeros((STATS, HD), F32)
        for b in range(rows // HD):
            line = jnp.sum(
                jnp.where(eye, total[b * HD : (b + 1) * HD], 0.0), axis=0, keepdims=True
            )
            high, low = two_parts(line)
            lines = jnp.where(row == 2 * b, high.astype(F32), lines)
            lines = jnp.where(row == 2 * b + 1, low.astype(F32), lines)
        lines = lines.astype(BF16)
        part = jnp.dot(scaled[...], wkv[...], preferred_element_type=F32).astype(BF16)
        for j in range(heads):
            first = j * pitch + rows
            for c in range(4):
                send[first + 16 * c : first + 16 * c + 16, :] = part[
                    16 * j : 16 * j + 16, c * HD : (c + 1) * HD
                ]
            send[first + 64 : first + 64 + STATS, :] = lines
        for i in range(heads // per):
            part = jnp.dot(
                scaled[...], wq[:, i * per * HD : (i + 1) * per * HD], preferred_element_type=F32
            ).astype(BF16)
            for j in range(per):
                first = (i * per + j) * pitch
                send[first : first + rows, :] = part[:, j * HD : (j + 1) * HD]

    @pl.when(jnp.logical_not(active))
    def _():
        if wout:
            gram_parts(wout[0], lambda h: (send, pl.multiple_of(h * pitch, 16)))
            for j in range(heads):
                first = j * pitch + rows
                send[first : first + 64 + STATS, :] = jnp.zeros((64 + STATS, HD), BF16)
        else:
            send[...] = jnp.zeros_like(send)


def project(step, pieces, gain, wkv, *weights):
    rows, cols = pieces[0].shape[-2:]
    wide = cols * N_TENSOR
    pitch = rows + 64 + STATS
    vmem = pl.BlockSpec(memory_space=VMEM)
    send = pl.pallas_call(
        functools.partial(project_kernel, step, len(pieces)),
        out_shape=jax.ShapeDtypeStruct((N_DP * pitch, HD), BF16),
        in_specs=[vmem] * (len(pieces) + 2 + len(weights)),
        out_specs=vmem,
        scratch_shapes=[VMEM((rows, wide), BF16)],
        compiler_params=pltpu.CompilerParams(vmem_limit_bytes=8 * 2**20),
        name="project",
    )(*pieces, gain, wkv, *weights)
    return send.reshape(N_DP, pitch, HD)


def combine_kernel(step, width, recv, cosine, sine, query, kv, *rest):
    *gram, scale = rest
    rows = cosine.shape[0]
    active = lax.axis_index("pipe") == step

    def total(first, size):
        at = slice(first, first + size)
        value = recv[0, at, :].astype(F32)
        for s in range(1, N_DP):
            value = value + recv[s, at, :].astype(F32)
        return value

    @pl.when(active)
    def _():
        raw = total(0, rows)
        tail = total(rows, 64 + STATS)
        eye = diagonal()
        for b in range(rows // HD):
            line = tail[64 + 2 * b : 65 + 2 * b, :] + tail[65 + 2 * b : 66 + 2 * b, :]
            column = jnp.sum(jnp.where(eye, line, 0.0), axis=1, keepdims=True)
            factor = lax.rsqrt(column / width + EPS_NORM)
            scale[b * HD : (b + 1) * HD, :] = jnp.broadcast_to(factor, (HD, HD))
        query[...] = rotated(raw * scale[...], cosine[...], sine[...]).astype(BF16)
        first = pl.multiple_of(lax.axis_index("dp") * 16, 16)
        here = scale[pl.ds(first, 16), :]
        cos_here = cosine[pl.ds(first, 16), :]
        sin_here = sine[pl.ds(first, 16), :]
        for g in range(2):
            keys = tail[32 * g : 32 * g + 16] * here
            vals = tail[32 * g + 16 : 32 * g + 32] * here
            kv[g, :, :HD] = rotated(keys, cos_here, sin_here).astype(BF16)
            kv[g, :, HD:] = vals.astype(BF16)
        for ref in gram:
            ref[...] = jnp.zeros_like(ref)

    @pl.when(jnp.logical_not(active))
    def _():
        for ref in gram:
            ref[...] = total(0, HD) + total(HD, HD)
        query[...] = jnp.zeros_like(query)
        kv[...] = jnp.zeros_like(kv)


def combine(step, recv, cosine, sine, width):
    rows = cosine.shape[0]
    vmem = pl.BlockSpec(memory_space=VMEM)
    shapes = (
        jax.ShapeDtypeStruct((rows, HD), BF16),
        jax.ShapeDtypeStruct((2, 16, 2 * HD), BF16),
        jax.ShapeDtypeStruct((HD, HD), F32),
    )[: 2 + step]
    return pl.pallas_call(
        functools.partial(combine_kernel, step, float(width)),
        out_shape=shapes,
        in_specs=[vmem] * 3,
        out_specs=(vmem,) * len(shapes),
        scratch_shapes=[VMEM((rows, HD), F32)],
        compiler_params=pltpu.CompilerParams(vmem_limit_bytes=8 * 2**20),
        name="combine",
    )(recv, cosine, sine)


def plan_kernel(group, choice, picked):
    tensor, data = lax.axis_index("tensor"), lax.axis_index("dp")
    chip, core = tensor // 2, tensor % 2
    row = lax.broadcasted_iota(jnp.int32, (16, 64), 0)
    col = lax.broadcasted_iota(jnp.int32, (16, 64), 1)
    for d in range(N_DP):
        for a in range(2):
            wanted = group[(2 * a + core) * N_DP + d]
            place = jnp.where(wanted % 4 // 2 == core, 0, 2) + wanted % 2
            place = jnp.where(wanted // 4 == chip, place, 4)
            first = (2 * d + a) * 16
            hit = col == place * 16 + row
            choice[first : first + 16, :] = jnp.where(hit, 1.0, 0.0).astype(BF16)
    lane = lax.broadcasted_iota(jnp.int32, picked.shape, 1)
    picked[...] = jnp.where(lane == group[tensor * N_DP + data], 1.0, 0.0).astype(F32)


def plan(group):
    vmem = pl.BlockSpec(memory_space=VMEM)
    return pl.pallas_call(
        plan_kernel,
        out_shape=(
            jax.ShapeDtypeStruct((2 * N_DP * 16, 64), BF16),
            jax.ShapeDtypeStruct((8, HD), F32),
        ),
        in_specs=[pl.BlockSpec(memory_space=pltpu.SMEM)],
        out_specs=(vmem,) * 2,
        compiler_params=pltpu.CompilerParams(vmem_limit_bytes=2 * 2**20),
        name="plan",
    )(group)


def choose_kernel(choice, own, other, send):
    four = jnp.concatenate([own[0], own[1], other[0], other[1]], axis=0)
    send[...] = jnp.dot(choice[...], four, preferred_element_type=F32).astype(BF16)


def choose(choice, own, other):
    vmem = pl.BlockSpec(memory_space=VMEM)
    send = pl.pallas_call(
        choose_kernel,
        out_shape=jax.ShapeDtypeStruct((choice.shape[0], own.shape[2]), BF16),
        in_specs=[vmem] * 3,
        out_specs=vmem,
        compiler_params=pltpu.CompilerParams(vmem_limit_bytes=4 * 2**20),
        name="choose",
    )(choice, own, other)
    return send.reshape((2 * N_DP,) + own.shape[1:])


def attended(query, recv, kv):
    rows = query.shape[0]
    few = rows // N_DP
    for d in range(N_DP):
        both = recv[2 * d].astype(F32) + recv[2 * d + 1].astype(F32)
        kv[d * few : (d + 1) * few, :] = both.astype(BF16)
    scores = lax.dot_general(
        query, kv[:, :HD], (((1,), (1,)), ((), ())), preferred_element_type=F32
    )
    allowed = lax.broadcasted_iota(jnp.int32, (rows, rows), 0) >= lax.broadcasted_iota(
        jnp.int32, (rows, rows), 1
    )
    expo = jnp.where(allowed, jnp.exp(scores * (1.0 / math.sqrt(HD))), 0.0)
    weights = (expo / jnp.sum(expo, axis=1, keepdims=True)).astype(BF16)
    return jnp.dot(weights, kv[:, HD:], preferred_element_type=F32).astype(BF16)


def attend_kernel(query, recv, wout, send, kv):
    active = lax.axis_index("pipe") == 0

    @pl.when(active)
    def _():
        result = attended(query[...], recv, kv)
        for j in range(N_DP):
            send[j] = result

    @pl.when(jnp.logical_not(active))
    def _():
        gram_parts(wout, lambda h: (send.at[h], 0))


def attend(query, recv, wout):
    rows = query.shape[0]
    vmem = pl.BlockSpec(memory_space=VMEM)
    return pl.pallas_call(
        attend_kernel,
        out_shape=jax.ShapeDtypeStruct((N_DP, rows, HD), BF16),
        in_specs=[vmem] * 3,
        out_specs=vmem,
        scratch_shapes=[VMEM((rows, 2 * HD), BF16)],
        compiler_params=pltpu.CompilerParams(vmem_limit_bytes=8 * 2**20),
        name="attend",
    )(query, recv, wout)


def attend_last_kernel(width, query, recv, before, gram0, gram1, picked, send, kv):
    rows = query.shape[0]
    result = attended(query[...], recv, kv)
    first_section = lax.axis_index("pipe") == 0
    mine = jnp.where(first_section, before[0], result)
    gram = jnp.where(first_section, gram1[...], gram0[...])
    high, low = two_parts(gram)
    image = jnp.dot(mine, high, preferred_element_type=F32) + jnp.dot(
        mine, low, preferred_element_type=F32
    )
    squares = jnp.sum(image * mine.astype(F32), axis=1, keepdims=True)
    spread = jnp.sqrt(jnp.maximum(squares / width, 0.0) + EPS_RMS)
    mean = jnp.sum(spread, axis=0, keepdims=True) / rows
    high, low = two_parts(mean * picked[0:1, :])
    row = lax.broadcasted_iota(jnp.int32, (STATS, HD), 0)
    lines = jnp.where(row == 0, high.astype(F32), jnp.where(row == 1, low.astype(F32), 0.0))
    lines = lines.astype(BF16)
    for j in range(N_DP):
        send[j, :rows] = result
        send[j, rows:] = lines


def attend_last(query, recv, before, gram0, gram1, picked, width):
    rows = query.shape[0]
    vmem = pl.BlockSpec(memory_space=VMEM)
    return pl.pallas_call(
        functools.partial(attend_last_kernel, float(width)),
        out_shape=jax.ShapeDtypeStruct((N_DP, rows + STATS, HD), BF16),
        in_specs=[vmem] * 6,
        out_specs=vmem,
        scratch_shapes=[VMEM((rows, 2 * HD), BF16)],
        compiler_params=pltpu.CompilerParams(vmem_limit_bytes=8 * 2**20),
        name="attend_last",
    )(query, recv, before, gram0, gram1, picked)


def out_kernel(rows, masks, last, *refs):
    if last:
        recv, saved, wout, parts = refs
    else:
        recv, wout, parts, *gram = refs
    heads = recv.shape[0]
    cols = parts.shape[2]
    tensor = lax.axis_index("tensor")
    active = lax.axis_index("pipe") == (1 if last else 0)
    if last:
        sums = jnp.zeros((1, HD), F32)
        for h in range(heads):
            sums = sums + (
                recv[h, rows : rows + 1, :].astype(F32)
                + recv[h, rows + 1 : rows + 2, :].astype(F32)
            )
        sums = jnp.concatenate([sums, jnp.zeros((1, cols - HD), F32)], axis=1)
        high, low = two_parts(sums)
        row = lax.broadcasted_iota(jnp.int32, (STATS, cols), 0)
        lines = jnp.where(
            row == 0, high.astype(F32), jnp.where(row == 1, low.astype(F32), 0.0)
        ).astype(BF16)
        for n in range(2):
            parts[n, rows:] = lines
    for parity in range(2):

        @pl.when(jnp.logical_and(active, (tensor + masks[0] + parity) % 2 == 0))
        def _():
            for place in (parity, parity + 2):
                total = None
                for h in range(0, heads, 2):
                    pair = jnp.concatenate([recv[h, :rows, :], recv[h + 1, :rows, :]], axis=1)
                    one = jnp.dot(
                        pair,
                        wout[h * HD : (h + 2) * HD, place * cols : (place + 1) * cols],
                        preferred_element_type=F32,
                    )
                    total = one if total is None else total + one
                n = lax.bitwise_xor(tensor, place) // 2
                parts[n, :rows] = total.astype(BF16)

    @pl.when(jnp.logical_not(active))
    def _():
        for n in range(2):
            parts[n, :rows] = saved[n] if last else jnp.zeros((rows, cols), BF16)
        if not last and gram:
            total = jnp.zeros((HD, HD), F32)
            for s in range(heads):
                total = total + (recv[s, :HD].astype(F32) + recv[s, HD : 2 * HD].astype(F32))
            gram[0][...] = total

    if not last and gram:

        @pl.when(active)
        def _():
            gram[0][...] = jnp.zeros((HD, HD), F32)


def project_out(recv, wout, rows, masks, saved=None):
    heads, deep, _ = recv.shape
    cols = wout.shape[1] // N_TENSOR
    last = saved is not None
    vmem = pl.BlockSpec(memory_space=VMEM)
    shapes = (jax.ShapeDtypeStruct((2, deep, cols), BF16),)
    if not last and masks[0] == 0:
        shapes += (jax.ShapeDtypeStruct((HD, HD), F32),)
    operands = (recv, saved, wout) if last else (recv, wout)
    return pl.pallas_call(
        functools.partial(out_kernel, rows, masks, last),
        out_shape=shapes,
        in_specs=[vmem] * len(operands),
        out_specs=(vmem,) * len(shapes),
        compiler_params=pltpu.CompilerParams(vmem_limit_bytes=6 * 2**20),
        cost_estimate=pl.CostEstimate(
            flops=4 * rows * heads * HD * cols, bytes_accessed=2**22, transcendentals=0
        ),
        name="project_out",
    )(*operands)


def pair_kernel(a, b, out0, out1):
    for n, out in enumerate((out0, out1)):
        out[...] = (a[n].astype(F32) + b[n].astype(F32)).astype(BF16)


def add_pair(a, b):
    vmem = pl.BlockSpec(memory_space=VMEM)
    return pl.pallas_call(
        pair_kernel,
        out_shape=(jax.ShapeDtypeStruct(a.shape[1:], BF16),) * 2,
        in_specs=[vmem] * 2,
        out_specs=(vmem,) * 2,
        compiler_params=pltpu.CompilerParams(vmem_limit_bytes=4 * 2**20),
        name="add_pair",
    )(a, b)


def last_pair_kernel(rows, a, b, out0, out1):
    for n, out in enumerate((out0, out1)):
        total = a[n].astype(F32) + b[n].astype(F32)
        out[:rows] = total[:rows].astype(BF16)
        high, low = two_parts(total[rows : rows + 1] + total[rows + 1 : rows + 2])
        row = lax.broadcasted_iota(jnp.int32, (STATS, out.shape[1]), 0)
        lines = jnp.where(row == 0, high.astype(F32), 0.0)
        out[rows:] = jnp.where(row == 1, low.astype(F32), lines).astype(BF16)


def add_last_pair(a, b, rows):
    vmem = pl.BlockSpec(memory_space=VMEM)
    return pl.pallas_call(
        functools.partial(last_pair_kernel, rows),
        out_shape=(jax.ShapeDtypeStruct(a.shape[1:], BF16),) * 2,
        in_specs=[vmem] * 2,
        out_specs=(vmem,) * 2,
        compiler_params=pltpu.CompilerParams(vmem_limit_bytes=4 * 2**20),
        name="add_last_pair",
    )(a, b)


def next_kernel(wide, here, there, fresh):
    fresh[...] = (
        wide[...].astype(F32) + (here[...].astype(F32) + there[...].astype(F32))
    ).astype(BF16)


def add_next(wide, here, there):
    vmem = pl.BlockSpec(memory_space=VMEM)
    return pl.pallas_call(
        next_kernel,
        out_shape=jax.ShapeDtypeStruct(wide.shape, BF16),
        in_specs=[vmem] * 3,
        out_specs=vmem,
        compiler_params=pltpu.CompilerParams(vmem_limit_bytes=4 * 2**20),
        name="add_next",
    )(wide, here, there)


def last_kernel(mine, state, here, there, out, importance):
    rows = mine.shape[0]
    total = here[...].astype(F32) + there[...].astype(F32)
    wide = jnp.where(lax.axis_index("pipe") == 0, mine[...], state[...]).astype(F32)
    out[...] = (wide + total[:rows]).astype(BF16)
    importance[...] = total[rows : rows + 1, :HD] + total[rows + 1 : rows + 2, :HD]


def add_last(mine, state, here, there):
    vmem = pl.BlockSpec(memory_space=VMEM)
    return pl.pallas_call(
        last_kernel,
        out_shape=(
            jax.ShapeDtypeStruct(mine.shape, BF16),
            jax.ShapeDtypeStruct((1, HD), F32),
        ),
        in_specs=[vmem] * 4,
        out_specs=(vmem, vmem),
        compiler_params=pltpu.CompilerParams(vmem_limit_bytes=4 * 2**20),
        name="add_last",
    )(mine, state, here, there)


def swap(block, *masks):
    route = [
        (p * N_TENSOR + t, p * N_TENSOR + (t ^ masks[min(p, len(masks) - 1)]))
        for p in range(2)
        for t in range(N_TENSOR)
    ]
    return lax.ppermute(block, ("pipe", "tensor"), route)


def to_next_section(block, mask):
    route = [(t, N_TENSOR + (t ^ mask)) for t in range(N_TENSOR)]
    return lax.ppermute(block, ("pipe", "tensor"), route)


def local(hidden_in, norm_gain, w_query, w_keyval, w_out, head_group):
    rows, cols = hidden_in.shape[0], hidden_in.shape[3]
    width = cols * N_TENSOR * N_DP
    wq, wout = w_query[0], w_out[0]
    wkv = w_keyval[0].reshape(wq.shape[0], -1)
    cosine, sine = map(jnp.asarray, rotary_tables(rows))
    choice, picked = plan(head_group)

    runs = [
        [d * N_TENSOR + 2 * a + core for d in range(N_DP) for a in range(2)] for core in range(2)
    ]

    def to_heads(step, pieces, *weights):
        send = project(step, pieces, norm_gain, wkv, wq, *weights)
        recv = lax.all_to_all(send, "dp", 0, 0)
        query, kv, *gram = combine(step, recv, cosine, sine, width)
        send = choose(choice, kv, swap(kv, 1))
        recv = lax.all_to_all(send, ("dp", "tensor"), 0, 0, axis_index_groups=runs)
        return query, recv, *gram

    mine = hidden_in.reshape(rows, cols)
    tile = ready(mine, norm_gain, wkv, cosine, sine, choice)
    far = hand_on(swap(mine, 2, 1), tile)
    pieces = (mine, swap(mine, 1), far, swap(far, 1))
    query, kv = to_heads(0, pieces)
    att0 = attend(query, kv, wout)
    recv = lax.all_to_all(att0, "dp", 0, 0)
    (other0,) = project_out(recv, wout, rows, (1, 3))
    own0, gram0 = project_out(recv, wout, rows, (0, 2))
    here, away = add_pair(own0, swap(other0, 1))
    fresh = add_next(mine, here, swap(away, 2, 1))
    far = to_next_section(fresh, 2)
    near = to_next_section(fresh, 0)

    query, kv, gram1 = to_heads(1, (near, swap(near, 1), far, swap(far, 1)), wout)
    att1 = attend_last(query, kv, att0, gram0, gram1, picked, width)
    recv = lax.all_to_all(att1, "dp", 0, 0)
    (other1,) = project_out(recv, wout, rows, (1, 3), other0)
    (own1,) = project_out(recv, wout, rows, (0, 2), own0)
    here, away = add_last_pair(own1, swap(other1, 1), rows)
    out, importance = add_last(mine, near, here, swap(away, 2))
    return out.reshape(1, rows, 1, 1, cols), importance[:, :GROUPS]


def solution(mesh):
    in_specs = (
        P(None, "dp", "tensor", None),
        P("pipe", "dp"),
        P("pipe", "dp", "tensor"),
        P("pipe", "dp", "tensor", None),
        P("pipe", "tensor", "dp"),
        P(),
    )
    out_specs = (P("pipe", None, "dp", "tensor", None), P("pipe", None))
    return jax.shard_map(local, mesh=mesh, in_specs=in_specs, out_specs=out_specs, check_vma=False)
```

```python
import functools
import math

import jax
import jax.numpy as jnp
import numpy as np
from jax import lax
from jax.experimental import pallas as pl
from jax.experimental.pallas import tpu as pltpu
from jax.sharding import PartitionSpec as P

HD = 128
GROUPS = 8
N_TENSOR = 4
N_DP = 16
THETA = 500000.0
EPS_NORM = 1e-05
EPS_RMS = 1e-06
STATS = 16

BF16 = jnp.bfloat16
F32 = jnp.float32
VMEM = pltpu.VMEM


def rotary_tables(rows):
    positions = np.arange(rows, dtype=np.float64)[:, None]
    lanes = np.arange(HD)
    angle = positions * THETA ** (-2.0 * (lanes // 2) / HD)[None, :]
    sign = np.where(lanes % 2 == 0, -1.0, 1.0)[None, :]
    return np.cos(angle).astype(np.float32), (np.sin(angle) * sign).astype(np.float32)


def rotated(values, cosine, sine):
    lanes = lax.broadcasted_iota(jnp.int32, values.shape, 1)
    swapped = jnp.where(
        lanes % 2 == 0, pltpu.roll(values, HD - 1, 1), pltpu.roll(values, 1, 1)
    )
    return values * cosine + swapped * sine


def diagonal():
    return lax.broadcasted_iota(jnp.int32, (HD, HD), 0) == lax.broadcasted_iota(
        jnp.int32, (HD, HD), 1
    )


def two_parts(values):
    high = values.astype(BF16)
    return high, (values - high.astype(F32)).astype(BF16)


def ready_kernel(*refs):
    out = refs[-1]
    out[...] = jnp.zeros_like(out)


def ready(*arrays):
    vmem = pl.BlockSpec(memory_space=VMEM)
    return pl.pallas_call(
        ready_kernel,
        out_shape=jax.ShapeDtypeStruct((16, HD), BF16),
        in_specs=[vmem] * len(arrays),
        out_specs=vmem,
        compiler_params=pltpu.CompilerParams(vmem_limit_bytes=12 * 2**20),
        cost_estimate=pl.CostEstimate(flops=10**9, bytes_accessed=10**7, transcendentals=0),
        name="ready",
    )(*arrays)


def hand_on_kernel(block, tile, out):
    out[...] = block[...]


def hand_on(block, tile):
    vmem = pl.BlockSpec(memory_space=VMEM)
    return pl.pallas_call(
        hand_on_kernel,
        out_shape=jax.ShapeDtypeStruct(block.shape, BF16),
        in_specs=[vmem] * 2,
        out_specs=vmem,
        compiler_params=pltpu.CompilerParams(vmem_limit_bytes=2 * 2**20),
        name="hand_on",
    )(block, tile)


def gram_parts(wout, target):
    @pl.loop(0, wout.shape[0] // (2 * HD))
    def _(i):
        pair = wout[pl.ds(pl.multiple_of(i * 2 * HD, 2 * HD), 2 * HD), :]
        both = lax.dot_general(pair, pair, (((1,), (1,)), ((), ())), preferred_element_type=F32)
        for n in range(2):
            high, low = two_parts(both[n * HD : (n + 1) * HD, n * HD : (n + 1) * HD])
            ref, first = target(2 * i + n)
            ref[pl.ds(first, HD), :] = high
            ref[pl.ds(first + HD, HD), :] = low


def project_kernel(step, count, *refs):
    pieces, refs = refs[:count], refs[count:]
    gain, wkv, wq, *wout, send, scaled = refs
    rows, cols = pieces[0].shape[-2:]
    per = 4
    heads = N_DP
    pitch = rows + 64 + STATS
    tensor = lax.axis_index("tensor")
    if count == 4:
        by_mask = [ref[...] for ref in pieces]
    else:
        by_mask = [pieces[mask % 2][mask // 2] for mask in range(4)]

    def block(place):
        low = [jnp.where(tensor % 2 == place % 2, by_mask[n], by_mask[n + 1]) for n in (0, 2)]
        return jnp.where(tensor // 2 == place // 2, low[0], low[1])

    active = lax.axis_index("pipe") == step

    @pl.when(active)
    def _():
        total = jnp.zeros((rows, 1), F32)
        for place in range(N_TENSOR):
            at = slice(place * cols, (place + 1) * cols)
            wide = block(place).astype(F32)
            total = total + jnp.sum(wide * wide, axis=1, keepdims=True)
            scaled[:, at] = (wide * gain[:, at].astype(F32)).astype(BF16)
        eye = diagonal()
        row = lax.broadcasted_iota(jnp.int32, (STATS, HD), 0)
        lines = jnp.zeros((STATS, HD), F32)
        for b in range(rows // HD):
            line = jnp.sum(
                jnp.where(eye, total[b * HD : (b + 1) * HD], 0.0), axis=0, keepdims=True
            )
            high, low = two_parts(line)
            lines = jnp.where(row == 2 * b, high.astype(F32), lines)
            lines = jnp.where(row == 2 * b + 1, low.astype(F32), lines)
        lines = lines.astype(BF16)
        part = jnp.dot(scaled[...], wkv[...], preferred_element_type=F32).astype(BF16)
        for j in range(heads):
            first = j * pitch + rows
            for c in range(4):
                send[first + 16 * c : first + 16 * c + 16, :] = part[
                    16 * j : 16 * j + 16, c * HD : (c + 1) * HD
                ]
            send[first + 64 : first + 64 + STATS, :] = lines
        for i in range(heads // per):
            part = jnp.dot(
                scaled[...], wq[:, i * per * HD : (i + 1) * per * HD], preferred_element_type=F32
            ).astype(BF16)
            for j in range(per):
                first = (i * per + j) * pitch
                send[first : first + rows, :] = part[:, j * HD : (j + 1) * HD]

    @pl.when(jnp.logical_not(active))
    def _():
        if wout:
            gram_parts(wout[0], lambda h: (send, pl.multiple_of(h * pitch, 16)))
            for j in range(heads):
                first = j * pitch + rows
                send[first : first + 64 + STATS, :] = jnp.zeros((64 + STATS, HD), BF16)
        else:
            send[...] = jnp.zeros_like(send)


def project(step, pieces, gain, wkv, *weights):
    rows, cols = pieces[0].shape[-2:]
    wide = cols * N_TENSOR
    pitch = rows + 64 + STATS
    vmem = pl.BlockSpec(memory_space=VMEM)
    send = pl.pallas_call(
        functools.partial(project_kernel, step, len(pieces)),
        out_shape=jax.ShapeDtypeStruct((N_DP * pitch, HD), BF16),
        in_specs=[vmem] * (len(pieces) + 2 + len(weights)),
        out_specs=vmem,
        scratch_shapes=[VMEM((rows, wide), BF16)],
        compiler_params=pltpu.CompilerParams(vmem_limit_bytes=8 * 2**20),
        name="project",
    )(*pieces, gain, wkv, *weights)
    return send.reshape(N_DP, pitch, HD)


def combine_kernel(step, width, recv, cosine, sine, query, kv, *rest):
    *gram, scale = rest
    rows = cosine.shape[0]
    active = lax.axis_index("pipe") == step

    def total(first, size):
        at = slice(first, first + size)
        value = recv[0, at, :].astype(F32)
        for s in range(1, N_DP):
            value = value + recv[s, at, :].astype(F32)
        return value

    @pl.when(active)
    def _():
        raw = total(0, rows)
        tail = total(rows, 64 + STATS)
        eye = diagonal()
        for b in range(rows // HD):
            line = tail[64 + 2 * b : 65 + 2 * b, :] + tail[65 + 2 * b : 66 + 2 * b, :]
            column = jnp.sum(jnp.where(eye, line, 0.0), axis=1, keepdims=True)
            factor = lax.rsqrt(column / width + EPS_NORM)
            scale[b * HD : (b + 1) * HD, :] = jnp.broadcast_to(factor, (HD, HD))
        query[...] = rotated(raw * scale[...], cosine[...], sine[...]).astype(BF16)
        first = pl.multiple_of(lax.axis_index("dp") * 16, 16)
        here = scale[pl.ds(first, 16), :]
        cos_here = cosine[pl.ds(first, 16), :]
        sin_here = sine[pl.ds(first, 16), :]
        for g in range(2):
            keys = tail[32 * g : 32 * g + 16] * here
            vals = tail[32 * g + 16 : 32 * g + 32] * here
            kv[g, :, :HD] = rotated(keys, cos_here, sin_here).astype(BF16)
            kv[g, :, HD:] = vals.astype(BF16)
        for ref in gram:
            ref[...] = jnp.zeros_like(ref)

    @pl.when(jnp.logical_not(active))
    def _():
        for ref in gram:
            ref[...] = total(0, HD) + total(HD, HD)
        query[...] = jnp.zeros_like(query)
        kv[...] = jnp.zeros_like(kv)


def combine(step, recv, cosine, sine, width):
    rows = cosine.shape[0]
    vmem = pl.BlockSpec(memory_space=VMEM)
    shapes = (
        jax.ShapeDtypeStruct((rows, HD), BF16),
        jax.ShapeDtypeStruct((2, 16, 2 * HD), BF16),
        jax.ShapeDtypeStruct((HD, HD), F32),
    )[: 2 + step]
    return pl.pallas_call(
        functools.partial(combine_kernel, step, float(width)),
        out_shape=shapes,
        in_specs=[vmem] * 3,
        out_specs=(vmem,) * len(shapes),
        scratch_shapes=[VMEM((rows, HD), F32)],
        compiler_params=pltpu.CompilerParams(vmem_limit_bytes=8 * 2**20),
        name="combine",
    )(recv, cosine, sine)


def plan_kernel(group, choice, picked):
    tensor, data = lax.axis_index("tensor"), lax.axis_index("dp")
    chip, core = tensor // 2, tensor % 2
    row = lax.broadcasted_iota(jnp.int32, (16, 64), 0)
    col = lax.broadcasted_iota(jnp.int32, (16, 64), 1)
    for d in range(N_DP):
        for a in range(2):
            wanted = group[(2 * a + core) * N_DP + d]
            place = jnp.where(wanted % 4 // 2 == core, 0, 2) + wanted % 2
            place = jnp.where(wanted // 4 == chip, place, 4)
            first = (2 * d + a) * 16
            hit = col == place * 16 + row
            choice[first : first + 16, :] = jnp.where(hit, 1.0, 0.0).astype(BF16)
    lane = lax.broadcasted_iota(jnp.int32, picked.shape, 1)
    picked[...] = jnp.where(lane == group[tensor * N_DP + data], 1.0, 0.0).astype(F32)


def plan(group):
    vmem = pl.BlockSpec(memory_space=VMEM)
    return pl.pallas_call(
        plan_kernel,
        out_shape=(
            jax.ShapeDtypeStruct((2 * N_DP * 16, 64), BF16),
            jax.ShapeDtypeStruct((8, HD), F32),
        ),
        in_specs=[pl.BlockSpec(memory_space=pltpu.SMEM)],
        out_specs=(vmem,) * 2,
        compiler_params=pltpu.CompilerParams(vmem_limit_bytes=2 * 2**20),
        name="plan",
    )(group)


def choose_kernel(choice, own, other, send):
    four = jnp.concatenate([own[0], own[1], other[0], other[1]], axis=0)
    send[...] = jnp.dot(choice[...], four, preferred_element_type=F32).astype(BF16)


def choose(choice, own, other):
    vmem = pl.BlockSpec(memory_space=VMEM)
    send = pl.pallas_call(
        choose_kernel,
        out_shape=jax.ShapeDtypeStruct((choice.shape[0], own.shape[2]), BF16),
        in_specs=[vmem] * 3,
        out_specs=vmem,
        compiler_params=pltpu.CompilerParams(vmem_limit_bytes=4 * 2**20),
        name="choose",
    )(choice, own, other)
    return send.reshape((2 * N_DP,) + own.shape[1:])


def attended(query, recv, kv):
    rows = query.shape[0]
    few = rows // N_DP
    for d in range(N_DP):
        both = recv[2 * d].astype(F32) + recv[2 * d + 1].astype(F32)
        kv[d * few : (d + 1) * few, :] = both.astype(BF16)
    scores = lax.dot_general(
        query, kv[:, :HD], (((1,), (1,)), ((), ())), preferred_element_type=F32
    )
    allowed = lax.broadcasted_iota(jnp.int32, (rows, rows), 0) >= lax.broadcasted_iota(
        jnp.int32, (rows, rows), 1
    )
    expo = jnp.where(allowed, jnp.exp(scores * (1.0 / math.sqrt(HD))), 0.0)
    weights = (expo / jnp.sum(expo, axis=1, keepdims=True)).astype(BF16)
    return jnp.dot(weights, kv[:, HD:], preferred_element_type=F32).astype(BF16)


def attend_kernel(query, recv, wout, send, kv):
    active = lax.axis_index("pipe") == 0

    @pl.when(active)
    def _():
        result = attended(query[...], recv, kv)
        for j in range(N_DP):
            send[j] = result

    @pl.when(jnp.logical_not(active))
    def _():
        gram_parts(wout, lambda h: (send.at[h], 0))


def attend(query, recv, wout):
    rows = query.shape[0]
    vmem = pl.BlockSpec(memory_space=VMEM)
    return pl.pallas_call(
        attend_kernel,
        out_shape=jax.ShapeDtypeStruct((N_DP, rows, HD), BF16),
        in_specs=[vmem] * 3,
        out_specs=vmem,
        scratch_shapes=[VMEM((rows, 2 * HD), BF16)],
        compiler_params=pltpu.CompilerParams(vmem_limit_bytes=8 * 2**20),
        name="attend",
    )(query, recv, wout)


def attend_last_kernel(width, query, recv, before, gram0, gram1, picked, send, kv):
    rows = query.shape[0]
    result = attended(query[...], recv, kv)
    first_section = lax.axis_index("pipe") == 0
    mine = jnp.where(first_section, before[0], result)
    gram = jnp.where(first_section, gram1[...], gram0[...])
    high, low = two_parts(gram)
    image = jnp.dot(mine, high, preferred_element_type=F32) + jnp.dot(
        mine, low, preferred_element_type=F32
    )
    squares = jnp.sum(image * mine.astype(F32), axis=1, keepdims=True)
    spread = jnp.sqrt(jnp.maximum(squares / width, 0.0) + EPS_RMS)
    mean = jnp.sum(spread, axis=0, keepdims=True) / rows
    high, low = two_parts(mean * picked[0:1, :])
    row = lax.broadcasted_iota(jnp.int32, (STATS, HD), 0)
    lines = jnp.where(row == 0, high.astype(F32), jnp.where(row == 1, low.astype(F32), 0.0))
    lines = lines.astype(BF16)
    for j in range(N_DP):
        send[j, :rows] = result
        send[j, rows:] = lines


def attend_last(query, recv, before, gram0, gram1, picked, width):
    rows = query.shape[0]
    vmem = pl.BlockSpec(memory_space=VMEM)
    return pl.pallas_call(
        functools.partial(attend_last_kernel, float(width)),
        out_shape=jax.ShapeDtypeStruct((N_DP, rows + STATS, HD), BF16),
        in_specs=[vmem] * 6,
        out_specs=vmem,
        scratch_shapes=[VMEM((rows, 2 * HD), BF16)],
        compiler_params=pltpu.CompilerParams(vmem_limit_bytes=8 * 2**20),
        name="attend_last",
    )(query, recv, before, gram0, gram1, picked)


def out_kernel(rows, masks, last, *refs):
    if last:
        recv, saved, wout, parts = refs
    else:
        recv, wout, parts, *gram = refs
    heads = recv.shape[0]
    cols = parts.shape[2]
    tensor = lax.axis_index("tensor")
    active = lax.axis_index("pipe") == (1 if last else 0)
    if last:
        sums = jnp.zeros((1, HD), F32)
        for h in range(heads):
            sums = sums + (
                recv[h, rows : rows + 1, :].astype(F32)
                + recv[h, rows + 1 : rows + 2, :].astype(F32)
            )
        sums = jnp.concatenate([sums, jnp.zeros((1, cols - HD), F32)], axis=1)
        high, low = two_parts(sums)
        row = lax.broadcasted_iota(jnp.int32, (STATS, cols), 0)
        lines = jnp.where(
            row == 0, high.astype(F32), jnp.where(row == 1, low.astype(F32), 0.0)
        ).astype(BF16)
        for n in range(2):
            parts[n, rows:] = lines
    for parity in range(2):

        @pl.when(jnp.logical_and(active, (tensor + masks[0] + parity) % 2 == 0))
        def _():
            for place in (parity, parity + 2):
                total = None
                for h in range(0, heads, 2):
                    pair = jnp.concatenate([recv[h, :rows, :], recv[h + 1, :rows, :]], axis=1)
                    one = jnp.dot(
                        pair,
                        wout[h * HD : (h + 2) * HD, place * cols : (place + 1) * cols],
                        preferred_element_type=F32,
                    )
                    total = one if total is None else total + one
                n = lax.bitwise_xor(tensor, place) // 2
                parts[n, :rows] = total.astype(BF16)

    @pl.when(jnp.logical_not(active))
    def _():
        for n in range(2):
            parts[n, :rows] = saved[n] if last else jnp.zeros((rows, cols), BF16)
        if not last and gram:
            total = jnp.zeros((HD, HD), F32)
            for s in range(heads):
                total = total + (recv[s, :HD].astype(F32) + recv[s, HD : 2 * HD].astype(F32))
            gram[0][...] = total

    if not last and gram:

        @pl.when(active)
        def _():
            gram[0][...] = jnp.zeros((HD, HD), F32)


def project_out(recv, wout, rows, masks, saved=None):
    heads, deep, _ = recv.shape
    cols = wout.shape[1] // N_TENSOR
    last = saved is not None
    vmem = pl.BlockSpec(memory_space=VMEM)
    shapes = (jax.ShapeDtypeStruct((2, deep, cols), BF16),)
    if not last and masks[0] == 0:
        shapes += (jax.ShapeDtypeStruct((HD, HD), F32),)
    operands = (recv, saved, wout) if last else (recv, wout)
    return pl.pallas_call(
        functools.partial(out_kernel, rows, masks, last),
        out_shape=shapes,
        in_specs=[vmem] * len(operands),
        out_specs=(vmem,) * len(shapes),
        compiler_params=pltpu.CompilerParams(vmem_limit_bytes=6 * 2**20),
        cost_estimate=pl.CostEstimate(
            flops=4 * rows * heads * HD * cols, bytes_accessed=2**22, transcendentals=0
        ),
        name="project_out",
    )(*operands)


def pair_kernel(a, b, out0, out1):
    for n, out in enumerate((out0, out1)):
        out[...] = (a[n].astype(F32) + b[n].astype(F32)).astype(BF16)


def add_pair(a, b):
    vmem = pl.BlockSpec(memory_space=VMEM)
    return pl.pallas_call(
        pair_kernel,
        out_shape=(jax.ShapeDtypeStruct(a.shape[1:], BF16),) * 2,
        in_specs=[vmem] * 2,
        out_specs=(vmem,) * 2,
        compiler_params=pltpu.CompilerParams(vmem_limit_bytes=4 * 2**20),
        name="add_pair",
    )(a, b)


def last_pair_kernel(rows, a, b, out0, out1):
    for n, out in enumerate((out0, out1)):
        total = a[n].astype(F32) + b[n].astype(F32)
        out[:rows] = total[:rows].astype(BF16)
        high, low = two_parts(total[rows : rows + 1] + total[rows + 1 : rows + 2])
        row = lax.broadcasted_iota(jnp.int32, (STATS, out.shape[1]), 0)
        lines = jnp.where(row == 0, high.astype(F32), 0.0)
        out[rows:] = jnp.where(row == 1, low.astype(F32), lines).astype(BF16)


def add_last_pair(a, b, rows):
    vmem = pl.BlockSpec(memory_space=VMEM)
    return pl.pallas_call(
        functools.partial(last_pair_kernel, rows),
        out_shape=(jax.ShapeDtypeStruct(a.shape[1:], BF16),) * 2,
        in_specs=[vmem] * 2,
        out_specs=(vmem,) * 2,
        compiler_params=pltpu.CompilerParams(vmem_limit_bytes=4 * 2**20),
        name="add_last_pair",
    )(a, b)


def next_kernel(wide, here, there, fresh):
    fresh[...] = (
        wide[...].astype(F32) + (here[...].astype(F32) + there[...].astype(F32))
    ).astype(BF16)


def add_next(wide, here, there):
    vmem = pl.BlockSpec(memory_space=VMEM)
    return pl.pallas_call(
        next_kernel,
        out_shape=jax.ShapeDtypeStruct(wide.shape, BF16),
        in_specs=[vmem] * 3,
        out_specs=vmem,
        compiler_params=pltpu.CompilerParams(vmem_limit_bytes=4 * 2**20),
        name="add_next",
    )(wide, here, there)


def last_kernel(mine, state, here, there, out, importance):
    rows = mine.shape[0]
    total = here[...].astype(F32) + there[...].astype(F32)
    wide = jnp.where(lax.axis_index("pipe") == 0, mine[...], state[...]).astype(F32)
    out[...] = (wide + total[:rows]).astype(BF16)
    importance[...] = total[rows : rows + 1, :HD] + total[rows + 1 : rows + 2, :HD]


def add_last(mine, state, here, there):
    vmem = pl.BlockSpec(memory_space=VMEM)
    return pl.pallas_call(
        last_kernel,
        out_shape=(
            jax.ShapeDtypeStruct(mine.shape, BF16),
            jax.ShapeDtypeStruct((1, HD), F32),
        ),
        in_specs=[vmem] * 4,
        out_specs=(vmem, vmem),
        compiler_params=pltpu.CompilerParams(vmem_limit_bytes=4 * 2**20),
        name="add_last",
    )(mine, state, here, there)


def swap(block, *masks):
    route = [
        (p * N_TENSOR + t, p * N_TENSOR + (t ^ masks[min(p, len(masks) - 1)]))
        for p in range(2)
        for t in range(N_TENSOR)
    ]
    return lax.ppermute(block, ("pipe", "tensor"), route)


def to_next_section(block, mask):
    route = [(t, N_TENSOR + (t ^ mask)) for t in range(N_TENSOR)]
    return lax.ppermute(block, ("pipe", "tensor"), route)


def local(hidden_in, norm_gain, w_query, w_keyval, w_out, head_group):
    rows, cols = hidden_in.shape[0], hidden_in.shape[3]
    width = cols * N_TENSOR * N_DP
    wq, wout = w_query[0], w_out[0]
    wkv = w_keyval[0].reshape(wq.shape[0], -1)
    cosine, sine = map(jnp.asarray, rotary_tables(rows))
    choice, picked = plan(head_group)

    runs = [
        [d * N_TENSOR + 2 * a + core for d in range(N_DP) for a in range(2)] for core in range(2)
    ]

    def to_heads(step, pieces, *weights):
        send = project(step, pieces, norm_gain, wkv, wq, *weights)
        recv = lax.all_to_all(send, "dp", 0, 0)
        query, kv, *gram = combine(step, recv, cosine, sine, width)
        send = choose(choice, kv, swap(kv, 1))
        recv = lax.all_to_all(send, ("dp", "tensor"), 0, 0, axis_index_groups=runs)
        return query, recv, *gram

    mine = hidden_in.reshape(rows, cols)
    tile = ready(mine, norm_gain, wkv, cosine, sine, choice)
    far = hand_on(swap(mine, 2, 1), tile)
    pieces = (mine, swap(mine, 1), far, swap(far, 1))
    query, kv = to_heads(0, pieces)
    att0 = attend(query, kv, wout)
    recv = lax.all_to_all(att0, "dp", 0, 0)
    (other0,) = project_out(recv, wout, rows, (1, 3))
    own0, gram0 = project_out(recv, wout, rows, (0, 2))
    here, away = add_pair(own0, swap(other0, 1))
    fresh = add_next(mine, here, swap(away, 2, 1))
    near = to_next_section(fresh, 0)
    beside = swap(near, 1)
    far = hand_on(to_next_section(fresh, 2), beside)

    query, kv, gram1 = to_heads(1, (near, beside, far, swap(far, 1)), wout)
    att1 = attend_last(query, kv, att0, gram0, gram1, picked, width)
    recv = lax.all_to_all(att1, "dp", 0, 0)
    (other1,) = project_out(recv, wout, rows, (1, 3), other0)
    (own1,) = project_out(recv, wout, rows, (0, 2), own0)
    here, away = add_last_pair(own1, swap(other1, 1), rows)
    out, importance = add_last(mine, near, here, swap(away, 2))
    return out.reshape(1, rows, 1, 1, cols), importance[:, :GROUPS]


def solution(mesh):
    in_specs = (
        P(None, "dp", "tensor", None),
        P("pipe", "dp"),
        P("pipe", "dp", "tensor"),
        P("pipe", "dp", "tensor", None),
        P("pipe", "tensor", "dp"),
        P(),
    )
    out_specs = (P("pipe", None, "dp", "tensor", None), P("pipe", None))
    return jax.shard_map(local, mesh=mesh, in_specs=in_specs, out_specs=out_specs, check_vma=False)
```
